32 devices in a mesh: leaf: 4 (over y, core), node: 8 (over z, x).
Axes of the slice: x: 2, y: 2, z: 4, core: 2. Of those that a mesh axis runs over, the one named last changes fastest.
Arguments:
- sources: bfloat16 [2048, 16384], P('node', 'leaf'), may hold values from -6 to 6
- block_inverse: bfloat16 [512, 16384], P(None, ('leaf', 'node')), may hold values from -0.25 to 0.25
- basis_left: bfloat16 [64, 16384], P(None, ('leaf', 'node')), may hold values from -0.09375 to 0.09375
- basis_right: bfloat16 [64, 16384], P(None, ('leaf', 'node')), may hold values from -0.75 to 0.75
- couple_in: bfloat16 [64, 16384], P(None, ('leaf', 'node')), may hold values from -0.09375 to 0.09375
- couple_out: bfloat16 [64, 16384], P(None, ('leaf', 'node')), may hold values from -0.5 to 0.5
- column_of_shot: int32 [2048], replicated, may hold values from 0 to 2047, each once
- cell_map: int32 [16384], P(('leaf', 'node')), may hold values from 0 to 16383
Outputs:
- solution: bfloat16 [2048, 16384], P(None, ('leaf', 'node'))
- gradient: float32 [16384], P('node')
The draws below stay inside these ranges and needn't reach their ends.
Inputs may be any that keep to these rules, and one draw needn't show every extreme that they name: `column_of_shot`: a permutation of the 2048 column numbers.
All inputs are finite; a program needn't handle non-finite values.
Results may differ from the reference program's by a relative error of at most 0.02.
Values may be sent and summed in bfloat16 or wider, within the bound.
A program may use at most 64 MiB of HBM per device.

```python
import jax
import jax.numpy as jnp
from jax import lax

BLOCK = 512
K = 64
NCOL = 2048
FRONT = 4096
ROWS = 16384
CELLS = 16384
N_LEAF = 4


def touch_ends(result, key, least, largest):
    dims = result.shape
    place = [jax.random.randint(jax.random.fold_in(key, axis), (), 0, dims[axis]) for axis in range(len(dims))]
    result = result.at[tuple(place)].set(least)
    longest = dims.index(max(dims))
    place[longest] = (place[longest] + 1) % dims[longest]
    return result.at[tuple(place)].set(largest)


def steps_of(key, dims, split, low, largest):
    gain = 1.0
    for position, parts in split:
        steps = jax.random.uniform(jax.random.fold_in(jax.random.fold_in(key, 6), position), (parts,), jnp.float32, low / len(split), largest / len(split))
        gain = gain * jnp.repeat(jnp.exp(steps), dims[position] // parts).reshape((-1,) + (1,) * (len(dims) - 1 - position))
    return gain


def centred(stream_key, shape, width, limit, pieces=(), kind=jnp.bfloat16):
    drawn = jax.random.normal(stream_key, shape, jnp.float32) * width
    if len(pieces) > 0:
        drawn = steps_of(stream_key, shape, pieces, -0.22, 0.18) * drawn
    return jnp.clip(drawn, min=-limit, max=limit).astype(kind)


def setup_inputs(seed: int = 0) -> dict:
    streams_of = jax.random.split(jax.random.key(seed), 9)
    return {
        "sources": centred(streams_of[0], (NCOL, ROWS), 1.0, 6.0, ((0, 8), (1, 4))),
        "block_inverse": centred(streams_of[1], (BLOCK, ROWS), BLOCK ** -0.5, 0.25, ((1, 32),)),
        "basis_left": centred(streams_of[2], (K, ROWS), FRONT ** -0.5, 0.09375, ((1, 32),)),
        "basis_right": centred(streams_of[3], (K, ROWS), K ** -0.5, 0.75, ((1, 32),)),
        "couple_in": centred(streams_of[4], (K, ROWS), FRONT ** -0.5, 0.09375, ((1, 32),)),
        "couple_out": centred(streams_of[5], (K, ROWS), 0.08, 0.5, ((1, 32),)),
        "column_of_shot": jax.random.permutation(streams_of[6], NCOL).astype(jnp.int32),
        "cell_map": touch_ends(jax.random.randint(streams_of[7], (ROWS,), 0, CELLS), jax.random.fold_in(streams_of[7], 1), 0, CELLS - 1).astype(jnp.int32),
    }


def apply_group(values, inverse_blocks, left_basis, right_basis, transposed):
    count = values.shape[0]
    value_blocks = values.reshape(count, -1, BLOCK).astype(jnp.float32)
    matrix_blocks = inverse_blocks.reshape(BLOCK, -1, BLOCK).astype(jnp.float32)
    if transposed:
        local_part = jnp.einsum('rmi,jmi->rmj', value_blocks, matrix_blocks, precision=lax.Precision.HIGHEST)
    else:
        local_part = jnp.einsum('rmi,imj->rmj', value_blocks, matrix_blocks, precision=lax.Precision.HIGHEST)
    local_part = local_part.reshape(count, -1)
    projected = jnp.dot(values, left_basis.T, preferred_element_type=jnp.float32).astype(jnp.bfloat16)
    return (local_part + jnp.dot(projected, right_basis, preferred_element_type=jnp.float32)).astype(jnp.bfloat16)

def reference(sources, block_inverse, basis_left, basis_right, couple_in, couple_out, column_of_shot, cell_map):
    inverse = jnp.zeros((NCOL,), jnp.int32).at[column_of_shot].set(jnp.arange(NCOL, dtype=jnp.int32))
    rhs_cols = sources[inverse]
    incoming = jnp.zeros((NCOL, K), jnp.float32)
    forwards = []
    for group in range(N_LEAF):
        window = slice(group * FRONT, (group + 1) * FRONT)
        fwd_rhs = apply_group(rhs_cols[:, window], block_inverse[:, window], basis_left[:, window], basis_right[:, window], False)
        fwd_couple = apply_group(couple_in[:, window], block_inverse[:, window], basis_left[:, window], basis_right[:, window], False)
        carry = jnp.dot(fwd_rhs, couple_out[:, window].T, preferred_element_type=jnp.float32)
        step_map = -jnp.dot(fwd_couple, couple_out[:, window].T, preferred_element_type=jnp.float32)
        forward = fwd_rhs.astype(jnp.float32) - jnp.dot(incoming, fwd_couple.astype(jnp.float32), precision=lax.Precision.HIGHEST)
        forwards.append(forward.astype(jnp.bfloat16))
        incoming = carry + jnp.dot(incoming, step_map, precision=lax.Precision.HIGHEST)
    returning = jnp.zeros((NCOL, K), jnp.float32)
    solutions = [None] * N_LEAF
    for group in range(N_LEAF - 1, -1, -1):
        window = slice(group * FRONT, (group + 1) * FRONT)
        back_rhs = apply_group(forwards[group], block_inverse[:, window], basis_right[:, window], basis_left[:, window], True)
        back_couple = apply_group(couple_out[:, window], block_inverse[:, window], basis_right[:, window], basis_left[:, window], True)
        lift = jnp.dot(back_rhs, couple_in[:, window].T, preferred_element_type=jnp.float32)
        turn_map = -jnp.dot(back_couple, couple_in[:, window].T, preferred_element_type=jnp.float32)
        solved = back_rhs.astype(jnp.float32) - jnp.dot(returning, back_couple.astype(jnp.float32), precision=lax.Precision.HIGHEST)
        solutions[group] = solved.astype(jnp.bfloat16)
        returning = lift + jnp.dot(returning, turn_map, precision=lax.Precision.HIGHEST)
    solution = jnp.concatenate(solutions, axis=1)
    forward_all = jnp.concatenate(forwards, axis=1)
    corr = lax.optimization_barrier(jnp.sum(solution.astype(jnp.float32) * forward_all.astype(jnp.float32), axis=0)) / jnp.sqrt(jnp.float32(NCOL))
    gradient = jnp.zeros((CELLS,), jnp.float32).at[cell_map].add(corr)
    return (solution, gradient)
```

```python
import functools

import jax
import jax.numpy as jnp
from jax import lax
from jax.experimental import pallas as pl
from jax.experimental.pallas import tpu as pltpu
from jax.sharding import PartitionSpec as P

CELL_DEV = 2048
LANES = 128
MESH = pl.DeviceIdType.MESH


def dot_rows(a, b):
    return lax.dot_general(a, b, (((1,), (1,)), ((), ())), preferred_element_type=jnp.float32)


def dot(a, b):
    return jnp.dot(a, b, preferred_element_type=jnp.float32)


def half(x):
    return x.astype(jnp.bfloat16)


class Tree:
    def __init__(self, buf, zsend, xsend, recv, leaf, node, zs, xs):
        self.buf, self.zsend, self.xsend, self.recv = buf, zsend, xsend, recv
        self.leaf, self.zs, self.xs = leaf, zs, xs
        self.z, self.x = node // xs, node % xs

    def copy(self, slot, dst, sem):
        return pltpu.make_async_remote_copy(
            src_ref=self.buf.at[slot],
            dst_ref=self.buf.at[slot],
            send_sem=sem,
            recv_sem=self.recv.at[slot],
            device_id=(self.leaf, dst),
            device_id_type=MESH,
        )

    def slot(self, zz):
        return zz * self.xs + self.x

    def up(self, zz, sem):
        return self.copy(self.slot(zz), (self.z + 1) * self.xs + self.x, self.zsend.at[sem])

    def down(self, zz, sem):
        return self.copy(self.slot(zz), (self.z - 1) * self.xs + self.x, self.zsend.at[sem])

    def across(self, zz):
        return [
            self.copy(
                self.slot(zz),
                self.z * self.xs + (self.x + i) % self.xs,
                self.xsend.at[zz * (self.xs - 1) + i - 1],
            )
            for i in range(1, self.xs)
        ]

    def start(self):
        pl.when(self.z + 1 < self.zs)(lambda: self.up(self.z, self.z).start())
        pl.when(self.z > 0)(lambda: self.down(self.z, self.zs).start())
        for c in self.across(self.z):
            c.start()

    def wait_slot(self, slot):
        self.copy(slot, 0, self.zsend.at[0]).wait_recv()

    def relay(self, hop, use):
        below, above = self.z - hop, self.z + hop

        @pl.when(below >= 0)
        def _():
            self.wait_slot(self.slot(below))
            pl.when(self.z + 1 < self.zs)(lambda: self.up(below, below).start())
            for c in self.across(below):
                c.start()

        @pl.when(above < self.zs)
        def _():
            self.wait_slot(self.slot(above))
            pl.when(self.z > 0)(lambda: self.down(above, above).start())
            for c in self.across(above):
                c.start()

        if use is not None:
            pl.when(below >= 0)(lambda: use(self.slot(below)))
            pl.when(above < self.zs)(lambda: use(self.slot(above)))

    def partners(self, use):
        for i in range(1, self.xs):
            @pl.loop(0, self.zs)
            def _(zz):
                slot = zz * self.xs + (self.x + i) % self.xs
                self.wait_slot(slot)
                if use is not None:
                    use(slot)

    def finish(self):
        @pl.loop(0, self.zs)
        def _(zz):
            for c in self.across(zz):
                c.wait_send()
            pl.when((zz <= self.z) & (self.z + 1 < self.zs))(
                lambda: self.up(zz, zz).wait_send()
            )
            pl.when((zz > self.z) & (self.z > 0))(lambda: self.down(zz, zz).wait_send())
        pl.when(self.z > 0)(lambda: self.down(self.z, self.zs).wait_send())


def kernel(
    n, leaves, xs,
    src, b_ref, bl_ref, br_ref, ci_ref, co_ref, shot_ref, cell_ref,
    sol_ref, grad_ref,
    src_v, rg, rhs, lg, cg, onehot, zacc, u_ref, t_ref, gpart, gbuf, lbuf,
    src_sem, own_sem, rz, rx, rr, a_send, a_recv, l_send, l_recv, cz, cx, cr,
    g_send, g_recv, h_send, h_recv,
):
    leaf, node = lax.axis_index("leaf"), lax.axis_index("node")
    zs = n // xs
    k, block = bl_ref.shape
    shots = src.shape[0]
    total = n * shots

    barrier = pltpu.get_barrier_semaphore()

    @pl.loop(1, n)
    def _(i):
        pl.semaphore_signal(
            barrier, inc=1, device_id=(leaf, (node + i) % n), device_id_type=MESH
        )

    @pl.loop(1, leaves)
    def _(i):
        pl.semaphore_signal(
            barrier, inc=1, device_id=((leaf + i) % leaves, node), device_id_type=MESH
        )

    src_copy = pltpu.make_async_copy(src, src_v, src_sem)
    src_copy.start()

    def columns(j):
        return pl.ds(pl.multiple_of(j * block, block), block)

    own_copy = pltpu.make_async_copy(src.at[:, columns(node)], rhs.at[node], own_sem)
    own_copy.start()

    b = b_ref[...]
    u = dot(ci_ref[...], b)
    u_ref[...] = u
    stacked = jnp.concatenate([co_ref[...], br_ref[...], half(u)], axis=0)
    t = dot_rows(stacked, b)
    t_ref[...] = t[:k]
    v = jnp.concatenate([bl_ref[...], half(t)], axis=0)
    rg[node, : 4 * k] = v
    rg[node, 4 * k :, : 4 * k] = half(dot_rows(ci_ref[...], v))
    rg[node, 4 * k :, 4 * k : 8 * k] = half(
        dot_rows(br_ref[...], jnp.concatenate([bl_ref[...], stacked], axis=0))
    )

    pl.semaphore_wait(barrier, n - 1 + leaves - 1)

    basis = Tree(rg, rz, rx, rr, leaf, node, zs, xs)
    basis.start()

    def shot_copy(j):
        return pltpu.make_async_remote_copy(
            src_ref=src.at[:, columns(j)],
            dst_ref=rhs.at[node],
            send_sem=a_send.at[j],
            recv_sem=a_recv.at[node],
            device_id=(leaf, j),
            device_id_type=MESH,
        )

    @pl.loop(1, n)
    def _(i):
        shot_copy((node + i) % n).start()

    rows_at = 256

    @pl.loop(0, n)
    def _(j):
        @pl.loop(0, total // rows_at)
        def _(r):
            at = pl.multiple_of(r * rows_at, rows_at)
            row = lax.broadcasted_iota(jnp.int32, (rows_at, shots), 0) + at
            onehot[j, pl.ds(at, rows_at), :] = half(jnp.where(row == shot_ref[j], 1.0, 0.0))

    src_copy.wait()
    zacc[...] = dot_rows(src_v[:, columns(node)], rg[node, : 4 * k])

    def project(slot):
        zacc[...] += dot_rows(src_v[:, columns(slot)], rg[slot, : 4 * k])

    for hop in range(1, zs):
        basis.relay(hop, project)
    basis.partners(project)

    s = rg[0, 4 * k :, :].astype(jnp.float32)
    for j in range(1, n):
        s = s + rg[j, 4 * k :, :].astype(jnp.float32)
    s3t = half(s[:, :k])
    ss = half(s[:, 4 * k : 8 * k])
    f = s[:, : 4 * k] + dot(s3t, ss)
    z = zacc[...]
    proj = half(z[:, :k])
    zf = z + dot(proj, ss)
    carry, z2, z3 = zf[:, k : 2 * k], zf[:, 2 * k : 3 * k], zf[:, 3 * k :]
    fb = f[:, 2 * k : 3 * k]
    lift = z3 + dot_rows(half(z2), s3t)
    lift_map = f[:, 3 * k :] + dot_rows(half(fb), s3t)
    lg[leaf, :shots] = half(jnp.concatenate([carry, lift], axis=1))
    lg[leaf, shots:] = half(-jnp.concatenate([f[:, k : 2 * k], lift_map], axis=1))

    def leaf_copy(i):
        return pltpu.make_async_remote_copy(
            src_ref=lg.at[leaf],
            dst_ref=lg.at[leaf],
            send_sem=l_send.at[i],
            recv_sem=l_recv.at[leaf],
            device_id=((leaf + i) % leaves, node),
            device_id_type=MESH,
        )

    for i in range(1, leaves):
        leaf_copy(i).start()

    fc = half(u_ref[...] + dot(s3t, br_ref[...]))
    s1 = half(s[:, 5 * k : 6 * k])
    bc = half(
        t_ref[...]
        + lax.dot_general(s1, bl_ref[...], (((0,), (0,)), ((), ())), preferred_element_type=jnp.float32)
    )
    fwd_low = jnp.concatenate([br_ref[...], fc], axis=0)
    back_low = jnp.concatenate([bl_ref[...], bc], axis=0)

    for i in range(1, leaves):
        j = (leaf + i) % leaves
        pltpu.make_async_remote_copy(
            src_ref=lg.at[leaf], dst_ref=lg.at[j], send_sem=l_send.at[0],
            recv_sem=l_recv.at[j], device_id=(j, node), device_id_type=MESH,
        ).wait_recv()

    incoming = jnp.zeros((shots, k), jnp.float32)
    own_in = jnp.zeros((shots, k), jnp.float32)
    lifts = []
    for g in range(leaves):
        own_in = jnp.where(leaf == g, incoming, own_in)
        both = lg[g, :shots].astype(jnp.float32)
        if g > 0:
            both = both + dot(half(incoming), lg[g, shots:])
        incoming = both[:, :k]
        lifts.append(both[:, k:])
    returning = jnp.zeros((shots, k), jnp.float32)
    own_ret = jnp.zeros((shots, k), jnp.float32)
    for g in range(leaves - 1, -1, -1):
        own_ret = jnp.where(leaf == g, returning, own_ret)
        if g < leaves - 1:
            returning = lifts[g] + dot_rows(half(returning), lg[g, shots:, :k])
        else:
            returning = lifts[g]
    proj_fwd = z2 - dot(half(own_in), half(fb))
    cg[node] = half(
        jnp.concatenate([z[:, :k], -own_in, proj_fwd, -own_ret], axis=1)
    )

    coefs = Tree(cg, cz, cx, cr, leaf, node, zs, xs)
    coefs.start()
    for hop in range(1, zs):
        coefs.relay(hop, None)
    coefs.partners(None)

    own_copy.wait()
    sums = jnp.zeros((1, block), jnp.float32)

    def shot_block(j, sums, first):
        low = cg[j]
        fwd = half(dot(rhs[j], b_ref[...]) + dot(low[:, : 2 * k], fwd_low))
        sol = half(dot_rows(fwd, b_ref[...]) + dot(low[:, 2 * k :], back_low))

        @pl.loop(0, total // rows_at)
        def _(r):
            rows = pl.ds(pl.multiple_of(r * rows_at, rows_at), rows_at)
            part = half(dot(onehot[j, rows, :], sol))
            if first:
                sol_ref[rows, :] = part
            else:
                sol_ref[rows, :] += part

        return sums + jnp.sum(
            sol.astype(jnp.float32) * fwd.astype(jnp.float32), axis=0, keepdims=True
        )

    sums = shot_block(node, sums, True)

    def later(i, sums):
        j = (node + n - i) % n
        pltpu.make_async_remote_copy(
            src_ref=rhs.at[j], dst_ref=rhs.at[j], send_sem=a_send.at[j],
            recv_sem=a_recv.at[j], device_id=(leaf, j), device_id_type=MESH,
        ).wait_recv()
        return shot_block(j, sums, False)

    sums = lax.fori_loop(1, n, later, sums)
    corr = sums / jnp.sqrt(jnp.float32(total))

    cell = cell_ref[...]
    slab = gpart.shape[1]
    high = lax.broadcasted_iota(jnp.int32, (n * slab, block), 0) == cell // LANES
    low_hit = lax.broadcasted_iota(jnp.int32, (LANES, block), 0) == cell % LANES
    placed = lax.dot_general(
        jnp.where(high, corr, 0.0),
        jnp.where(low_hit, 1.0, 0.0),
        (((1,), (1,)), ((), ())),
        preferred_element_type=jnp.float32,
        precision=lax.Precision.HIGHEST,
    )
    gpart[...] = placed.reshape(gpart.shape)

    def slab_copy(j, frm):
        return pltpu.make_async_remote_copy(
            src_ref=gpart.at[j], dst_ref=gbuf.at[frm], send_sem=g_send.at[j],
            recv_sem=g_recv.at[frm], device_id=(leaf, j), device_id_type=MESH,
        )

    @pl.loop(1, n)
    def _(i):
        slab_copy((node + i) % n, node).start()

    own = gpart[node]

    def add_slab(i, acc):
        j = (node + n - i) % n
        slab_copy(j, j).wait_recv()
        return acc + gbuf[j]

    own = lax.fori_loop(1, n, add_slab, own)
    lbuf[leaf] = own

    def grad_copy(i, frm):
        return pltpu.make_async_remote_copy(
            src_ref=lbuf.at[leaf], dst_ref=lbuf.at[frm], send_sem=h_send.at[i],
            recv_sem=h_recv.at[frm], device_id=((leaf + i) % leaves, node),
            device_id_type=MESH,
        )

    for i in range(1, leaves):
        grad_copy(i, leaf).start()
    for i in range(1, leaves):
        grad_copy(i, (leaf + leaves - i) % leaves).wait_recv()
    acc = lbuf[0]
    for g in range(1, leaves):
        acc = acc + lbuf[g]
    grad_ref[...] = acc

    basis.finish()
    coefs.finish()
    for i in range(1, leaves):
        leaf_copy(i).wait_send()
        grad_copy(i, leaf).wait_send()

    @pl.loop(1, n)
    def _(i):
        j = (node + i) % n
        shot_copy(j).wait_send()
        slab_copy(j, node).wait_send()


def per_device(n, leaves, sources, block_inverse, basis_left, basis_right, couple_in, couple_out, column_of_shot, cell_map):
    xs = max(d for d in range(1, n + 1) if n % d == 0 and (2 * d * d <= n or d == 1))
    zs = n // xs
    k, block = basis_left.shape
    shots = sources.shape[0]
    total = n * shots
    slab = CELL_DEV // LANES
    bf16, f32 = jnp.bfloat16, jnp.float32
    dma = pltpu.SemaphoreType.DMA
    vmem = pl.BlockSpec(memory_space=pltpu.VMEM)
    solution_out, grad = pl.pallas_call(
        functools.partial(kernel, n, leaves, xs),
        out_shape=(
            jax.ShapeDtypeStruct((total, block), bf16),
            jax.ShapeDtypeStruct((slab, LANES), f32),
        ),
        in_specs=[pl.BlockSpec(memory_space=pl.ANY)] + [vmem] * 7,
        out_specs=(vmem, vmem),
        scratch_shapes=[
            pltpu.VMEM(sources.shape, bf16),
            pltpu.VMEM((n, 5 * k, block), bf16),
            pltpu.VMEM((n, shots, block), bf16),
            pltpu.VMEM((leaves, shots + k, 2 * k), bf16),
            pltpu.VMEM((n, shots, 4 * k), bf16),
            pltpu.VMEM((n, total, shots), bf16),
            pltpu.VMEM((shots, 4 * k), f32),
            pltpu.VMEM((k, block), f32),
            pltpu.VMEM((k, block), f32),
            pltpu.VMEM((n, slab, LANES), f32),
            pltpu.VMEM((n, slab, LANES), f32),
            pltpu.VMEM((leaves, slab, LANES), f32),
            dma, dma,
            dma((zs + 1,)), dma((max(zs * (xs - 1), 1),)), dma((n,)),
            dma((n,)), dma((n,)),
            dma((leaves,)), dma((leaves,)),
            dma((zs + 1,)), dma((max(zs * (xs - 1), 1),)), dma((n,)),
            dma((n,)), dma((n,)),
            dma((leaves,)), dma((leaves,)),
        ],
        compiler_params=pltpu.CompilerParams(
            collective_id=0, has_side_effects=True, vmem_limit_bytes=56 * 1024 * 1024
        ),
    )(
        sources, block_inverse, basis_left, basis_right, couple_in, couple_out,
        column_of_shot.reshape(n, 1, shots), cell_map.reshape(1, -1),
    )
    return solution_out, grad.reshape(-1)


def solution(mesh):
    both = P(None, ("leaf", "node"))
    return jax.shard_map(
        functools.partial(per_device, mesh.shape["node"], mesh.shape["leaf"]),
        mesh=mesh,
        in_specs=(P("node", "leaf"), both, both, both, both, both, P(), P(("leaf", "node"))),
        out_specs=(both, P("node")),
        check_vma=False,
    )
```

```python
import functools

import jax
import jax.numpy as jnp
from jax import lax
from jax.experimental import pallas as pl
from jax.experimental.pallas import tpu as pltpu
from jax.sharding import PartitionSpec as P

CELL_DEV = 2048
LANES = 128
MESH = pl.DeviceIdType.MESH


def dot_rows(a, b):
    return lax.dot_general(a, b, (((1,), (1,)), ((), ())), preferred_element_type=jnp.float32)


def dot(a, b):
    return jnp.dot(a, b, preferred_element_type=jnp.float32)


def half(x):
    return x.astype(jnp.bfloat16)


class Tree:
    def __init__(self, buf, zsend, xsend, recv, leaf, node, zs, xs):
        self.buf, self.zsend, self.xsend, self.recv = buf, zsend, xsend, recv
        self.leaf, self.zs, self.xs = leaf, zs, xs
        self.z, self.x = node // xs, node % xs

    def copy(self, slot, dst, sem):
        return pltpu.make_async_remote_copy(
            src_ref=self.buf.at[slot],
            dst_ref=self.buf.at[slot],
            send_sem=sem,
            recv_sem=self.recv.at[slot],
            device_id=(self.leaf, dst),
            device_id_type=MESH,
        )

    def slot(self, zz):
        return zz * self.xs + self.x

    def up(self, zz, sem):
        return self.copy(self.slot(zz), (self.z + 1) * self.xs + self.x, self.zsend.at[sem])

    def down(self, zz, sem):
        return self.copy(self.slot(zz), (self.z - 1) * self.xs + self.x, self.zsend.at[sem])

    def across(self, zz):
        return [
            self.copy(
                self.slot(zz),
                self.z * self.xs + (self.x + i) % self.xs,
                self.xsend.at[zz * (self.xs - 1) + i - 1],
            )
            for i in range(1, self.xs)
        ]

    def start(self):
        pl.when(self.z + 1 < self.zs)(lambda: self.up(self.z, self.z).start())
        pl.when(self.z > 0)(lambda: self.down(self.z, self.zs).start())
        for c in self.across(self.z):
            c.start()

    def wait_slot(self, slot):
        self.copy(slot, 0, self.zsend.at[0]).wait_recv()

    def relay(self, hop, use):
        below, above = self.z - hop, self.z + hop

        @pl.when(below >= 0)
        def _():
            self.wait_slot(self.slot(below))
            pl.when(self.z + 1 < self.zs)(lambda: self.up(below, below).start())
            for c in self.across(below):
                c.start()

        @pl.when(above < self.zs)
        def _():
            self.wait_slot(self.slot(above))
            pl.when(self.z > 0)(lambda: self.down(above, above).start())
            for c in self.across(above):
                c.start()

        if use is not None:
            pl.when(below >= 0)(lambda: use(self.slot(below)))
            pl.when(above < self.zs)(lambda: use(self.slot(above)))

    def partners(self, use):
        for i in range(1, self.xs):
            @pl.loop(0, self.zs)
            def _(zz):
                slot = zz * self.xs + (self.x + i) % self.xs
                self.wait_slot(slot)
                if use is not None:
                    use(slot)

    def finish(self):
        @pl.loop(0, self.zs)
        def _(zz):
            for c in self.across(zz):
                c.wait_send()
            pl.when((zz <= self.z) & (self.z + 1 < self.zs))(
                lambda: self.up(zz, zz).wait_send()
            )
            pl.when((zz > self.z) & (self.z > 0))(lambda: self.down(zz, zz).wait_send())
        pl.when(self.z > 0)(lambda: self.down(self.z, self.zs).wait_send())


def kernel(
    n, leaves, xs,
    src, b_ref, bl_ref, br_ref, ci_ref, co_ref, shot_ref, cell_ref,
    sol_ref, grad_ref,
    src_v, rg, rhs, lg, cg, onehot, zacc, u_ref, t_ref, gpart, gbuf, lbuf,
    src_sem, own_sem, rz, rx, rr, a_send, a_recv, l_send, l_recv, cz, cx, cr,
    g_send, g_recv, h_send, h_recv,
):
    leaf, node = lax.axis_index("leaf"), lax.axis_index("node")
    zs = n // xs
    k, block = bl_ref.shape
    shots = src.shape[0]
    total = n * shots

    barrier = pltpu.get_barrier_semaphore()

    @pl.loop(1, n)
    def _(i):
        pl.semaphore_signal(
            barrier, inc=1, device_id=(leaf, (node + i) % n), device_id_type=MESH
        )

    @pl.loop(1, leaves)
    def _(i):
        pl.semaphore_signal(
            barrier, inc=1, device_id=((leaf + i) % leaves, node), device_id_type=MESH
        )

    src_copy = pltpu.make_async_copy(src, src_v, src_sem)
    src_copy.start()

    def columns(j):
        return pl.ds(pl.multiple_of(j * block, block), block)

    own_copy = pltpu.make_async_copy(src.at[:, columns(node)], rhs.at[node], own_sem)
    own_copy.start()

    b = b_ref[...]
    u = dot(ci_ref[...], b)
    u_ref[...] = u
    stacked = jnp.concatenate([co_ref[...], br_ref[...], half(u)], axis=0)
    t = dot_rows(stacked, b)
    t_ref[...] = t[:k]
    v = jnp.concatenate([bl_ref[...], half(t)], axis=0)
    rg[node, : 4 * k] = v
    rg[node, 4 * k :, : 4 * k] = half(dot_rows(ci_ref[...], v))
    rg[node, 4 * k :, 4 * k : 8 * k] = half(
        dot_rows(br_ref[...], jnp.concatenate([bl_ref[...], stacked], axis=0))
    )

    pl.semaphore_wait(barrier, n - 1 + leaves - 1)

    basis = Tree(rg, rz, rx, rr, leaf, node, zs, xs)
    basis.start()

    def shot_copy(j):
        return pltpu.make_async_remote_copy(
            src_ref=src.at[:, columns(j)],
            dst_ref=rhs.at[node],
            send_sem=a_send.at[j],
            recv_sem=a_recv.at[node],
            device_id=(leaf, j),
            device_id_type=MESH,
        )

    def peer(i, sign):
        z, x = node // xs, node % xs
        over = (i - zs) // zs + 1
        same = ((z + sign * i + zs) % zs) * xs + x
        cross = ((z + sign * (i % zs) + zs) % zs) * xs + (x + sign * over + xs) % xs
        return jnp.where(i < zs, same, cross)

    def send_shots(first, last):
        @pl.loop(first, last)
        def _(i):
            shot_copy(peer(i, 1)).start()

    send_shots(1, 2)

    rows_at = 256

    @pl.loop(0, n)
    def _(j):
        @pl.loop(0, total // rows_at)
        def _(r):
            at = pl.multiple_of(r * rows_at, rows_at)
            row = lax.broadcasted_iota(jnp.int32, (rows_at, shots), 0) + at
            onehot[j, pl.ds(at, rows_at), :] = half(jnp.where(row == shot_ref[j], 1.0, 0.0))

    src_copy.wait()
    zacc[...] = dot_rows(src_v[:, columns(node)], rg[node, : 4 * k])

    def project(slot):
        zacc[...] += dot_rows(src_v[:, columns(slot)], rg[slot, : 4 * k])

    for hop in range(1, zs):
        basis.relay(hop, project)
        if hop + 1 < zs:
            send_shots(hop + 1, hop + 2)
    crossing = n - zs
    send_shots(zs, zs + crossing // 4)
    basis.partners(project)

    s = rg[0, 4 * k :, :].astype(jnp.float32)
    for j in range(1, n):
        s = s + rg[j, 4 * k :, :].astype(jnp.float32)
    s3t = half(s[:, :k])
    ss = half(s[:, 4 * k : 8 * k])
    f = s[:, : 4 * k] + dot(s3t, ss)
    z = zacc[...]
    proj = half(z[:, :k])
    zf = z + dot(proj, ss)
    carry, z2, z3 = zf[:, k : 2 * k], zf[:, 2 * k : 3 * k], zf[:, 3 * k :]
    fb = f[:, 2 * k : 3 * k]
    lift = z3 + dot_rows(half(z2), s3t)
    lift_map = f[:, 3 * k :] + dot_rows(half(fb), s3t)
    lg[leaf, :shots] = half(jnp.concatenate([carry, lift], axis=1))
    lg[leaf, shots:] = half(-jnp.concatenate([f[:, k : 2 * k], lift_map], axis=1))

    def leaf_copy(i):
        return pltpu.make_async_remote_copy(
            src_ref=lg.at[leaf],
            dst_ref=lg.at[leaf],
            send_sem=l_send.at[i],
            recv_sem=l_recv.at[leaf],
            device_id=((leaf + i) % leaves, node),
            device_id_type=MESH,
        )

    for i in range(1, leaves):
        leaf_copy(i).start()
    send_shots(zs + crossing // 4, zs + crossing // 2)

    fc = half(u_ref[...] + dot(s3t, br_ref[...]))
    s1 = half(s[:, 5 * k : 6 * k])
    bc = half(
        t_ref[...]
        + lax.dot_general(s1, bl_ref[...], (((0,), (0,)), ((), ())), preferred_element_type=jnp.float32)
    )
    fwd_low = jnp.concatenate([br_ref[...], fc], axis=0)
    back_low = jnp.concatenate([bl_ref[...], bc], axis=0)

    for i in range(1, leaves):
        j = (leaf + i) % leaves
        pltpu.make_async_remote_copy(
            src_ref=lg.at[leaf], dst_ref=lg.at[j], send_sem=l_send.at[0],
            recv_sem=l_recv.at[j], device_id=(j, node), device_id_type=MESH,
        ).wait_recv()

    incoming = jnp.zeros((shots, k), jnp.float32)
    own_in = jnp.zeros((shots, k), jnp.float32)
    lifts = []
    for g in range(leaves):
        own_in = jnp.where(leaf == g, incoming, own_in)
        both = lg[g, :shots].astype(jnp.float32)
        if g > 0:
            both = both + dot(half(incoming), lg[g, shots:])
        incoming = both[:, :k]
        lifts.append(both[:, k:])
    returning = jnp.zeros((shots, k), jnp.float32)
    own_ret = jnp.zeros((shots, k), jnp.float32)
    for g in range(leaves - 1, -1, -1):
        own_ret = jnp.where(leaf == g, returning, own_ret)
        if g < leaves - 1:
            returning = lifts[g] + dot_rows(half(returning), lg[g, shots:, :k])
        else:
            returning = lifts[g]
    proj_fwd = z2 - dot(half(own_in), half(fb))
    cg[node] = half(
        jnp.concatenate([z[:, :k], -own_in, proj_fwd, -own_ret], axis=1)
    )

    coefs = Tree(cg, cz, cx, cr, leaf, node, zs, xs)
    coefs.start()
    for hop in range(1, zs):
        coefs.relay(hop, None)
    send_shots(zs + crossing // 2, n)
    coefs.partners(None)

    own_copy.wait()
    sums = jnp.zeros((1, block), jnp.float32)

    def shot_block(j, sums, first):
        low = cg[j]
        fwd = half(dot(rhs[j], b_ref[...]) + dot(low[:, : 2 * k], fwd_low))
        sol = half(dot_rows(fwd, b_ref[...]) + dot(low[:, 2 * k :], back_low))

        @pl.loop(0, total // rows_at)
        def _(r):
            rows = pl.ds(pl.multiple_of(r * rows_at, rows_at), rows_at)
            part = half(dot(onehot[j, rows, :], sol))
            if first:
                sol_ref[rows, :] = part
            else:
                sol_ref[rows, :] += part

        return sums + jnp.sum(
            sol.astype(jnp.float32) * fwd.astype(jnp.float32), axis=0, keepdims=True
        )

    sums = shot_block(node, sums, True)

    def later(i, sums):
        j = peer(i, -1)
        pltpu.make_async_remote_copy(
            src_ref=rhs.at[j], dst_ref=rhs.at[j], send_sem=a_send.at[j],
            recv_sem=a_recv.at[j], device_id=(leaf, j), device_id_type=MESH,
        ).wait_recv()
        return shot_block(j, sums, False)

    sums = lax.fori_loop(1, n, later, sums)
    corr = sums / jnp.sqrt(jnp.float32(total))

    cell = cell_ref[...]
    slab = gpart.shape[1]
    high = lax.broadcasted_iota(jnp.int32, (n * slab, block), 0) == cell // LANES
    low_hit = lax.broadcasted_iota(jnp.int32, (LANES, block), 0) == cell % LANES
    placed = lax.dot_general(
        jnp.where(high, corr, 0.0),
        jnp.where(low_hit, 1.0, 0.0),
        (((1,), (1,)), ((), ())),
        preferred_element_type=jnp.float32,
        precision=lax.Precision.HIGHEST,
    )
    gpart[...] = placed.reshape(gpart.shape)

    def slab_copy(j, frm):
        return pltpu.make_async_remote_copy(
            src_ref=gpart.at[j], dst_ref=gbuf.at[frm], send_sem=g_send.at[j],
            recv_sem=g_recv.at[frm], device_id=(leaf, j), device_id_type=MESH,
        )

    @pl.loop(1, n)
    def _(i):
        slab_copy((node + i) % n, node).start()

    own = gpart[node]

    def add_slab(i, acc):
        j = (node + n - i) % n
        slab_copy(j, j).wait_recv()
        return acc + gbuf[j]

    own = lax.fori_loop(1, n, add_slab, own)
    lbuf[leaf] = own

    def grad_copy(i, frm):
        return pltpu.make_async_remote_copy(
            src_ref=lbuf.at[leaf], dst_ref=lbuf.at[frm], send_sem=h_send.at[i],
            recv_sem=h_recv.at[frm], device_id=((leaf + i) % leaves, node),
            device_id_type=MESH,
        )

    for i in range(1, leaves):
        grad_copy(i, leaf).start()
    for i in range(1, leaves):
        grad_copy(i, (leaf + leaves - i) % leaves).wait_recv()
    acc = lbuf[0]
    for g in range(1, leaves):
        acc = acc + lbuf[g]
    grad_ref[...] = acc

    basis.finish()
    coefs.finish()
    for i in range(1, leaves):
        leaf_copy(i).wait_send()
        grad_copy(i, leaf).wait_send()

    @pl.loop(1, n)
    def _(i):
        j = (node + i) % n
        shot_copy(j).wait_send()
        slab_copy(j, node).wait_send()


def per_device(n, leaves, sources, block_inverse, basis_left, basis_right, couple_in, couple_out, column_of_shot, cell_map):
    xs = max(d for d in range(1, n + 1) if n % d == 0 and (2 * d * d <= n or d == 1))
    zs = n // xs
    k, block = basis_left.shape
    shots = sources.shape[0]
    total = n * shots
    slab = CELL_DEV // LANES
    bf16, f32 = jnp.bfloat16, jnp.float32
    dma = pltpu.SemaphoreType.DMA
    vmem = pl.BlockSpec(memory_space=pltpu.VMEM)
    solution_out, grad = pl.pallas_call(
        functools.partial(kernel, n, leaves, xs),
        out_shape=(
            jax.ShapeDtypeStruct((total, block), bf16),
            jax.ShapeDtypeStruct((slab, LANES), f32),
        ),
        in_specs=[pl.BlockSpec(memory_space=pl.ANY)] + [vmem] * 7,
        out_specs=(vmem, vmem),
        scratch_shapes=[
            pltpu.VMEM(sources.shape, bf16),
            pltpu.VMEM((n, 5 * k, block), bf16),
            pltpu.VMEM((n, shots, block), bf16),
            pltpu.VMEM((leaves, shots + k, 2 * k), bf16),
            pltpu.VMEM((n, shots, 4 * k), bf16),
            pltpu.VMEM((n, total, shots), bf16),
            pltpu.VMEM((shots, 4 * k), f32),
            pltpu.VMEM((k, block), f32),
            pltpu.VMEM((k, block), f32),
            pltpu.VMEM((n, slab, LANES), f32),
            pltpu.VMEM((n, slab, LANES), f32),
            pltpu.VMEM((leaves, slab, LANES), f32),
            dma, dma,
            dma((zs + 1,)), dma((max(zs * (xs - 1), 1),)), dma((n,)),
            dma((n,)), dma((n,)),
            dma((leaves,)), dma((leaves,)),
            dma((zs + 1,)), dma((max(zs * (xs - 1), 1),)), dma((n,)),
            dma((n,)), dma((n,)),
            dma((leaves,)), dma((leaves,)),
        ],
        compiler_params=pltpu.CompilerParams(
            collective_id=0, has_side_effects=True, vmem_limit_bytes=56 * 1024 * 1024
        ),
    )(
        sources, block_inverse, basis_left, basis_right, couple_in, couple_out,
        column_of_shot.reshape(n, 1, shots), cell_map.reshape(1, -1),
    )
    return solution_out, grad.reshape(-1)


def solution(mesh):
    both = P(None, ("leaf", "node"))
    return jax.shard_map(
        functools.partial(per_device, mesh.shape["node"], mesh.shape["leaf"]),
        mesh=mesh,
        in_specs=(P("node", "leaf"), both, both, both, both, both, P(), P(("leaf", "node"))),
        out_specs=(both, P("node")),
        check_vma=False,
    )
```

```python
import functools

import jax
import jax.numpy as jnp
from jax import lax
from jax.experimental import pallas as pl
from jax.experimental.pallas import tpu as pltpu
from jax.sharding import PartitionSpec as P

CELL_DEV = 2048
LANES = 128
MESH = pl.DeviceIdType.MESH


def dot_rows(a, b):
    return lax.dot_general(a, b, (((1,), (1,)), ((), ())), preferred_element_type=jnp.float32)


def dot(a, b):
    return jnp.dot(a, b, preferred_element_type=jnp.float32)


def half(x):
    return x.astype(jnp.bfloat16)


class Tree:
    def __init__(self, buf, zsend, xsend, recv, leaf, node, zs, xs):
        self.buf, self.zsend, self.xsend, self.recv = buf, zsend, xsend, recv
        self.leaf, self.zs, self.xs = leaf, zs, xs
        self.z, self.x = node // xs, node % xs

    def copy(self, slot, dst, sem):
        return pltpu.make_async_remote_copy(
            src_ref=self.buf.at[slot],
            dst_ref=self.buf.at[slot],
            send_sem=sem,
            recv_sem=self.recv.at[slot],
            device_id=(self.leaf, dst),
            device_id_type=MESH,
        )

    def slot(self, zz):
        return zz * self.xs + self.x

    def up(self, zz, sem):
        return self.copy(self.slot(zz), (self.z + 1) * self.xs + self.x, self.zsend.at[sem])

    def down(self, zz, sem):
        return self.copy(self.slot(zz), (self.z - 1) * self.xs + self.x, self.zsend.at[sem])

    def across(self, zz):
        return [
            self.copy(
                self.slot(zz),
                self.z * self.xs + (self.x + i) % self.xs,
                self.xsend.at[zz * (self.xs - 1) + i - 1],
            )
            for i in range(1, self.xs)
        ]

    def start(self):
        pl.when(self.z + 1 < self.zs)(lambda: self.up(self.z, self.z).start())
        pl.when(self.z > 0)(lambda: self.down(self.z, self.zs).start())
        for c in self.across(self.z):
            c.start()

    def wait_slot(self, slot):
        self.copy(slot, 0, self.zsend.at[0]).wait_recv()

    def relay(self, hop, use):
        below, above = self.z - hop, self.z + hop

        @pl.when(below >= 0)
        def _():
            self.wait_slot(self.slot(below))
            pl.when(self.z + 1 < self.zs)(lambda: self.up(below, below).start())
            for c in self.across(below):
                c.start()

        @pl.when(above < self.zs)
        def _():
            self.wait_slot(self.slot(above))
            pl.when(self.z > 0)(lambda: self.down(above, above).start())
            for c in self.across(above):
                c.start()

        if use is not None:
            pl.when(below >= 0)(lambda: use(self.slot(below)))
            pl.when(above < self.zs)(lambda: use(self.slot(above)))

    def partners(self, use):
        for i in range(1, self.xs):
            @pl.loop(0, self.zs)
            def _(zz):
                slot = zz * self.xs + (self.x + i) % self.xs
                self.wait_slot(slot)
                if use is not None:
                    use(slot)

    def finish(self):
        @pl.loop(0, self.zs)
        def _(zz):
            for c in self.across(zz):
                c.wait_send()
            pl.when((zz <= self.z) & (self.z + 1 < self.zs))(
                lambda: self.up(zz, zz).wait_send()
            )
            pl.when((zz > self.z) & (self.z > 0))(lambda: self.down(zz, zz).wait_send())
        pl.when(self.z > 0)(lambda: self.down(self.z, self.zs).wait_send())


def gather_kernel(
    n, leaves, xs,
    src, b_ref, bl_ref, br_ref, ci_ref, co_ref,
    rhs, cg, fwd_low, back_low,
    src_v, rg, lg, zacc, u_ref, t_ref,
    src_sem, own_sem, rz, rx, rr, a_send, a_recv, l_send, l_recv, cz, cx, cr,
):
    leaf, node = lax.axis_index("leaf"), lax.axis_index("node")
    zs = n // xs
    k, block = bl_ref.shape
    shots = src.shape[0]

    barrier = pltpu.get_barrier_semaphore()

    @pl.loop(1, n)
    def _(i):
        pl.semaphore_signal(
            barrier, inc=1, device_id=(leaf, (node + i) % n), device_id_type=MESH
        )

    @pl.loop(1, leaves)
    def _(i):
        pl.semaphore_signal(
            barrier, inc=1, device_id=((leaf + i) % leaves, node), device_id_type=MESH
        )

    src_copy = pltpu.make_async_copy(src, src_v, src_sem)
    src_copy.start()

    def columns(j):
        return pl.ds(pl.multiple_of(j * block, block), block)

    own_copy = pltpu.make_async_copy(src.at[:, columns(node)], rhs.at[node], own_sem)
    own_copy.start()

    b = b_ref[...]
    u = dot(ci_ref[...], b)
    u_ref[...] = u
    stacked = jnp.concatenate([co_ref[...], br_ref[...], half(u)], axis=0)
    t = dot_rows(stacked, b)
    t_ref[...] = t[:k]
    v = jnp.concatenate([bl_ref[...], half(t)], axis=0)
    rg[node, : 4 * k] = v
    rg[node, 4 * k :, : 4 * k] = half(dot_rows(ci_ref[...], v))
    rg[node, 4 * k :, 4 * k : 8 * k] = half(
        dot_rows(br_ref[...], jnp.concatenate([bl_ref[...], stacked], axis=0))
    )

    pl.semaphore_wait(barrier, n - 1 + leaves - 1)

    basis = Tree(rg, rz, rx, rr, leaf, node, zs, xs)
    basis.start()

    def shot_copy(j):
        return pltpu.make_async_remote_copy(
            src_ref=src.at[:, columns(j)],
            dst_ref=rhs.at[node],
            send_sem=a_send.at[j],
            recv_sem=a_recv.at[node],
            device_id=(leaf, j),
            device_id_type=MESH,
        )

    def peer(i, sign):
        z, x = node // xs, node % xs
        over = (i - zs) // zs + 1
        same = ((z + sign * i + zs) % zs) * xs + x
        cross = ((z + sign * (i % zs) + zs) % zs) * xs + (x + sign * over + xs) % xs
        return jnp.where(i < zs, same, cross)

    def send_shots(first, last):
        @pl.loop(first, last)
        def _(i):
            shot_copy(peer(i, 1)).start()

    send_shots(1, 2)

    src_copy.wait()
    zacc[...] = dot_rows(src_v[:, columns(node)], rg[node, : 4 * k])

    def project(slot):
        zacc[...] += dot_rows(src_v[:, columns(slot)], rg[slot, : 4 * k])

    for hop in range(1, zs):
        basis.relay(hop, project)
        if hop + 1 < zs:
            send_shots(hop + 1, hop + 2)
    crossing = n - zs
    send_shots(zs, zs + crossing // 4)
    basis.partners(project)

    s = rg[0, 4 * k :, :].astype(jnp.float32)
    for j in range(1, n):
        s = s + rg[j, 4 * k :, :].astype(jnp.float32)
    s3t = half(s[:, :k])
    ss = half(s[:, 4 * k : 8 * k])
    f = s[:, : 4 * k] + dot(s3t, ss)
    z = zacc[...]
    proj = half(z[:, :k])
    zf = z + dot(proj, ss)
    carry, z2, z3 = zf[:, k : 2 * k], zf[:, 2 * k : 3 * k], zf[:, 3 * k :]
    fb = f[:, 2 * k : 3 * k]
    lift = z3 + dot_rows(half(z2), s3t)
    lift_map = f[:, 3 * k :] + dot_rows(half(fb), s3t)
    lg[leaf, :shots] = half(jnp.concatenate([carry, lift], axis=1))
    lg[leaf, shots:] = half(-jnp.concatenate([f[:, k : 2 * k], lift_map], axis=1))

    def leaf_copy(i):
        return pltpu.make_async_remote_copy(
            src_ref=lg.at[leaf],
            dst_ref=lg.at[leaf],
            send_sem=l_send.at[i],
            recv_sem=l_recv.at[leaf],
            device_id=((leaf + i) % leaves, node),
            device_id_type=MESH,
        )

    for i in range(1, leaves):
        leaf_copy(i).start()
    send_shots(zs + crossing // 4, zs + crossing // 2)

    fc = half(u_ref[...] + dot(s3t, br_ref[...]))
    s1 = half(s[:, 5 * k : 6 * k])
    bc = half(
        t_ref[...]
        + lax.dot_general(s1, bl_ref[...], (((0,), (0,)), ((), ())), preferred_element_type=jnp.float32)
    )
    fwd_low[...] = jnp.concatenate([br_ref[...], fc], axis=0)
    back_low[...] = jnp.concatenate([bl_ref[...], bc], axis=0)

    for i in range(1, leaves):
        j = (leaf + i) % leaves
        pltpu.make_async_remote_copy(
            src_ref=lg.at[leaf], dst_ref=lg.at[j], send_sem=l_send.at[0],
            recv_sem=l_recv.at[j], device_id=(j, node), device_id_type=MESH,
        ).wait_recv()

    incoming = jnp.zeros((shots, k), jnp.float32)
    own_in = jnp.zeros((shots, k), jnp.float32)
    lifts = []
    for g in range(leaves):
        own_in = jnp.where(leaf == g, incoming, own_in)
        both = lg[g, :shots].astype(jnp.float32)
        if g > 0:
            both = both + dot(half(incoming), lg[g, shots:])
        incoming = both[:, :k]
        lifts.append(both[:, k:])
    returning = jnp.zeros((shots, k), jnp.float32)
    own_ret = jnp.zeros((shots, k), jnp.float32)
    for g in range(leaves - 1, -1, -1):
        own_ret = jnp.where(leaf == g, returning, own_ret)
        if g < leaves - 1:
            returning = lifts[g] + dot_rows(half(returning), lg[g, shots:, :k])
        else:
            returning = lifts[g]
    proj_fwd = z2 - dot(half(own_in), half(fb))
    cg[node] = half(
        jnp.concatenate([z[:, :k], -own_in, proj_fwd, -own_ret], axis=1)
    )

    coefs = Tree(cg, cz, cx, cr, leaf, node, zs, xs)
    coefs.start()
    for hop in range(1, zs):
        coefs.relay(hop, None)
    send_shots(zs + crossing // 2, n)
    coefs.partners(None)

    own_copy.wait()

    @pl.loop(1, n)
    def _(i):
        j = peer(i, -1)
        pltpu.make_async_remote_copy(
            src_ref=rhs.at[j], dst_ref=rhs.at[j], send_sem=a_send.at[j],
            recv_sem=a_recv.at[j], device_id=(leaf, j), device_id_type=MESH,
        ).wait_recv()

    basis.finish()
    coefs.finish()
    for i in range(1, leaves):
        leaf_copy(i).wait_send()

    @pl.loop(1, n)
    def _(i):
        shot_copy((node + i) % n).wait_send()


def sweep_kernel(
    rhs, low, b_ref, fwd_low, back_low, shot_ref, sol_ref, corr_ref, sol, bt, sums
):
    n, shots, block = rhs.shape
    k2 = fwd_low.shape[0]
    total = n * shots
    step = pl.program_id(0)

    @pl.when(step == 0)
    def _():
        bt[...] = b_ref[...].T
        sums[...] = jnp.zeros_like(sums)

        @pl.loop(0, n)
        def _(j):
            c = low[j]
            fwd = half(dot(rhs[j], b_ref[...]) + dot(c[:, :k2], fwd_low[...]))
            back = half(dot(fwd, bt[...]) + dot(c[:, k2:], back_low[...]))
            sol[pl.ds(pl.multiple_of(j * shots, shots), shots), :] = back
            sums[...] += jnp.sum(
                back.astype(jnp.float32) * fwd.astype(jnp.float32), axis=0, keepdims=True
            )
        corr_ref[...] = sums[...] / jnp.sqrt(jnp.float32(total))

    rows = sol_ref.shape[0]
    row = lax.broadcasted_iota(jnp.int32, (rows, total), 0) + step * rows
    hit = half(jnp.where(row == shot_ref[...], 1.0, 0.0))
    sol_ref[...] = half(dot(hit, sol[...]))


def gradient_kernel(
    n, leaves, corr_ref, cell_ref, grad_ref, gpart, gbuf, lbuf, g_send, g_recv, h_send, h_recv
):
    leaf, node = lax.axis_index("leaf"), lax.axis_index("node")
    block = corr_ref.shape[1]
    corr = corr_ref[...]
    barrier = pltpu.get_barrier_semaphore()

    @pl.loop(1, n)
    def _(i):
        pl.semaphore_signal(
            barrier, inc=1, device_id=(leaf, (node + i) % n), device_id_type=MESH
        )

    @pl.loop(1, leaves)
    def _(i):
        pl.semaphore_signal(
            barrier, inc=1, device_id=((leaf + i) % leaves, node), device_id_type=MESH
        )

    cell = cell_ref[...]
    slab = gpart.shape[1]
    high = lax.broadcasted_iota(jnp.int32, (n * slab, block), 0) == cell // LANES
    low_hit = lax.broadcasted_iota(jnp.int32, (LANES, block), 0) == cell % LANES
    placed = lax.dot_general(
        jnp.where(high, corr, 0.0),
        jnp.where(low_hit, 1.0, 0.0),
        (((1,), (1,)), ((), ())),
        preferred_element_type=jnp.float32,
        precision=lax.Precision.HIGHEST,
    )
    gpart[...] = placed.reshape(gpart.shape)
    pl.semaphore_wait(barrier, n - 1 + leaves - 1)

    def slab_copy(j, frm):
        return pltpu.make_async_remote_copy(
            src_ref=gpart.at[j], dst_ref=gbuf.at[frm], send_sem=g_send.at[j],
            recv_sem=g_recv.at[frm], device_id=(leaf, j), device_id_type=MESH,
        )

    @pl.loop(1, n)
    def _(i):
        slab_copy((node + i) % n, node).start()

    own = gpart[node]

    def add_slab(i, acc):
        j = (node + n - i) % n
        slab_copy(j, j).wait_recv()
        return acc + gbuf[j]

    own = lax.fori_loop(1, n, add_slab, own)
    lbuf[leaf] = own

    def grad_copy(i, frm):
        return pltpu.make_async_remote_copy(
            src_ref=lbuf.at[leaf], dst_ref=lbuf.at[frm], send_sem=h_send.at[i],
            recv_sem=h_recv.at[frm], device_id=((leaf + i) % leaves, node),
            device_id_type=MESH,
        )

    for i in range(1, leaves):
        grad_copy(i, leaf).start()
    for i in range(1, leaves):
        grad_copy(i, (leaf + leaves - i) % leaves).wait_recv()
    acc = lbuf[0]
    for g in range(1, leaves):
        acc = acc + lbuf[g]
    grad_ref[...] = acc

    for i in range(1, leaves):
        grad_copy(i, leaf).wait_send()

    @pl.loop(1, n)
    def _(i):
        slab_copy((node + i) % n, node).wait_send()


def per_device(n, leaves, sources, block_inverse, basis_left, basis_right, couple_in, couple_out, column_of_shot, cell_map):
    xs = max(d for d in range(1, n + 1) if n % d == 0 and (2 * d * d <= n or d == 1))
    zs = n // xs
    k, block = basis_left.shape
    shots = sources.shape[0]
    total = n * shots
    slab = CELL_DEV // LANES
    bf16, f32 = jnp.bfloat16, jnp.float32
    dma = pltpu.SemaphoreType.DMA
    vmem = pl.BlockSpec(memory_space=pltpu.VMEM)
    rhs, low, fwd_low, back_low = pl.pallas_call(
        functools.partial(gather_kernel, n, leaves, xs),
        out_shape=(
            jax.ShapeDtypeStruct((n, shots, block), bf16),
            jax.ShapeDtypeStruct((n, shots, 4 * k), bf16),
            jax.ShapeDtypeStruct((2 * k, block), bf16),
            jax.ShapeDtypeStruct((2 * k, block), bf16),
        ),
        in_specs=[pl.BlockSpec(memory_space=pl.ANY)] + [vmem] * 5,
        out_specs=(pl.BlockSpec(memory_space=pl.ANY), vmem, vmem, vmem),
        scratch_shapes=[
            pltpu.VMEM(sources.shape, bf16),
            pltpu.VMEM((n, 5 * k, block), bf16),
            pltpu.VMEM((leaves, shots + k, 2 * k), bf16),
            pltpu.VMEM((shots, 4 * k), f32),
            pltpu.VMEM((k, block), f32),
            pltpu.VMEM((k, block), f32),
            dma, dma,
            dma((zs + 1,)), dma((max(zs * (xs - 1), 1),)), dma((n,)),
            dma((n,)), dma((n,)),
            dma((leaves,)), dma((leaves,)),
            dma((zs + 1,)), dma((max(zs * (xs - 1), 1),)), dma((n,)),
        ],
        compiler_params=pltpu.CompilerParams(
            collective_id=0, has_side_effects=True, vmem_limit_bytes=48 * 1024 * 1024
        ),
    )(sources, block_inverse, basis_left, basis_right, couple_in, couple_out)

    rows = min(256, total)
    whole = lambda *dims: pl.BlockSpec(dims, lambda r: (0,) * len(dims))
    solution_out, corr = pl.pallas_call(
        sweep_kernel,
        grid=(total // rows,),
        out_shape=(
            jax.ShapeDtypeStruct((total, block), bf16),
            jax.ShapeDtypeStruct((1, block), f32),
        ),
        in_specs=[
            whole(n, shots, block), whole(n, shots, 4 * k), whole(block, block),
            whole(2 * k, block), whole(2 * k, block), whole(1, total),
        ],
        out_specs=(pl.BlockSpec((rows, block), lambda r: (r, 0)), whole(1, block)),
        scratch_shapes=[
            pltpu.VMEM((total, block), bf16),
            pltpu.VMEM((block, block), bf16),
            pltpu.VMEM((1, block), f32),
        ],
        compiler_params=pltpu.CompilerParams(vmem_limit_bytes=48 * 1024 * 1024),
    )(rhs, low, block_inverse, fwd_low, back_low, column_of_shot.reshape(1, -1))

    grad = pl.pallas_call(
        functools.partial(gradient_kernel, n, leaves),
        out_shape=jax.ShapeDtypeStruct((slab, LANES), f32),
        in_specs=[vmem] * 2,
        out_specs=vmem,
        scratch_shapes=[
            pltpu.VMEM((n, slab, LANES), f32),
            pltpu.VMEM((n, slab, LANES), f32),
            pltpu.VMEM((leaves, slab, LANES), f32),
            dma((n,)), dma((n,)),
            dma((leaves,)), dma((leaves,)),
        ],
        compiler_params=pltpu.CompilerParams(
            collective_id=1, has_side_effects=True, vmem_limit_bytes=16 * 1024 * 1024
        ),
    )(corr, cell_map.reshape(1, -1))
    return solution_out, grad.reshape(-1)


def solution(mesh):
    both = P(None, ("leaf", "node"))
    return jax.shard_map(
        functools.partial(per_device, mesh.shape["node"], mesh.shape["leaf"]),
        mesh=mesh,
        in_specs=(P("node", "leaf"), both, both, both, both, both, P(), P(("leaf", "node"))),
        out_specs=(both, P("node")),
        check_vma=False,
    )
```

```python
import functools

import jax
import jax.numpy as jnp
from jax import lax
from jax.experimental import pallas as pl
from jax.experimental.pallas import tpu as pltpu
from jax.sharding import PartitionSpec as P

CELL_DEV = 2048
LANES = 128
MESH = pl.DeviceIdType.MESH


def dot_rows(a, b):
    return lax.dot_general(a, b, (((1,), (1,)), ((), ())), preferred_element_type=jnp.float32)


def dot(a, b):
    return jnp.dot(a, b, preferred_element_type=jnp.float32)


def half(x):
    return x.astype(jnp.bfloat16)


class Tree:
    def __init__(self, buf, zsend, xsend, recv, leaf, node, zs, xs):
        self.buf, self.zsend, self.xsend, self.recv = buf, zsend, xsend, recv
        self.leaf, self.zs, self.xs = leaf, zs, xs
        self.z, self.x = node // xs, node % xs

    def copy(self, slot, dst, sem):
        return pltpu.make_async_remote_copy(
            src_ref=self.buf.at[slot],
            dst_ref=self.buf.at[slot],
            send_sem=sem,
            recv_sem=self.recv.at[slot],
            device_id=(self.leaf, dst),
            device_id_type=MESH,
        )

    def slot(self, zz):
        return zz if self.xsend is None else zz * self.xs + self.x

    def up(self, zz, sem):
        return self.copy(self.slot(zz), (self.z + 1) * self.xs + self.x, self.zsend.at[sem])

    def down(self, zz, sem):
        return self.copy(self.slot(zz), (self.z - 1) * self.xs + self.x, self.zsend.at[sem])

    def across(self, zz):
        if self.xsend is None:
            return []
        return [
            self.copy(
                self.slot(zz),
                self.z * self.xs + (self.x + i) % self.xs,
                self.xsend.at[zz * (self.xs - 1) + i - 1],
            )
            for i in range(1, self.xs)
        ]

    def start(self):
        pl.when(self.z + 1 < self.zs)(lambda: self.up(self.z, self.z).start())
        pl.when(self.z > 0)(lambda: self.down(self.z, self.zs).start())
        for c in self.across(self.z):
            c.start()

    def wait_slot(self, slot):
        self.copy(slot, 0, self.zsend.at[0]).wait_recv()

    def relay(self, hop, use):
        below, above = self.z - hop, self.z + hop

        @pl.when(below >= 0)
        def _():
            self.wait_slot(self.slot(below))
            pl.when(self.z + 1 < self.zs)(lambda: self.up(below, below).start())
            for c in self.across(below):
                c.start()

        @pl.when(above < self.zs)
        def _():
            self.wait_slot(self.slot(above))
            pl.when(self.z > 0)(lambda: self.down(above, above).start())
            for c in self.across(above):
                c.start()

        if use is not None:
            pl.when(below >= 0)(lambda: use(self.slot(below)))
            pl.when(above < self.zs)(lambda: use(self.slot(above)))

    def partners(self, use):
        for i in range(1, self.xs):
            @pl.loop(0, self.zs)
            def _(zz):
                slot = zz * self.xs + (self.x + i) % self.xs
                self.wait_slot(slot)
                if use is not None:
                    use(slot)

    def finish(self):
        @pl.loop(0, self.zs)
        def _(zz):
            for c in self.across(zz):
                c.wait_send()
            pl.when((zz <= self.z) & (self.z + 1 < self.zs))(
                lambda: self.up(zz, zz).wait_send()
            )
            pl.when((zz > self.z) & (self.z > 0))(lambda: self.down(zz, zz).wait_send())
        pl.when(self.z > 0)(lambda: self.down(self.z, self.zs).wait_send())


def kernel(
    n, leaves, xs,
    src, b_hbm, bl_hbm, br_hbm, ci_hbm, co_hbm, shot_ref, cell_ref,
    sol_ref, grad_ref,
    b_ref, bl_ref, br_ref, ci_ref, co_ref, bt, col, buf, rg, zpart, zbuf, lg, cg,
    fwd_low, back_low, onehot, sols, zacc, u_ref, t_ref, sums, gpart, gbuf, lbuf,
    in_sem, col_sem, rz, rr, x_send, o_send, f_send, a_recv, z_send, z_recv,
    l_send, l_recv, cz, cx, cr, g_send, g_recv, h_send, h_recv,
):
    leaf, node = lax.axis_index("leaf"), lax.axis_index("node")
    zs = n // xs
    z_at, x_at = node // xs, node % xs
    k, block = bl_ref.shape
    shots = src.shape[0]
    total = n * shots

    pairs = (
        (b_hbm, b_ref), (bl_hbm, bl_ref), (br_hbm, br_ref), (ci_hbm, ci_ref), (co_hbm, co_ref),
    )
    loads = [pltpu.make_async_copy(a, v, in_sem.at[i]) for i, (a, v) in enumerate(pairs)]
    for c in loads:
        c.start()

    barrier = pltpu.get_barrier_semaphore()

    @pl.loop(1, n)
    def _(i):
        pl.semaphore_signal(
            barrier, inc=1, device_id=(leaf, (node + i) % n), device_id_type=MESH
        )

    @pl.loop(1, leaves)
    def _(i):
        pl.semaphore_signal(
            barrier, inc=1, device_id=((leaf + i) % leaves, node), device_id_type=MESH
        )

    def columns(j):
        return pl.ds(pl.multiple_of(j * block, block), block)

    def column_copy(zz):
        return pltpu.make_async_copy(
            src.at[:, columns(zz * xs + x_at)], col.at[zz], col_sem.at[zz]
        )

    for zz in range(zs):
        column_copy(zz).start()

    def send(a, slot, sem, dst):
        return pltpu.make_async_remote_copy(
            src_ref=a, dst_ref=buf.at[slot], send_sem=sem, recv_sem=a_recv.at[slot],
            device_id=(leaf, dst), device_id_type=MESH,
        )

    def arrived(slot):
        send(buf.at[slot], slot, f_send.at[0], node).wait_recv()

    def passing(x, zz):
        return jnp.where(zz == z_at, z_at * xs + x, n + x * zs + zz)

    def over_x(i, d):
        x, zz = (x_at + i) % xs, (z_at + d) % zs
        return send(
            src.at[:, columns(zz * xs + x)], passing(x_at, zz),
            x_send.at[(i - 1) * zs + d], z_at * xs + x,
        )

    def own_over_z(d):
        dst = ((z_at + d) % zs) * xs + x_at
        return send(src.at[:, columns(dst)], node, o_send.at[d], dst)

    def onward(i, d):
        x, zz = (x_at + i) % xs, (z_at + d) % zs
        slot = passing(x, zz)
        return send(buf.at[slot], z_at * xs + x, f_send.at[(i - 1) * zs + d], zz * xs + x_at)

    pl.semaphore_wait(barrier, n - 1 + leaves - 1)

    for i in range(1, xs):
        @pl.loop(1, zs + 1)
        def _(d):
            over_x(i, d % zs).start()

    if zs > 1:
        own_over_z(1).start()

    for c in loads:
        c.wait()
    b = b_ref[...]
    u = dot(ci_ref[...], b)
    u_ref[...] = u
    stacked = jnp.concatenate([co_ref[...], br_ref[...], half(u)], axis=0)
    t = dot_rows(stacked, b)
    t_ref[...] = t[:k]
    v = jnp.concatenate([bl_ref[...], half(t)], axis=0)
    rg[z_at, : 4 * k] = v
    rg[z_at, 4 * k :, : 4 * k] = half(dot_rows(ci_ref[...], v))
    rg[z_at, 4 * k :, 4 * k : 8 * k] = half(
        dot_rows(br_ref[...], jnp.concatenate([bl_ref[...], stacked], axis=0))
    )
    basis = Tree(rg, rz, None, rr, leaf, node, zs, xs)
    basis.start()

    bt[...] = b.T

    rows_at = min(256, total)

    @pl.loop(0, total // rows_at)
    def _(r):
        at = pl.multiple_of(r * rows_at, rows_at)
        row = lax.broadcasted_iota(jnp.int32, (rows_at, total), 0) + at
        onehot[pl.ds(at, rows_at), :] = half(jnp.where(row == shot_ref[...], 1.0, 0.0))

    for zz in range(zs):
        column_copy(zz).wait()
    zacc[...] = dot_rows(col[z_at], rg[z_at, : 4 * k])

    def project(zz):
        zacc[...] += dot_rows(col[zz], rg[zz, : 4 * k])

    for hop in range(1, zs):
        basis.relay(hop, project)
        if hop + 1 < zs:
            own_over_z(hop + 1).start()

    late = max(zs - zs // 3, 1)
    for i in range(1, xs):
        @pl.loop(1, zs)
        def _(d):
            arrived(passing((x_at + i) % xs, (z_at + d) % zs))
            pl.when(d < late)(lambda: onward(i, d).start())
        arrived(passing((x_at + i) % xs, z_at))

    s_part = rg[0, 4 * k :, :].astype(jnp.float32)
    for j in range(1, zs):
        s_part = s_part + rg[j, 4 * k :, :].astype(jnp.float32)

    def partial_copy(i, frm):
        return pltpu.make_async_remote_copy(
            src_ref=zpart.at[i - 1], dst_ref=zbuf.at[frm], send_sem=z_send.at[i],
            recv_sem=z_recv.at[frm], device_id=(leaf, z_at * xs + (x_at + i) % xs),
            device_id_type=MESH,
        )

    for i in range(1, xs):
        x = (x_at + i) % xs
        acc = jnp.zeros((shots, 4 * k), jnp.float32)
        for zz in range(zs):
            acc = acc + dot_rows(buf[passing(x, zz)], rg[zz, : 4 * k])
        zpart[i - 1, :shots] = half(acc)
        zpart[i - 1, shots : shots + k] = half(s_part[:, : 4 * k])
        zpart[i - 1, shots + k :] = half(s_part[:, 4 * k : 8 * k])
        partial_copy(i, x_at).start()
    z = zacc[...]
    left, right = s_part[:, : 4 * k], s_part[:, 4 * k : 8 * k]
    for i in range(1, xs):
        x = (x_at + i) % xs
        partial_copy(i, x).wait_recv()
        z = z + zbuf[x, :shots].astype(jnp.float32)
        left = left + zbuf[x, shots : shots + k].astype(jnp.float32)
        right = right + zbuf[x, shots + k :].astype(jnp.float32)

    s3t = half(left[:, :k])
    ss = half(right)
    f = left + dot(s3t, ss)
    proj = half(z[:, :k])
    zf = z + dot(proj, ss)
    carry, z2, z3 = zf[:, k : 2 * k], zf[:, 2 * k : 3 * k], zf[:, 3 * k :]
    fb = f[:, 2 * k : 3 * k]
    lift = z3 + dot_rows(half(z2), s3t)
    lift_map = f[:, 3 * k :] + dot_rows(half(fb), s3t)
    lg[leaf, :shots] = half(jnp.concatenate([carry, lift], axis=1))
    lg[leaf, shots:] = half(-jnp.concatenate([f[:, k : 2 * k], lift_map], axis=1))

    def leaf_copy(i, frm):
        return pltpu.make_async_remote_copy(
            src_ref=lg.at[leaf], dst_ref=lg.at[frm], send_sem=l_send.at[i],
            recv_sem=l_recv.at[frm], device_id=((leaf + i) % leaves, node),
            device_id_type=MESH,
        )

    for i in range(1, leaves):
        leaf_copy(i, leaf).start()

    fc = half(u_ref[...] + dot(s3t, br_ref[...]))
    s1 = half(right[:, k : 2 * k])
    bc = half(
        t_ref[...]
        + lax.dot_general(s1, bl_ref[...], (((0,), (0,)), ((), ())), preferred_element_type=jnp.float32)
    )
    fwd_low[...] = jnp.concatenate([br_ref[...], fc], axis=0)
    back_low[...] = jnp.concatenate([bl_ref[...], bc], axis=0)

    for i in range(1, leaves):
        leaf_copy(i, (leaf + i) % leaves).wait_recv()

    incoming = jnp.zeros((shots, k), jnp.float32)
    own_in = jnp.zeros((shots, k), jnp.float32)
    lifts = []
    for g in range(leaves):
        own_in = jnp.where(leaf == g, incoming, own_in)
        both = lg[g, :shots].astype(jnp.float32)
        if g > 0:
            both = both + dot(half(incoming), lg[g, shots:])
        incoming = both[:, :k]
        lifts.append(both[:, k:])
    returning = jnp.zeros((shots, k), jnp.float32)
    own_ret = jnp.zeros((shots, k), jnp.float32)
    for g in range(leaves - 1, -1, -1):
        own_ret = jnp.where(leaf == g, returning, own_ret)
        if g < leaves - 1:
            returning = lifts[g] + dot_rows(half(returning), lg[g, shots:, :k])
        else:
            returning = lifts[g]
    proj_fwd = z2 - dot(half(own_in), half(fb))
    cg[node] = half(
        jnp.concatenate([z[:, :k], -own_in, proj_fwd, -own_ret], axis=1)
    )

    coefs = Tree(cg, cz, cx, cr, leaf, node, zs, xs)
    coefs.start()
    for hop in range(1, zs):
        coefs.relay(hop, None)
        if hop == 1:
            for i in range(1, xs):
                @pl.loop(late, zs)
                def _(d):
                    onward(i, d).start()
    coefs.partners(None)

    sums[...] = jnp.zeros_like(sums)

    def shot_block(j, rhs):
        low = cg[j]
        fwd = half(dot(rhs, b_ref[...]) + dot(low[:, : 2 * k], fwd_low[...]))
        sol = half(dot(fwd, bt[...]) + dot(low[:, 2 * k :], back_low[...]))
        sols[pl.ds(pl.multiple_of(j * shots, shots), shots), :] = sol
        sums[...] += jnp.sum(
            sol.astype(jnp.float32) * fwd.astype(jnp.float32), axis=0, keepdims=True
        )

    shot_block(node, col[z_at])
    for i in range(1, xs):
        j = z_at * xs + (x_at + i) % xs
        shot_block(j, buf[j])
    for i in range(xs):
        @pl.loop(1, zs)
        def _(d):
            j = ((z_at + zs - d) % zs) * xs + (x_at + i) % xs
            arrived(j)
            shot_block(j, buf[j])

    corr = sums[...] / jnp.sqrt(jnp.float32(total))

    cell = cell_ref[...]
    slab = gpart.shape[1]
    high = lax.broadcasted_iota(jnp.int32, (n * slab, block), 0) == cell // LANES
    low_hit = lax.broadcasted_iota(jnp.int32, (LANES, block), 0) == cell % LANES
    placed = lax.dot_general(
        jnp.where(high, corr, 0.0),
        jnp.where(low_hit, 1.0, 0.0),
        (((1,), (1,)), ((), ())),
        preferred_element_type=jnp.float32,
        precision=lax.Precision.HIGHEST,
    )
    gpart[...] = placed.reshape(gpart.shape)

    def slab_copy(j, frm):
        return pltpu.make_async_remote_copy(
            src_ref=gpart.at[j], dst_ref=gbuf.at[frm], send_sem=g_send.at[j],
            recv_sem=g_recv.at[frm], device_id=(leaf, j), device_id_type=MESH,
        )

    @pl.loop(1, n)
    def _(i):
        slab_copy((node + i) % n, node).start()

    def permute(first, last):
        @pl.loop(first, last)
        def _(r):
            rows = pl.ds(pl.multiple_of(r * rows_at, rows_at), rows_at)
            sol_ref[rows, :] = half(dot(onehot[rows, :], sols[...]))

    steps = total // rows_at
    permute(0, steps // 2)

    own = gpart[node]

    def add_slab(i, acc):
        j = (node + n - i) % n
        slab_copy(j, j).wait_recv()
        return acc + gbuf[j]

    own = lax.fori_loop(1, n, add_slab, own)
    lbuf[leaf] = own

    def grad_copy(i, frm):
        return pltpu.make_async_remote_copy(
            src_ref=lbuf.at[leaf], dst_ref=lbuf.at[frm], send_sem=h_send.at[i],
            recv_sem=h_recv.at[frm], device_id=((leaf + i) % leaves, node),
            device_id_type=MESH,
        )

    for i in range(1, leaves):
        grad_copy(i, leaf).start()
    permute(steps // 2, steps)
    for i in range(1, leaves):
        grad_copy(i, (leaf + leaves - i) % leaves).wait_recv()
    acc = lbuf[0]
    for g in range(1, leaves):
        acc = acc + lbuf[g]
    grad_ref[...] = acc


    basis.finish()
    coefs.finish()
    for i in range(1, leaves):
        leaf_copy(i, leaf).wait_send()
        grad_copy(i, leaf).wait_send()
    for i in range(1, xs):
        partial_copy(i, x_at).wait_send()

        @pl.loop(0, zs)
        def _(d):
            over_x(i, d).wait_send()
            pl.when(d > 0)(lambda: onward(i, d).wait_send())

    @pl.loop(1, zs)
    def _(d):
        own_over_z(d).wait_send()

    @pl.loop(1, n)
    def _(i):
        slab_copy((node + i) % n, node).wait_send()


def per_device(n, leaves, sources, block_inverse, basis_left, basis_right, couple_in, couple_out, column_of_shot, cell_map):
    xs = max(d for d in range(1, n + 1) if n % d == 0 and (2 * d * d <= n or d == 1))
    zs = n // xs
    k, block = basis_left.shape
    shots = sources.shape[0]
    total = n * shots
    slab = CELL_DEV // LANES
    bf16, f32 = jnp.bfloat16, jnp.float32
    dma = pltpu.SemaphoreType.DMA
    anywhere = pl.BlockSpec(memory_space=pl.ANY)
    vmem = pl.BlockSpec(memory_space=pltpu.VMEM)
    vectors = max(zs * (xs - 1), 1)
    small = pltpu.VMEM((k, block), bf16)
    solution_out, grad = pl.pallas_call(
        functools.partial(kernel, n, leaves, xs),
        out_shape=(
            jax.ShapeDtypeStruct((total, block), bf16),
            jax.ShapeDtypeStruct((slab, LANES), f32),
        ),
        in_specs=[anywhere] * 6 + [vmem] * 2,
        out_specs=(vmem, vmem),
        scratch_shapes=[
            pltpu.VMEM((block, block), bf16), small, small, small, small,
            pltpu.VMEM((block, block), bf16),
            pltpu.VMEM((zs, shots, block), bf16),
            pltpu.VMEM((2 * n, shots, block), bf16),
            pltpu.VMEM((zs, 5 * k, block), bf16),
            pltpu.VMEM((max(xs - 1, 1), shots + 2 * k, 4 * k), bf16),
            pltpu.VMEM((xs, shots + 2 * k, 4 * k), bf16),
            pltpu.VMEM((leaves, shots + k, 2 * k), bf16),
            pltpu.VMEM((n, shots, 4 * k), bf16),
            pltpu.VMEM((2 * k, block), bf16),
            pltpu.VMEM((2 * k, block), bf16),
            pltpu.VMEM((total, total), bf16),
            pltpu.VMEM((total, block), bf16),
            pltpu.VMEM((shots, 4 * k), f32),
            pltpu.VMEM((k, block), f32),
            pltpu.VMEM((k, block), f32),
            pltpu.VMEM((1, block), f32),
            pltpu.VMEM((n, slab, LANES), f32),
            pltpu.VMEM((n, slab, LANES), f32),
            pltpu.VMEM((leaves, slab, LANES), f32),
            dma((5,)), dma((zs,)),
            dma((zs + 1,)), dma((zs,)),
            dma((vectors,)), dma((zs,)), dma((vectors,)), dma((2 * n,)),
            dma((xs,)), dma((xs,)),
            dma((leaves,)), dma((leaves,)),
            dma((zs + 1,)), dma((vectors,)), dma((n,)),
            dma((n,)), dma((n,)),
            dma((leaves,)), dma((leaves,)),
        ],
        compiler_params=pltpu.CompilerParams(
            collective_id=0, has_side_effects=True, vmem_limit_bytes=56 * 1024 * 1024
        ),
    )(
        sources, block_inverse, basis_left, basis_right, couple_in, couple_out,
        column_of_shot.reshape(1, -1), cell_map.reshape(1, -1),
    )
    return solution_out, grad.reshape(-1)


def solution(mesh):
    both = P(None, ("leaf", "node"))
    return jax.shard_map(
        functools.partial(per_device, mesh.shape["node"], mesh.shape["leaf"]),
        mesh=mesh,
        in_specs=(P("node", "leaf"), both, both, both, both, both, P(), P(("leaf", "node"))),
        out_specs=(both, P("node")),
        check_vma=False,
    )
```

```python
import functools

import jax
import jax.numpy as jnp
from jax import lax
from jax.experimental import pallas as pl
from jax.experimental.pallas import tpu as pltpu
from jax.sharding import PartitionSpec as P

CELL_DEV = 2048
LANES = 128
MESH = pl.DeviceIdType.MESH


def dot_rows(a, b):
    return lax.dot_general(a, b, (((1,), (1,)), ((), ())), preferred_element_type=jnp.float32)


def dot(a, b):
    return jnp.dot(a, b, preferred_element_type=jnp.float32)


def half(x):
    return x.astype(jnp.bfloat16)


class Tree:
    def __init__(self, buf, zsend, xsend, recv, leaf, node, zs, xs):
        self.buf, self.zsend, self.xsend, self.recv = buf, zsend, xsend, recv
        self.leaf, self.zs, self.xs = leaf, zs, xs
        self.z, self.x = node // xs, node % xs

    def copy(self, slot, dst, sem):
        return pltpu.make_async_remote_copy(
            src_ref=self.buf.at[slot],
            dst_ref=self.buf.at[slot],
            send_sem=sem,
            recv_sem=self.recv.at[slot],
            device_id=(self.leaf, dst),
            device_id_type=MESH,
        )

    def slot(self, zz):
        return zz if self.xsend is None else zz * self.xs + self.x

    def up(self, zz, sem):
        return self.copy(self.slot(zz), (self.z + 1) * self.xs + self.x, self.zsend.at[sem])

    def down(self, zz, sem):
        return self.copy(self.slot(zz), (self.z - 1) * self.xs + self.x, self.zsend.at[sem])

    def across(self, zz):
        if self.xsend is None:
            return []
        return [
            self.copy(
                self.slot(zz),
                self.z * self.xs + (self.x + i) % self.xs,
                self.xsend.at[zz * (self.xs - 1) + i - 1],
            )
            for i in range(1, self.xs)
        ]

    def start(self):
        pl.when(self.z + 1 < self.zs)(lambda: self.up(self.z, self.z).start())
        pl.when(self.z > 0)(lambda: self.down(self.z, self.zs).start())
        for c in self.across(self.z):
            c.start()

    def wait_slot(self, slot):
        self.copy(slot, 0, self.zsend.at[0]).wait_recv()

    def relay(self, hop, use):
        below, above = self.z - hop, self.z + hop

        @pl.when(below >= 0)
        def _():
            self.wait_slot(self.slot(below))
            pl.when(self.z + 1 < self.zs)(lambda: self.up(below, below).start())
            for c in self.across(below):
                c.start()

        @pl.when(above < self.zs)
        def _():
            self.wait_slot(self.slot(above))
            pl.when(self.z > 0)(lambda: self.down(above, above).start())
            for c in self.across(above):
                c.start()

        if use is not None:
            pl.when(below >= 0)(lambda: use(self.slot(below)))
            pl.when(above < self.zs)(lambda: use(self.slot(above)))

    def partners(self, use):
        for i in range(1, self.xs):
            @pl.loop(0, self.zs)
            def _(zz):
                slot = zz * self.xs + (self.x + i) % self.xs
                self.wait_slot(slot)
                if use is not None:
                    use(slot)

    def finish(self):
        @pl.loop(0, self.zs)
        def _(zz):
            for c in self.across(zz):
                c.wait_send()
            pl.when((zz <= self.z) & (self.z + 1 < self.zs))(
                lambda: self.up(zz, zz).wait_send()
            )
            pl.when((zz > self.z) & (self.z > 0))(lambda: self.down(zz, zz).wait_send())
        pl.when(self.z > 0)(lambda: self.down(self.z, self.zs).wait_send())


def kernel(
    n, leaves, xs,
    src, b_hbm, bl_hbm, br_hbm, ci_hbm, co_hbm, shot_ref, cell_ref,
    sol_ref, grad_ref,
    b_ref, bl_ref, br_ref, ci_ref, co_ref, bt, col, buf, rg, zpart, zbuf, lg, cg,
    fwd_low, back_low, onehot, sols, zacc, u_ref, t_ref, sums, gpart, gbuf, lbuf,
    in_sem, col_sem, rz, rr, x_send, o_send, f_send, a_recv, z_send, z_recv,
    l_send, l_recv, cz, cx, cr, g_send, g_recv, h_send, h_recv,
):
    leaf, node = lax.axis_index("leaf"), lax.axis_index("node")
    zs = n // xs
    z_at, x_at = node // xs, node % xs
    k, block = bl_ref.shape
    shots = src.shape[0]
    total = n * shots

    pairs = (
        (b_hbm, b_ref), (bl_hbm, bl_ref), (br_hbm, br_ref), (ci_hbm, ci_ref), (co_hbm, co_ref),
    )
    loads = [pltpu.make_async_copy(a, v, in_sem.at[i]) for i, (a, v) in enumerate(pairs)]
    for c in loads:
        c.start()

    barrier = pltpu.get_barrier_semaphore()

    @pl.loop(1, n)
    def _(i):
        pl.semaphore_signal(
            barrier, inc=1, device_id=(leaf, (node + i) % n), device_id_type=MESH
        )

    @pl.loop(1, leaves)
    def _(i):
        pl.semaphore_signal(
            barrier, inc=1, device_id=((leaf + i) % leaves, node), device_id_type=MESH
        )

    def columns(j):
        return pl.ds(pl.multiple_of(j * block, block), block)

    def column_copy(zz):
        return pltpu.make_async_copy(
            src.at[:, columns(zz * xs + x_at)], col.at[zz], col_sem.at[zz]
        )

    for zz in range(zs):
        column_copy(zz).start()

    def send(a, slot, sem, dst):
        return pltpu.make_async_remote_copy(
            src_ref=a, dst_ref=buf.at[slot], send_sem=sem, recv_sem=a_recv.at[slot],
            device_id=(leaf, dst), device_id_type=MESH,
        )

    def arrived(slot):
        send(buf.at[slot], slot, f_send.at[0], node).wait_recv()

    def passing(x, zz):
        return jnp.where(zz == z_at, z_at * xs + x, n + x * zs + zz)

    def over_x(i, d):
        x, zz = (x_at + i) % xs, (z_at + d) % zs
        return send(
            src.at[:, columns(zz * xs + x)], passing(x_at, zz),
            x_send.at[(i - 1) * zs + d], z_at * xs + x,
        )

    def own_over_z(d):
        dst = ((z_at + d) % zs) * xs + x_at
        return send(src.at[:, columns(dst)], node, o_send.at[d], dst)

    def onward(i, d):
        x, zz = (x_at + i) % xs, (z_at + d) % zs
        slot = passing(x, zz)
        return send(buf.at[slot], z_at * xs + x, f_send.at[(i - 1) * zs + d], zz * xs + x_at)

    pl.semaphore_wait(barrier, n - 1 + leaves - 1)

    for i in range(1, xs):
        @pl.loop(1, zs + 1)
        def _(d):
            over_x(i, d % zs).start()

    if zs > 1:
        own_over_z(1).start()

    for c in loads:
        c.wait()
    b = b_ref[...]
    u = dot(ci_ref[...], b)
    u_ref[...] = u
    stacked = jnp.concatenate([co_ref[...], br_ref[...], half(u)], axis=0)
    t = dot_rows(stacked, b)
    t_ref[...] = t[:k]
    v = jnp.concatenate([bl_ref[...], half(t)], axis=0)
    rg[z_at, : 4 * k] = v
    rg[z_at, 4 * k :, : 4 * k] = half(dot_rows(ci_ref[...], v))
    rg[z_at, 4 * k :, 4 * k : 8 * k] = half(
        dot_rows(br_ref[...], jnp.concatenate([bl_ref[...], stacked], axis=0))
    )
    basis = Tree(rg, rz, None, rr, leaf, node, zs, xs)
    basis.start()

    for zz in range(zs):
        column_copy(zz).wait()
    zacc[...] = dot_rows(col[z_at], rg[z_at, : 4 * k])

    def project(zz):
        zacc[...] += dot_rows(col[zz], rg[zz, : 4 * k])

    for hop in range(1, zs):
        basis.relay(hop, project)
        if hop == max(zs - 2, 1):
            @pl.loop(2, zs)
            def _(d):
                own_over_z(d).start()

    late = max(zs // 2, 1)
    for i in range(1, xs):
        @pl.loop(1, zs)
        def _(d):
            arrived(passing((x_at + i) % xs, (z_at + d) % zs))
            pl.when(d < late)(lambda: onward(i, d).start())
        arrived(passing((x_at + i) % xs, z_at))

    s_part = rg[0, 4 * k :, :].astype(jnp.float32)
    for j in range(1, zs):
        s_part = s_part + rg[j, 4 * k :, :].astype(jnp.float32)

    def partial_copy(i, frm):
        return pltpu.make_async_remote_copy(
            src_ref=zpart.at[i - 1], dst_ref=zbuf.at[frm], send_sem=z_send.at[i],
            recv_sem=z_recv.at[frm], device_id=(leaf, z_at * xs + (x_at + i) % xs),
            device_id_type=MESH,
        )

    for i in range(1, xs):
        x = (x_at + i) % xs
        acc = jnp.zeros((shots, 4 * k), jnp.float32)
        for zz in range(zs):
            acc = acc + dot_rows(buf[passing(x, zz)], rg[zz, : 4 * k])
        zpart[i - 1, :shots] = half(acc)
        zpart[i - 1, shots : shots + k] = half(s_part[:, : 4 * k])
        zpart[i - 1, shots + k :] = half(s_part[:, 4 * k : 8 * k])
        partial_copy(i, x_at).start()

    rows_at = min(256, total)
    steps = total // rows_at

    def one_hot(first, last):
        @pl.loop(first, last)
        def _(r):
            at = pl.multiple_of(r * rows_at, rows_at)
            row = lax.broadcasted_iota(jnp.int32, (rows_at, total), 0) + at
            onehot[pl.ds(at, rows_at), :] = half(jnp.where(row == shot_ref[...], 1.0, 0.0))

    one_hot(0, steps // 2)
    z = zacc[...]
    left, right = s_part[:, : 4 * k], s_part[:, 4 * k : 8 * k]
    for i in range(1, xs):
        x = (x_at + i) % xs
        partial_copy(i, x).wait_recv()
        z = z + zbuf[x, :shots].astype(jnp.float32)
        left = left + zbuf[x, shots : shots + k].astype(jnp.float32)
        right = right + zbuf[x, shots + k :].astype(jnp.float32)

    s3t = half(left[:, :k])
    ss = half(right)
    f = left + dot(s3t, ss)
    proj = half(z[:, :k])
    zf = z + dot(proj, ss)
    carry, z2, z3 = zf[:, k : 2 * k], zf[:, 2 * k : 3 * k], zf[:, 3 * k :]
    fb = f[:, 2 * k : 3 * k]
    lift = z3 + dot_rows(half(z2), s3t)
    lift_map = f[:, 3 * k :] + dot_rows(half(fb), s3t)
    lg[leaf, :shots] = half(jnp.concatenate([carry, lift], axis=1))
    lg[leaf, shots:] = half(-jnp.concatenate([f[:, k : 2 * k], lift_map], axis=1))

    def leaf_copy(i, frm):
        return pltpu.make_async_remote_copy(
            src_ref=lg.at[leaf], dst_ref=lg.at[frm], send_sem=l_send.at[i],
            recv_sem=l_recv.at[frm], device_id=((leaf + i) % leaves, node),
            device_id_type=MESH,
        )

    for i in range(1, leaves):
        leaf_copy(i, leaf).start()

    fc = half(u_ref[...] + dot(s3t, br_ref[...]))
    s1 = half(right[:, k : 2 * k])
    bc = half(
        t_ref[...]
        + lax.dot_general(s1, bl_ref[...], (((0,), (0,)), ((), ())), preferred_element_type=jnp.float32)
    )
    fwd_low[...] = jnp.concatenate([br_ref[...], fc], axis=0)
    back_low[...] = jnp.concatenate([bl_ref[...], bc], axis=0)

    one_hot(steps // 2, steps)
    bt[...] = b_ref[...].T

    for i in range(1, leaves):
        leaf_copy(i, (leaf + i) % leaves).wait_recv()

    incoming = jnp.zeros((shots, k), jnp.float32)
    own_in = jnp.zeros((shots, k), jnp.float32)
    lifts = []
    for g in range(leaves):
        own_in = jnp.where(leaf == g, incoming, own_in)
        both = lg[g, :shots].astype(jnp.float32)
        if g > 0:
            both = both + dot(half(incoming), lg[g, shots:])
        incoming = both[:, :k]
        lifts.append(both[:, k:])
    returning = jnp.zeros((shots, k), jnp.float32)
    own_ret = jnp.zeros((shots, k), jnp.float32)
    for g in range(leaves - 1, -1, -1):
        own_ret = jnp.where(leaf == g, returning, own_ret)
        if g < leaves - 1:
            returning = lifts[g] + dot_rows(half(returning), lg[g, shots:, :k])
        else:
            returning = lifts[g]
    proj_fwd = z2 - dot(half(own_in), half(fb))
    cg[node] = half(
        jnp.concatenate([z[:, :k], -own_in, proj_fwd, -own_ret], axis=1)
    )

    coefs = Tree(cg, cz, cx, cr, leaf, node, zs, xs)
    coefs.start()
    for hop in range(1, zs):
        coefs.relay(hop, None)
        if hop == max(zs - 2, 1):
            for i in range(1, xs):
                @pl.loop(late, zs)
                def _(d):
                    onward(i, d).start()
    coefs.partners(None)

    sums[...] = jnp.zeros_like(sums)

    def shot_block(j, rhs):
        low = cg[j]
        fwd = half(dot(rhs, b_ref[...]) + dot(low[:, : 2 * k], fwd_low[...]))
        sol = half(dot(fwd, bt[...]) + dot(low[:, 2 * k :], back_low[...]))
        sols[pl.ds(pl.multiple_of(j * shots, shots), shots), :] = sol
        sums[...] += jnp.sum(
            sol.astype(jnp.float32) * fwd.astype(jnp.float32), axis=0, keepdims=True
        )

    shot_block(node, col[z_at])
    for i in range(1, xs):
        j = z_at * xs + (x_at + i) % xs
        shot_block(j, buf[j])
    for i in range(xs):
        @pl.loop(1, zs)
        def _(d):
            j = ((z_at + zs - d) % zs) * xs + (x_at + i) % xs
            arrived(j)
            shot_block(j, buf[j])

    corr = sums[...] / jnp.sqrt(jnp.float32(total))

    cell = cell_ref[...]
    slab = gpart.shape[1]
    high = lax.broadcasted_iota(jnp.int32, (n * slab, block), 0) == cell // LANES
    low_hit = lax.broadcasted_iota(jnp.int32, (LANES, block), 0) == cell % LANES
    placed = lax.dot_general(
        jnp.where(high, corr, 0.0),
        jnp.where(low_hit, 1.0, 0.0),
        (((1,), (1,)), ((), ())),
        preferred_element_type=jnp.float32,
        precision=lax.Precision.HIGHEST,
    )
    gpart[...] = placed.reshape(gpart.shape)

    def slab_copy(j, frm):
        return pltpu.make_async_remote_copy(
            src_ref=gpart.at[j], dst_ref=gbuf.at[frm], send_sem=g_send.at[j],
            recv_sem=g_recv.at[frm], device_id=(leaf, j), device_id_type=MESH,
        )

    @pl.loop(1, n)
    def _(i):
        slab_copy((node + i) % n, node).start()

    def permute(first, last):
        @pl.loop(first, last)
        def _(r):
            rows = pl.ds(pl.multiple_of(r * rows_at, rows_at), rows_at)
            sol_ref[rows, :] = half(dot(onehot[rows, :], sols[...]))

    permute(0, steps // 2)

    own = gpart[node]

    def add_slab(i, acc):
        j = (node + n - i) % n
        slab_copy(j, j).wait_recv()
        return acc + gbuf[j]

    own = lax.fori_loop(1, n, add_slab, own)
    lbuf[leaf] = own

    def grad_copy(i, frm):
        return pltpu.make_async_remote_copy(
            src_ref=lbuf.at[leaf], dst_ref=lbuf.at[frm], send_sem=h_send.at[i],
            recv_sem=h_recv.at[frm], device_id=((leaf + i) % leaves, node),
            device_id_type=MESH,
        )

    for i in range(1, leaves):
        grad_copy(i, leaf).start()
    permute(steps // 2, steps)
    for i in range(1, leaves):
        grad_copy(i, (leaf + leaves - i) % leaves).wait_recv()
    acc = lbuf[0]
    for g in range(1, leaves):
        acc = acc + lbuf[g]
    grad_ref[...] = acc


    basis.finish()
    coefs.finish()
    for i in range(1, leaves):
        leaf_copy(i, leaf).wait_send()
        grad_copy(i, leaf).wait_send()
    for i in range(1, xs):
        partial_copy(i, x_at).wait_send()

        @pl.loop(0, zs)
        def _(d):
            over_x(i, d).wait_send()
            pl.when(d > 0)(lambda: onward(i, d).wait_send())

    @pl.loop(1, zs)
    def _(d):
        own_over_z(d).wait_send()

    @pl.loop(1, n)
    def _(i):
        slab_copy((node + i) % n, node).wait_send()


def per_device(n, leaves, sources, block_inverse, basis_left, basis_right, couple_in, couple_out, column_of_shot, cell_map):
    xs = max(d for d in range(1, n + 1) if n % d == 0 and (2 * d * d <= n or d == 1))
    zs = n // xs
    k, block = basis_left.shape
    shots = sources.shape[0]
    total = n * shots
    slab = CELL_DEV // LANES
    bf16, f32 = jnp.bfloat16, jnp.float32
    dma = pltpu.SemaphoreType.DMA
    anywhere = pl.BlockSpec(memory_space=pl.ANY)
    vmem = pl.BlockSpec(memory_space=pltpu.VMEM)
    vectors = max(zs * (xs - 1), 1)
    small = pltpu.VMEM((k, block), bf16)
    solution_out, grad = pl.pallas_call(
        functools.partial(kernel, n, leaves, xs),
        out_shape=(
            jax.ShapeDtypeStruct((total, block), bf16),
            jax.ShapeDtypeStruct((slab, LANES), f32),
        ),
        in_specs=[anywhere] * 6 + [vmem] * 2,
        out_specs=(vmem, vmem),
        scratch_shapes=[
            pltpu.VMEM((block, block), bf16), small, small, small, small,
            pltpu.VMEM((block, block), bf16),
            pltpu.VMEM((zs, shots, block), bf16),
            pltpu.VMEM((2 * n, shots, block), bf16),
            pltpu.VMEM((zs, 5 * k, block), bf16),
            pltpu.VMEM((max(xs - 1, 1), shots + 2 * k, 4 * k), bf16),
            pltpu.VMEM((xs, shots + 2 * k, 4 * k), bf16),
            pltpu.VMEM((leaves, shots + k, 2 * k), bf16),
            pltpu.VMEM((n, shots, 4 * k), bf16),
            pltpu.VMEM((2 * k, block), bf16),
            pltpu.VMEM((2 * k, block), bf16),
            pltpu.VMEM((total, total), bf16),
            pltpu.VMEM((total, block), bf16),
            pltpu.VMEM((shots, 4 * k), f32),
            pltpu.VMEM((k, block), f32),
            pltpu.VMEM((k, block), f32),
            pltpu.VMEM((1, block), f32),
            pltpu.VMEM((n, slab, LANES), f32),
            pltpu.VMEM((n, slab, LANES), f32),
            pltpu.VMEM((leaves, slab, LANES), f32),
            dma((5,)), dma((zs,)),
            dma((zs + 1,)), dma((zs,)),
            dma((vectors,)), dma((zs,)), dma((vectors,)), dma((2 * n,)),
            dma((xs,)), dma((xs,)),
            dma((leaves,)), dma((leaves,)),
            dma((zs + 1,)), dma((vectors,)), dma((n,)),
            dma((n,)), dma((n,)),
            dma((leaves,)), dma((leaves,)),
        ],
        compiler_params=pltpu.CompilerParams(
            collective_id=0, has_side_effects=True, vmem_limit_bytes=56 * 1024 * 1024
        ),
    )(
        sources, block_inverse, basis_left, basis_right, couple_in, couple_out,
        column_of_shot.reshape(1, -1), cell_map.reshape(1, -1),
    )
    return solution_out, grad.reshape(-1)


def solution(mesh):
    both = P(None, ("leaf", "node"))
    return jax.shard_map(
        functools.partial(per_device, mesh.shape["node"], mesh.shape["leaf"]),
        mesh=mesh,
        in_specs=(P("node", "leaf"), both, both, both, both, both, P(), P(("leaf", "node"))),
        out_specs=(both, P("node")),
        check_vma=False,
    )
```

```python
import functools

import jax
import jax.numpy as jnp
from jax import lax
from jax.experimental import pallas as pl
from jax.experimental.pallas import tpu as pltpu
from jax.sharding import PartitionSpec as P

CELL_DEV = 2048
LANES = 128
MESH = pl.DeviceIdType.MESH


def dot_rows(a, b):
    return lax.dot_general(a, b, (((1,), (1,)), ((), ())), preferred_element_type=jnp.float32)


def dot(a, b):
    return jnp.dot(a, b, preferred_element_type=jnp.float32)


def half(x):
    return x.astype(jnp.bfloat16)


class Tree:
    def __init__(self, buf, part, parts, zsend, xsend, recv, leaf, node, zs, xs):
        step = buf.shape[1] // parts
        self.rows = pl.ds(part * step, step)
        zsend, recv = zsend.at[part], recv.at[part]
        xsend = None if xsend is None else xsend.at[part]
        self.buf, self.zsend, self.xsend, self.recv = buf, zsend, xsend, recv
        self.leaf, self.zs, self.xs = leaf, zs, xs
        self.z, self.x = node // xs, node % xs

    def copy(self, slot, dst, sem):
        return pltpu.make_async_remote_copy(
            src_ref=self.buf.at[slot, self.rows],
            dst_ref=self.buf.at[slot, self.rows],
            send_sem=sem,
            recv_sem=self.recv.at[slot],
            device_id=(self.leaf, dst),
            device_id_type=MESH,
        )

    def slot(self, zz):
        return zz if self.xsend is None else zz * self.xs + self.x

    def up(self, zz, sem):
        return self.copy(self.slot(zz), (self.z + 1) * self.xs + self.x, self.zsend.at[sem])

    def down(self, zz, sem):
        return self.copy(self.slot(zz), (self.z - 1) * self.xs + self.x, self.zsend.at[sem])

    def across(self, zz):
        if self.xsend is None:
            return []
        return [
            self.copy(
                self.slot(zz),
                self.z * self.xs + (self.x + i) % self.xs,
                self.xsend.at[zz * (self.xs - 1) + i - 1],
            )
            for i in range(1, self.xs)
        ]

    def start(self):
        pl.when(self.z + 1 < self.zs)(lambda: self.up(self.z, self.z).start())
        pl.when(self.z > 0)(lambda: self.down(self.z, self.zs).start())
        for c in self.across(self.z):
            c.start()

    def wait_slot(self, slot):
        self.copy(slot, 0, self.zsend.at[0]).wait_recv()

    def relay(self, hop):
        below, above = self.z - hop, self.z + hop

        @pl.when(below >= 0)
        def _():
            self.wait_slot(self.slot(below))
            pl.when(self.z + 1 < self.zs)(lambda: self.up(below, below).start())
            for c in self.across(below):
                c.start()

        @pl.when(above < self.zs)
        def _():
            self.wait_slot(self.slot(above))
            pl.when(self.z > 0)(lambda: self.down(above, above).start())
            for c in self.across(above):
                c.start()

    def partners(self):
        for i in range(1, self.xs):
            @pl.loop(0, self.zs)
            def _(zz):
                slot = zz * self.xs + (self.x + i) % self.xs
                self.wait_slot(slot)

    def finish(self):
        @pl.loop(0, self.zs)
        def _(zz):
            for c in self.across(zz):
                c.wait_send()
            pl.when((zz <= self.z) & (self.z + 1 < self.zs))(
                lambda: self.up(zz, zz).wait_send()
            )
            pl.when((zz > self.z) & (self.z > 0))(lambda: self.down(zz, zz).wait_send())
        pl.when(self.z > 0)(lambda: self.down(self.z, self.zs).wait_send())


def kernel(
    n, leaves, xs,
    src, b_hbm, bl_hbm, br_hbm, ci_hbm, co_hbm, shot_ref, cell_ref,
    sol_ref, grad_ref,
    b_ref, bl_ref, br_ref, ci_ref, co_ref, bt, col, buf, rg, zpart, zbuf, lg, cg,
    fwd_low, back_low, onehot, sols, zacc, u_ref, t_ref, sums, gpart, gbuf, lbuf,
    in_sem, col_sem, rz, rr, x_send, o_send, f_send, a_recv, z_send, z_recv,
    l_send, l_recv, cz, cx, cr, g_send, g_recv, h_send, h_recv,
):
    leaf, node = lax.axis_index("leaf"), lax.axis_index("node")
    zs = n // xs
    z_at, x_at = node // xs, node % xs
    k, block = bl_ref.shape
    shots = src.shape[0]
    total = n * shots

    pairs = (
        (b_hbm, b_ref), (bl_hbm, bl_ref), (br_hbm, br_ref), (ci_hbm, ci_ref), (co_hbm, co_ref),
    )
    loads = [pltpu.make_async_copy(a, v, in_sem.at[i]) for i, (a, v) in enumerate(pairs)]
    for c in loads:
        c.start()

    barrier = pltpu.get_barrier_semaphore()

    @pl.loop(1, n)
    def _(i):
        pl.semaphore_signal(
            barrier, inc=1, device_id=(leaf, (node + i) % n), device_id_type=MESH
        )

    @pl.loop(1, leaves)
    def _(i):
        pl.semaphore_signal(
            barrier, inc=1, device_id=((leaf + i) % leaves, node), device_id_type=MESH
        )

    def columns(j):
        return pl.ds(pl.multiple_of(j * block, block), block)

    def column_copy(zz):
        return pltpu.make_async_copy(
            src.at[:, columns(zz * xs + x_at)], col.at[zz], col_sem.at[zz]
        )

    for zz in range(zs):
        column_copy(zz).start()

    def send(a, slot, sem, dst):
        return pltpu.make_async_remote_copy(
            src_ref=a, dst_ref=buf.at[slot], send_sem=sem, recv_sem=a_recv.at[slot],
            device_id=(leaf, dst), device_id_type=MESH,
        )

    def arrived(slot):
        send(buf.at[slot], slot, f_send.at[0], node).wait_recv()

    def passing(x, zz):
        return jnp.where(zz == z_at, z_at * xs + x, n + x * zs + zz)

    def over_x(i, d):
        x, zz = (x_at + i) % xs, (z_at + d) % zs
        return send(
            src.at[:, columns(zz * xs + x)], passing(x_at, zz),
            x_send.at[(i - 1) * zs + d], z_at * xs + x,
        )

    def own_over_z(d):
        dst = ((z_at + d) % zs) * xs + x_at
        return send(col.at[(z_at + d) % zs], node, o_send.at[d], dst)

    def onward(i, d):
        x, zz = (x_at + i) % xs, (z_at + d) % zs
        slot = passing(x, zz)
        return send(buf.at[slot], z_at * xs + x, f_send.at[(i - 1) * zs + d], zz * xs + x_at)

    for c in loads:
        c.wait()
    b = b_ref[...]
    u = dot(ci_ref[...], b)
    u_ref[...] = u
    stacked = jnp.concatenate([co_ref[...], br_ref[...], half(u)], axis=0)
    t = dot_rows(stacked, b)
    t_ref[...] = t[:k]
    v = jnp.concatenate([bl_ref[...], half(t)], axis=0)
    rg[z_at, : 4 * k] = v
    rg[z_at, 4 * k :, : 4 * k] = half(dot_rows(ci_ref[...], v))
    rg[z_at, 4 * k :, 4 * k : 8 * k] = half(
        dot_rows(br_ref[...], jnp.concatenate([bl_ref[...], stacked], axis=0))
    )
    pl.semaphore_wait(barrier, n - 1 + leaves - 1)

    parts = 2
    basis = [Tree(rg, p, parts, rz, None, rr, leaf, node, zs, xs) for p in range(parts)]
    for part in basis:
        part.start()

    for i in range(1, xs):
        @pl.loop(1, zs + 1)
        def _(d):
            over_x(i, d % zs).start()

    for zz in range(zs):
        column_copy(zz).wait()
    if zs > 1:
        own_over_z(1).start()

    zacc[...] = dot_rows(col[z_at], rg[z_at, : 4 * k])

    def project(zz):
        zacc[...] += dot_rows(col[zz], rg[zz, : 4 * k])

    for hop in range(1, zs):
        for part in basis:
            part.relay(hop)
        pl.when(z_at >= hop)(lambda: project(z_at - hop))
        pl.when(z_at + hop < zs)(lambda: project(z_at + hop))
        if hop == max(zs - 2, 1):
            @pl.loop(2, zs)
            def _(d):
                own_over_z(d).start()

    early, late = 1 + (zs - 1) // 3, 1 + 2 * (zs - 1) // 3
    for i in range(1, xs):
        @pl.loop(1, zs)
        def _(d):
            arrived(passing((x_at + i) % xs, (z_at + d) % zs))
            pl.when(d < early)(lambda: onward(i, d).start())
        arrived(passing((x_at + i) % xs, z_at))

    s_part = rg[0, 4 * k :, :].astype(jnp.float32)
    for j in range(1, zs):
        s_part = s_part + rg[j, 4 * k :, :].astype(jnp.float32)

    def partial_copy(i, frm):
        return pltpu.make_async_remote_copy(
            src_ref=zpart.at[i - 1], dst_ref=zbuf.at[frm], send_sem=z_send.at[i],
            recv_sem=z_recv.at[frm], device_id=(leaf, z_at * xs + (x_at + i) % xs),
            device_id_type=MESH,
        )

    for i in range(1, xs):
        x = (x_at + i) % xs
        acc = jnp.zeros((shots, 4 * k), jnp.float32)
        for zz in range(zs):
            acc = acc + dot_rows(buf[passing(x, zz)], rg[zz, : 4 * k])
        zpart[i - 1, :shots] = half(acc)
        zpart[i - 1, shots : shots + k] = half(s_part[:, : 4 * k])
        zpart[i - 1, shots + k :] = half(s_part[:, 4 * k : 8 * k])
        partial_copy(i, x_at).start()

    rows_at = min(256, total)
    steps = total // rows_at

    def one_hot(first, last):
        @pl.loop(first, last)
        def _(r):
            at = pl.multiple_of(r * rows_at, rows_at)
            row = lax.broadcasted_iota(jnp.int32, (rows_at, total), 0) + at
            onehot[pl.ds(at, rows_at), :] = half(jnp.where(row == shot_ref[...], 1.0, 0.0))

    one_hot(0, steps // 2)
    z = zacc[...]
    left, right = s_part[:, : 4 * k], s_part[:, 4 * k : 8 * k]
    for i in range(1, xs):
        x = (x_at + i) % xs
        partial_copy(i, x).wait_recv()
        z = z + zbuf[x, :shots].astype(jnp.float32)
        left = left + zbuf[x, shots : shots + k].astype(jnp.float32)
        right = right + zbuf[x, shots + k :].astype(jnp.float32)

    s3t = half(left[:, :k])
    ss = half(right)
    f = left + dot(s3t, ss)
    proj = half(z[:, :k])
    zf = z + dot(proj, ss)
    carry, z2, z3 = zf[:, k : 2 * k], zf[:, 2 * k : 3 * k], zf[:, 3 * k :]
    fb = f[:, 2 * k : 3 * k]
    lift = z3 + dot_rows(half(z2), s3t)
    lift_map = f[:, 3 * k :] + dot_rows(half(fb), s3t)
    lg[leaf, :shots] = half(jnp.concatenate([carry, lift], axis=1))
    lg[leaf, shots:] = half(-jnp.concatenate([f[:, k : 2 * k], lift_map], axis=1))

    def leaf_copy(i, frm):
        return pltpu.make_async_remote_copy(
            src_ref=lg.at[leaf], dst_ref=lg.at[frm], send_sem=l_send.at[i],
            recv_sem=l_recv.at[frm], device_id=((leaf + i) % leaves, node),
            device_id_type=MESH,
        )

    for i in range(1, leaves):
        leaf_copy(i, leaf).start()
    for i in range(1, xs):
        @pl.loop(early, late)
        def _(d):
            onward(i, d).start()

    fc = half(u_ref[...] + dot(s3t, br_ref[...]))
    s1 = half(right[:, k : 2 * k])
    bc = half(
        t_ref[...]
        + lax.dot_general(s1, bl_ref[...], (((0,), (0,)), ((), ())), preferred_element_type=jnp.float32)
    )
    fwd_low[...] = jnp.concatenate([br_ref[...], fc], axis=0)
    back_low[...] = jnp.concatenate([bl_ref[...], bc], axis=0)

    one_hot(steps // 2, steps)
    bt[...] = b_ref[...].T

    for i in range(1, leaves):
        leaf_copy(i, (leaf + i) % leaves).wait_recv()

    incoming = jnp.zeros((shots, k), jnp.float32)
    own_in = jnp.zeros((shots, k), jnp.float32)
    lifts = []
    for g in range(leaves):
        own_in = jnp.where(leaf == g, incoming, own_in)
        both = lg[g, :shots].astype(jnp.float32)
        if g > 0:
            both = both + dot(half(incoming), lg[g, shots:])
        incoming = both[:, :k]
        lifts.append(both[:, k:])
    returning = jnp.zeros((shots, k), jnp.float32)
    own_ret = jnp.zeros((shots, k), jnp.float32)
    for g in range(leaves - 1, -1, -1):
        own_ret = jnp.where(leaf == g, returning, own_ret)
        if g < leaves - 1:
            returning = lifts[g] + dot_rows(half(returning), lg[g, shots:, :k])
        else:
            returning = lifts[g]
    proj_fwd = z2 - dot(half(own_in), half(fb))
    cg[node] = half(
        jnp.concatenate([z[:, :k], -own_in, proj_fwd, -own_ret], axis=1)
    )

    coefs = [Tree(cg, p, parts, cz, cx, cr, leaf, node, zs, xs) for p in range(parts)]
    for part in coefs:
        part.start()
    for hop in range(1, zs):
        for part in coefs:
            part.relay(hop)
        if hop == max(zs - 2, 1):
            for i in range(1, xs):
                @pl.loop(late, zs)
                def _(d):
                    onward(i, d).start()
    for part in coefs:
        part.partners()

    sums[...] = jnp.zeros_like(sums)

    def shot_block(j, rhs):
        low = cg[j]
        fwd = half(dot(rhs, b_ref[...]) + dot(low[:, : 2 * k], fwd_low[...]))
        sol = half(dot(fwd, bt[...]) + dot(low[:, 2 * k :], back_low[...]))
        sols[pl.ds(pl.multiple_of(j * shots, shots), shots), :] = sol
        sums[...] += jnp.sum(
            sol.astype(jnp.float32) * fwd.astype(jnp.float32), axis=0, keepdims=True
        )

    shot_block(node, col[z_at])
    for i in range(1, xs):
        j = z_at * xs + (x_at + i) % xs
        shot_block(j, buf[j])
    for i in range(xs):
        @pl.loop(1, zs)
        def _(d):
            j = ((z_at + zs - d) % zs) * xs + (x_at + i) % xs
            arrived(j)
            shot_block(j, buf[j])

    corr = sums[...] / jnp.sqrt(jnp.float32(total))

    cell = cell_ref[...]
    slab = gpart.shape[1]
    high = lax.broadcasted_iota(jnp.int32, (n * slab, block), 0) == cell // LANES
    low_hit = lax.broadcasted_iota(jnp.int32, (LANES, block), 0) == cell % LANES
    placed = lax.dot_general(
        jnp.where(high, corr, 0.0),
        jnp.where(low_hit, 1.0, 0.0),
        (((1,), (1,)), ((), ())),
        preferred_element_type=jnp.float32,
        precision=lax.Precision.HIGHEST,
    )
    gpart[...] = placed.reshape(gpart.shape)

    def slab_copy(j, frm):
        return pltpu.make_async_remote_copy(
            src_ref=gpart.at[j], dst_ref=gbuf.at[frm], send_sem=g_send.at[j],
            recv_sem=g_recv.at[frm], device_id=(leaf, j), device_id_type=MESH,
        )

    @pl.loop(1, n)
    def _(i):
        slab_copy((node + i) % n, node).start()

    def permute(first, last):
        @pl.loop(first, last)
        def _(r):
            rows = pl.ds(pl.multiple_of(r * rows_at, rows_at), rows_at)
            sol_ref[rows, :] = half(dot(onehot[rows, :], sols[...]))

    permute(0, steps // 2)

    own = gpart[node]

    def add_slab(i, acc):
        j = (node + n - i) % n
        slab_copy(j, j).wait_recv()
        return acc + gbuf[j]

    own = lax.fori_loop(1, n, add_slab, own)
    lbuf[leaf] = own

    def grad_copy(i, frm):
        return pltpu.make_async_remote_copy(
            src_ref=lbuf.at[leaf], dst_ref=lbuf.at[frm], send_sem=h_send.at[i],
            recv_sem=h_recv.at[frm], device_id=((leaf + i) % leaves, node),
            device_id_type=MESH,
        )

    for i in range(1, leaves):
        grad_copy(i, leaf).start()
    permute(steps // 2, steps)
    for i in range(1, leaves):
        grad_copy(i, (leaf + leaves - i) % leaves).wait_recv()
    acc = lbuf[0]
    for g in range(1, leaves):
        acc = acc + lbuf[g]
    grad_ref[...] = acc


    for part in basis + coefs:
        part.finish()
    for i in range(1, leaves):
        leaf_copy(i, leaf).wait_send()
        grad_copy(i, leaf).wait_send()
    for i in range(1, xs):
        partial_copy(i, x_at).wait_send()

        @pl.loop(0, zs)
        def _(d):
            over_x(i, d).wait_send()
            pl.when(d > 0)(lambda: onward(i, d).wait_send())

    @pl.loop(1, zs)
    def _(d):
        own_over_z(d).wait_send()

    @pl.loop(1, n)
    def _(i):
        slab_copy((node + i) % n, node).wait_send()


def per_device(n, leaves, sources, block_inverse, basis_left, basis_right, couple_in, couple_out, column_of_shot, cell_map):
    xs = max(d for d in range(1, n + 1) if n % d == 0 and (2 * d * d <= n or d == 1))
    zs = n // xs
    k, block = basis_left.shape
    shots = sources.shape[0]
    total = n * shots
    slab = CELL_DEV // LANES
    bf16, f32 = jnp.bfloat16, jnp.float32
    dma = pltpu.SemaphoreType.DMA
    anywhere = pl.BlockSpec(memory_space=pl.ANY)
    vmem = pl.BlockSpec(memory_space=pltpu.VMEM)
    vectors = max(zs * (xs - 1), 1)
    small = pltpu.VMEM((k, block), bf16)
    solution_out, grad = pl.pallas_call(
        functools.partial(kernel, n, leaves, xs),
        out_shape=(
            jax.ShapeDtypeStruct((total, block), bf16),
            jax.ShapeDtypeStruct((slab, LANES), f32),
        ),
        in_specs=[anywhere] * 6 + [vmem] * 2,
        out_specs=(vmem, vmem),
        scratch_shapes=[
            pltpu.VMEM((block, block), bf16), small, small, small, small,
            pltpu.VMEM((block, block), bf16),
            pltpu.VMEM((zs, shots, block), bf16),
            pltpu.VMEM((2 * n, shots, block), bf16),
            pltpu.VMEM((zs, 5 * k, block), bf16),
            pltpu.VMEM((max(xs - 1, 1), shots + 2 * k, 4 * k), bf16),
            pltpu.VMEM((xs, shots + 2 * k, 4 * k), bf16),
            pltpu.VMEM((leaves, shots + k, 2 * k), bf16),
            pltpu.VMEM((n, shots, 4 * k), bf16),
            pltpu.VMEM((2 * k, block), bf16),
            pltpu.VMEM((2 * k, block), bf16),
            pltpu.VMEM((total, total), bf16),
            pltpu.VMEM((total, block), bf16),
            pltpu.VMEM((shots, 4 * k), f32),
            pltpu.VMEM((k, block), f32),
            pltpu.VMEM((k, block), f32),
            pltpu.VMEM((1, block), f32),
            pltpu.VMEM((n, slab, LANES), f32),
            pltpu.VMEM((n, slab, LANES), f32),
            pltpu.VMEM((leaves, slab, LANES), f32),
            dma((5,)), dma((zs,)),
            dma((2, zs + 1)), dma((2, zs)),
            dma((vectors,)), dma((zs,)), dma((vectors,)), dma((2 * n,)),
            dma((xs,)), dma((xs,)),
            dma((leaves,)), dma((leaves,)),
            dma((2, zs + 1)), dma((2, vectors)), dma((2, n)),
            dma((n,)), dma((n,)),
            dma((leaves,)), dma((leaves,)),
        ],
        compiler_params=pltpu.CompilerParams(
            collective_id=0, has_side_effects=True, vmem_limit_bytes=56 * 1024 * 1024
        ),
    )(
        sources, block_inverse, basis_left, basis_right, couple_in, couple_out,
        column_of_shot.reshape(1, -1), cell_map.reshape(1, -1),
    )
    return solution_out, grad.reshape(-1)


def solution(mesh):
    both = P(None, ("leaf", "node"))
    return jax.shard_map(
        functools.partial(per_device, mesh.shape["node"], mesh.shape["leaf"]),
        mesh=mesh,
        in_specs=(P("node", "leaf"), both, both, both, both, both, P(), P(("leaf", "node"))),
        out_specs=(both, P("node")),
        check_vma=False,
    )
```

```python
import functools

import jax
import jax.numpy as jnp
from jax import lax
from jax.experimental import pallas as pl
from jax.experimental.pallas import tpu as pltpu
from jax.sharding import PartitionSpec as P

CELL_DEV = 2048
LANES = 128
MESH = pl.DeviceIdType.MESH


def dot_rows(a, b):
    return lax.dot_general(a, b, (((1,), (1,)), ((), ())), preferred_element_type=jnp.float32)


def dot(a, b):
    return jnp.dot(a, b, preferred_element_type=jnp.float32)


def half(x):
    return x.astype(jnp.bfloat16)


class Tree:
    def __init__(self, buf, part, parts, zsend, xsend, recv, leaf, node, zs, xs):
        step = buf.shape[1] // parts
        self.rows = pl.ds(part * step, step)
        zsend, recv = zsend.at[part], recv.at[part]
        xsend = None if xsend is None else xsend.at[part]
        self.buf, self.zsend, self.xsend, self.recv = buf, zsend, xsend, recv
        self.leaf, self.zs, self.xs = leaf, zs, xs
        self.z, self.x = node // xs, node % xs

    def copy(self, slot, dst, sem):
        return pltpu.make_async_remote_copy(
            src_ref=self.buf.at[slot, self.rows],
            dst_ref=self.buf.at[slot, self.rows],
            send_sem=sem,
            recv_sem=self.recv.at[slot],
            device_id=(self.leaf, dst),
            device_id_type=MESH,
        )

    def slot(self, zz):
        return zz if self.xsend is None else zz * self.xs + self.x

    def up(self, zz, sem):
        return self.copy(self.slot(zz), (self.z + 1) * self.xs + self.x, self.zsend.at[sem])

    def down(self, zz, sem):
        return self.copy(self.slot(zz), (self.z - 1) * self.xs + self.x, self.zsend.at[sem])

    def across(self, zz):
        if self.xsend is None:
            return []
        return [
            self.copy(
                self.slot(zz),
                self.z * self.xs + (self.x + i) % self.xs,
                self.xsend.at[zz * (self.xs - 1) + i - 1],
            )
            for i in range(1, self.xs)
        ]

    def start(self):
        pl.when(self.z + 1 < self.zs)(lambda: self.up(self.z, self.z).start())
        pl.when(self.z > 0)(lambda: self.down(self.z, self.zs).start())
        for c in self.across(self.z):
            c.start()

    def wait_slot(self, slot):
        self.copy(slot, 0, self.zsend.at[0]).wait_recv()

    def relay(self, hop):
        below, above = self.z - hop, self.z + hop

        @pl.when(below >= 0)
        def _():
            self.wait_slot(self.slot(below))
            pl.when(self.z + 1 < self.zs)(lambda: self.up(below, below).start())
            for c in self.across(below):
                c.start()

        @pl.when(above < self.zs)
        def _():
            self.wait_slot(self.slot(above))
            pl.when(self.z > 0)(lambda: self.down(above, above).start())
            for c in self.across(above):
                c.start()

    def partners(self):
        for i in range(1, self.xs):
            @pl.loop(0, self.zs)
            def _(zz):
                slot = zz * self.xs + (self.x + i) % self.xs
                self.wait_slot(slot)

    def finish(self):
        @pl.loop(0, self.zs)
        def _(zz):
            for c in self.across(zz):
                c.wait_send()
            pl.when((zz <= self.z) & (self.z + 1 < self.zs))(
                lambda: self.up(zz, zz).wait_send()
            )
            pl.when((zz > self.z) & (self.z > 0))(lambda: self.down(zz, zz).wait_send())
        pl.when(self.z > 0)(lambda: self.down(self.z, self.zs).wait_send())


def kernel(
    n, leaves, xs,
    src, b_hbm, bl_hbm, br_hbm, ci_hbm, co_hbm, shot_ref, cell_ref,
    sol_ref, grad_ref,
    b_ref, bl_ref, br_ref, ci_ref, co_ref, bt, col, buf, rg, zpart, zbuf, lg, cg,
    fwd_low, back_low, onehot, sols, zacc, u_ref, t_ref, sums, gpart, gbuf, lbuf,
    in_sem, col_sem, rz, rr, x_send, o_send, f_send, a_recv, z_send, z_recv,
    l_send, l_recv, cz, cx, cr, g_send, g_recv, h_send, h_recv,
):
    leaf, node = lax.axis_index("leaf"), lax.axis_index("node")
    zs = n // xs
    z_at, x_at = node // xs, node % xs
    k, block = bl_ref.shape
    shots = src.shape[0]
    total = n * shots

    pairs = (
        (b_hbm, b_ref), (bl_hbm, bl_ref), (br_hbm, br_ref), (ci_hbm, ci_ref), (co_hbm, co_ref),
    )
    loads = [pltpu.make_async_copy(a, v, in_sem.at[i]) for i, (a, v) in enumerate(pairs)]
    for c in loads:
        c.start()

    barrier = pltpu.get_barrier_semaphore()

    @pl.loop(1, n)
    def _(i):
        pl.semaphore_signal(
            barrier, inc=1, device_id=(leaf, (node + i) % n), device_id_type=MESH
        )

    @pl.loop(1, leaves)
    def _(i):
        pl.semaphore_signal(
            barrier, inc=1, device_id=((leaf + i) % leaves, node), device_id_type=MESH
        )

    def columns(j):
        return pl.ds(pl.multiple_of(j * block, block), block)

    def column_copy(zz):
        return pltpu.make_async_copy(
            src.at[:, columns(zz * xs + x_at)], col.at[zz], col_sem.at[zz]
        )

    for zz in range(zs):
        column_copy(zz).start()

    def send(a, slot, sem, dst):
        return pltpu.make_async_remote_copy(
            src_ref=a, dst_ref=buf.at[slot], send_sem=sem, recv_sem=a_recv.at[slot],
            device_id=(leaf, dst), device_id_type=MESH,
        )

    def arrived(slot):
        send(buf.at[slot], slot, f_send.at[0], node).wait_recv()

    def passing(x, zz):
        return jnp.where(zz == z_at, z_at * xs + x, n + x * zs + zz)

    def over_x(i, d):
        x, zz = (x_at + i) % xs, (z_at + d) % zs
        return send(
            src.at[:, columns(zz * xs + x)], passing(x_at, zz),
            x_send.at[(i - 1) * zs + d], z_at * xs + x,
        )

    def own_over_z(d):
        dst = ((z_at + d) % zs) * xs + x_at
        return send(col.at[(z_at + d) % zs], node, o_send.at[d], dst)

    def onward(i, d):
        x, zz = (x_at + i) % xs, (z_at + d) % zs
        slot = passing(x, zz)
        return send(buf.at[slot], z_at * xs + x, f_send.at[(i - 1) * zs + d], zz * xs + x_at)

    for c in loads:
        c.wait()
    b = b_ref[...]
    u = dot(ci_ref[...], b)
    u_ref[...] = u
    stacked = jnp.concatenate([co_ref[...], br_ref[...], half(u)], axis=0)
    t = dot_rows(stacked, b)
    t_ref[...] = t[:k]
    v = jnp.concatenate([bl_ref[...], half(t)], axis=0)
    rg[z_at, : 4 * k] = v
    rg[z_at, 4 * k :, : 4 * k] = half(dot_rows(ci_ref[...], v))
    rg[z_at, 4 * k :, 4 * k : 8 * k] = half(
        dot_rows(br_ref[...], jnp.concatenate([bl_ref[...], stacked], axis=0))
    )
    pl.semaphore_wait(barrier, n - 1 + leaves - 1)

    parts = rz.shape[0]
    basis = [Tree(rg, p, parts, rz, None, rr, leaf, node, zs, xs) for p in range(parts)]
    for part in basis:
        part.start()

    for i in range(1, xs):
        @pl.loop(1, zs + 1)
        def _(d):
            over_x(i, d % zs).start()

    for zz in range(zs):
        column_copy(zz).wait()
    if zs > 1:
        own_over_z(1).start()

    rows_at = min(256, total)
    steps = total // rows_at

    def one_hot(first, last):
        @pl.loop(first, last)
        def _(r):
            at = pl.multiple_of(r * rows_at, rows_at)
            row = lax.broadcasted_iota(jnp.int32, (rows_at, total), 0) + at
            onehot[pl.ds(at, rows_at), :] = half(jnp.where(row == shot_ref[...], 1.0, 0.0))

    one_hot(0, steps // 2)
    bt[...] = b.T

    for hop in range(1, zs):
        for part in basis:
            part.relay(hop)
        if hop == max(zs - 2, 1):
            @pl.loop(2, zs)
            def _(d):
                own_over_z(d).start()

    early, late = 1 + (zs - 1) // 3, 1 + 2 * (zs - 1) // 3
    for i in range(1, xs):
        @pl.loop(1, zs)
        def _(d):
            arrived(passing((x_at + i) % xs, (z_at + d) % zs))
            pl.when(d < early)(lambda: onward(i, d).start())
        arrived(passing((x_at + i) % xs, z_at))

    s_part = rg[0, 4 * k :, :].astype(jnp.float32)
    for j in range(1, zs):
        s_part = s_part + rg[j, 4 * k :, :].astype(jnp.float32)

    def partial_copy(i, frm, rows, sem):
        return pltpu.make_async_remote_copy(
            src_ref=zpart.at[i - 1, rows], dst_ref=zbuf.at[frm, rows],
            send_sem=z_send.at[sem, i], recv_sem=z_recv.at[sem, frm],
            device_id=(leaf, z_at * xs + (x_at + i) % xs), device_id_type=MESH,
        )

    grams, projections = pl.ds(shots, 2 * k), pl.ds(0, shots)
    for i in range(1, xs):
        zpart[i - 1, shots : shots + k] = half(s_part[:, : 4 * k])
        zpart[i - 1, shots + k :] = half(s_part[:, 4 * k : 8 * k])
        partial_copy(i, x_at, grams, 0).start()
    for i in range(1, xs):
        x = (x_at + i) % xs
        acc = jnp.zeros((shots, 4 * k), jnp.float32)
        for zz in range(zs):
            acc = acc + dot_rows(buf[passing(x, zz)], rg[zz, : 4 * k])
        zpart[i - 1, :shots] = half(acc)
        partial_copy(i, x_at, projections, 1).start()

    z = jnp.zeros((shots, 4 * k), jnp.float32)
    for zz in range(zs):
        z = z + dot_rows(col[zz], rg[zz, : 4 * k])
    zacc[...] = z
    left, right = s_part[:, : 4 * k], s_part[:, 4 * k : 8 * k]
    for i in range(1, xs):
        x = (x_at + i) % xs
        partial_copy(i, x, grams, 0).wait_recv()
        left = left + zbuf[x, shots : shots + k].astype(jnp.float32)
        right = right + zbuf[x, shots + k :].astype(jnp.float32)
    s3t = half(left[:, :k])
    ss = half(right)
    f = left + dot(s3t, ss)
    fb = f[:, 2 * k : 3 * k]
    lift_map = f[:, 3 * k :] + dot_rows(half(fb), s3t)
    lg[leaf, shots:] = half(-jnp.concatenate([f[:, k : 2 * k], lift_map], axis=1))

    z = zacc[...]
    for i in range(1, xs):
        x = (x_at + i) % xs
        partial_copy(i, x, projections, 1).wait_recv()
        z = z + zbuf[x, :shots].astype(jnp.float32)
    proj = half(z[:, :k])
    zf = z + dot(proj, ss)
    carry, z2, z3 = zf[:, k : 2 * k], zf[:, 2 * k : 3 * k], zf[:, 3 * k :]
    lift = z3 + dot_rows(half(z2), s3t)
    lg[leaf, :shots] = half(jnp.concatenate([carry, lift], axis=1))

    def leaf_copy(i, frm):
        return pltpu.make_async_remote_copy(
            src_ref=lg.at[leaf], dst_ref=lg.at[frm], send_sem=l_send.at[i],
            recv_sem=l_recv.at[frm], device_id=((leaf + i) % leaves, node),
            device_id_type=MESH,
        )

    for i in range(1, leaves):
        leaf_copy(i, leaf).start()
    for i in range(1, xs):
        @pl.loop(early, late)
        def _(d):
            onward(i, d).start()

    fc = half(u_ref[...] + dot(s3t, br_ref[...]))
    s1 = half(right[:, k : 2 * k])
    bc = half(
        t_ref[...]
        + lax.dot_general(s1, bl_ref[...], (((0,), (0,)), ((), ())), preferred_element_type=jnp.float32)
    )
    fwd_low[...] = jnp.concatenate([br_ref[...], fc], axis=0)
    back_low[...] = jnp.concatenate([bl_ref[...], bc], axis=0)

    one_hot(steps // 2, steps)

    for i in range(1, leaves):
        leaf_copy(i, (leaf + i) % leaves).wait_recv()

    incoming = jnp.zeros((shots, k), jnp.float32)
    own_in = jnp.zeros((shots, k), jnp.float32)
    lifts = []
    for g in range(leaves):
        own_in = jnp.where(leaf == g, incoming, own_in)
        both = lg[g, :shots].astype(jnp.float32)
        if g > 0:
            both = both + dot(half(incoming), lg[g, shots:])
        incoming = both[:, :k]
        lifts.append(both[:, k:])
    returning = jnp.zeros((shots, k), jnp.float32)
    own_ret = jnp.zeros((shots, k), jnp.float32)
    for g in range(leaves - 1, -1, -1):
        own_ret = jnp.where(leaf == g, returning, own_ret)
        if g < leaves - 1:
            returning = lifts[g] + dot_rows(half(returning), lg[g, shots:, :k])
        else:
            returning = lifts[g]
    proj_fwd = z2 - dot(half(own_in), half(fb))
    cg[node] = half(
        jnp.concatenate([z[:, :k], -own_in, proj_fwd, -own_ret], axis=1)
    )

    coefs = [Tree(cg, p, parts, cz, cx, cr, leaf, node, zs, xs) for p in range(parts)]
    for part in coefs:
        part.start()
    for hop in range(1, zs):
        for part in coefs:
            part.relay(hop)
        if hop == max(zs - 2, 1):
            for i in range(1, xs):
                @pl.loop(late, zs)
                def _(d):
                    onward(i, d).start()
    for part in coefs:
        part.partners()

    sums[...] = jnp.zeros_like(sums)

    def shot_block(j, rhs):
        low = cg[j]
        fwd = half(dot(rhs, b_ref[...]) + dot(low[:, : 2 * k], fwd_low[...]))
        sol = half(dot(fwd, bt[...]) + dot(low[:, 2 * k :], back_low[...]))
        sols[pl.ds(pl.multiple_of(j * shots, shots), shots), :] = sol
        sums[...] += jnp.sum(
            sol.astype(jnp.float32) * fwd.astype(jnp.float32), axis=0, keepdims=True
        )

    shot_block(node, col[z_at])
    for i in range(1, xs):
        j = z_at * xs + (x_at + i) % xs
        shot_block(j, buf[j])
    for i in range(xs):
        @pl.loop(1, zs)
        def _(d):
            j = ((z_at + zs - d) % zs) * xs + (x_at + i) % xs
            arrived(j)
            shot_block(j, buf[j])

    corr = sums[...] / jnp.sqrt(jnp.float32(total))

    cell = cell_ref[...]
    slab = gpart.shape[1]
    high = lax.broadcasted_iota(jnp.int32, (n * slab, block), 0) == cell // LANES
    low_hit = lax.broadcasted_iota(jnp.int32, (LANES, block), 0) == cell % LANES
    placed = lax.dot_general(
        jnp.where(high, corr, 0.0),
        jnp.where(low_hit, 1.0, 0.0),
        (((1,), (1,)), ((), ())),
        preferred_element_type=jnp.float32,
        precision=lax.Precision.HIGHEST,
    )
    gpart[...] = placed.reshape(gpart.shape)

    def slab_copy(j, frm):
        return pltpu.make_async_remote_copy(
            src_ref=gpart.at[j], dst_ref=gbuf.at[frm], send_sem=g_send.at[j],
            recv_sem=g_recv.at[frm], device_id=(leaf, j), device_id_type=MESH,
        )

    @pl.loop(1, n)
    def _(i):
        slab_copy((node + i) % n, node).start()

    def permute(first, last):
        @pl.loop(first, last)
        def _(r):
            rows = pl.ds(pl.multiple_of(r * rows_at, rows_at), rows_at)
            sol_ref[rows, :] = half(dot(onehot[rows, :], sols[...]))

    permute(0, steps // 2)

    own = gpart[node]

    def add_slab(i, acc):
        j = (node + n - i) % n
        slab_copy(j, j).wait_recv()
        return acc + gbuf[j]

    own = lax.fori_loop(1, n, add_slab, own)
    lbuf[leaf] = own

    def grad_copy(i, frm):
        return pltpu.make_async_remote_copy(
            src_ref=lbuf.at[leaf], dst_ref=lbuf.at[frm], send_sem=h_send.at[i],
            recv_sem=h_recv.at[frm], device_id=((leaf + i) % leaves, node),
            device_id_type=MESH,
        )

    for i in range(1, leaves):
        grad_copy(i, leaf).start()
    permute(steps // 2, steps)
    for i in range(1, leaves):
        grad_copy(i, (leaf + leaves - i) % leaves).wait_recv()
    acc = lbuf[0]
    for g in range(1, leaves):
        acc = acc + lbuf[g]
    grad_ref[...] = acc


    for part in basis + coefs:
        part.finish()
    for i in range(1, leaves):
        leaf_copy(i, leaf).wait_send()
        grad_copy(i, leaf).wait_send()
    for i in range(1, xs):
        partial_copy(i, x_at, grams, 0).wait_send()
        partial_copy(i, x_at, projections, 1).wait_send()

        @pl.loop(0, zs)
        def _(d):
            over_x(i, d).wait_send()
            pl.when(d > 0)(lambda: onward(i, d).wait_send())

    @pl.loop(1, zs)
    def _(d):
        own_over_z(d).wait_send()

    @pl.loop(1, n)
    def _(i):
        slab_copy((node + i) % n, node).wait_send()


def per_device(n, leaves, sources, block_inverse, basis_left, basis_right, couple_in, couple_out, column_of_shot, cell_map):
    xs = max(d for d in range(1, n + 1) if n % d == 0 and (2 * d * d <= n or d == 1))
    zs = n // xs
    k, block = basis_left.shape
    shots = sources.shape[0]
    total = n * shots
    slab = CELL_DEV // LANES
    bf16, f32 = jnp.bfloat16, jnp.float32
    dma = pltpu.SemaphoreType.DMA
    anywhere = pl.BlockSpec(memory_space=pl.ANY)
    vmem = pl.BlockSpec(memory_space=pltpu.VMEM)
    vectors = max(zs * (xs - 1), 1)
    parts = 4 if shots % 64 == 0 else 1
    small = pltpu.VMEM((k, block), bf16)
    solution_out, grad = pl.pallas_call(
        functools.partial(kernel, n, leaves, xs),
        out_shape=(
            jax.ShapeDtypeStruct((total, block), bf16),
            jax.ShapeDtypeStruct((slab, LANES), f32),
        ),
        in_specs=[anywhere] * 6 + [vmem] * 2,
        out_specs=(vmem, vmem),
        scratch_shapes=[
            pltpu.VMEM((block, block), bf16), small, small, small, small,
            pltpu.VMEM((block, block), bf16),
            pltpu.VMEM((zs, shots, block), bf16),
            pltpu.VMEM((2 * n, shots, block), bf16),
            pltpu.VMEM((zs, 5 * k, block), bf16),
            pltpu.VMEM((max(xs - 1, 1), shots + 2 * k, 4 * k), bf16),
            pltpu.VMEM((xs, shots + 2 * k, 4 * k), bf16),
            pltpu.VMEM((leaves, shots + k, 2 * k), bf16),
            pltpu.VMEM((n, shots, 4 * k), bf16),
            pltpu.VMEM((2 * k, block), bf16),
            pltpu.VMEM((2 * k, block), bf16),
            pltpu.VMEM((total, total), bf16),
            pltpu.VMEM((total, block), bf16),
            pltpu.VMEM((shots, 4 * k), f32),
            pltpu.VMEM((k, block), f32),
            pltpu.VMEM((k, block), f32),
            pltpu.VMEM((1, block), f32),
            pltpu.VMEM((n, slab, LANES), f32),
            pltpu.VMEM((n, slab, LANES), f32),
            pltpu.VMEM((leaves, slab, LANES), f32),
            dma((5,)), dma((zs,)),
            dma((parts, zs + 1)), dma((parts, zs)),
            dma((vectors,)), dma((zs,)), dma((vectors,)), dma((2 * n,)),
            dma((2, xs)), dma((2, xs)),
            dma((leaves,)), dma((leaves,)),
            dma((parts, zs + 1)), dma((parts, vectors)), dma((parts, n)),
            dma((n,)), dma((n,)),
            dma((leaves,)), dma((leaves,)),
        ],
        compiler_params=pltpu.CompilerParams(
            collective_id=0, has_side_effects=True, vmem_limit_bytes=56 * 1024 * 1024
        ),
    )(
        sources, block_inverse, basis_left, basis_right, couple_in, couple_out,
        column_of_shot.reshape(1, -1), cell_map.reshape(1, -1),
    )
    return solution_out, grad.reshape(-1)


def solution(mesh):
    both = P(None, ("leaf", "node"))
    return jax.shard_map(
        functools.partial(per_device, mesh.shape["node"], mesh.shape["leaf"]),
        mesh=mesh,
        in_specs=(P("node", "leaf"), both, both, both, both, both, P(), P(("leaf", "node"))),
        out_specs=(both, P("node")),
        check_vma=False,
    )
```

```python
import functools

import jax
import jax.numpy as jnp
from jax import lax
from jax.experimental import pallas as pl
from jax.experimental.pallas import tpu as pltpu
from jax.sharding import PartitionSpec as P

CELL_DEV = 2048
LANES = 128
MESH = pl.DeviceIdType.MESH


def dot_rows(a, b):
    return lax.dot_general(a, b, (((1,), (1,)), ((), ())), preferred_element_type=jnp.float32)


def dot(a, b):
    return jnp.dot(a, b, preferred_element_type=jnp.float32)


def half(x):
    return x.astype(jnp.bfloat16)


class Tree:
    def __init__(self, buf, part, parts, zsend, xsend, recv, leaf, node, zs, xs):
        step = buf.shape[1] // parts
        self.rows = pl.ds(part * step, step)
        zsend, recv = zsend.at[part], recv.at[part]
        xsend = None if xsend is None else xsend.at[part]
        self.buf, self.zsend, self.xsend, self.recv = buf, zsend, xsend, recv
        self.leaf, self.zs, self.xs = leaf, zs, xs
        self.z, self.x = node // xs, node % xs

    def copy(self, slot, dst, sem):
        return pltpu.make_async_remote_copy(
            src_ref=self.buf.at[slot, self.rows],
            dst_ref=self.buf.at[slot, self.rows],
            send_sem=sem,
            recv_sem=self.recv.at[slot],
            device_id=(self.leaf, dst),
            device_id_type=MESH,
        )

    def slot(self, zz):
        return zz if self.xsend is None else zz * self.xs + self.x

    def up(self, zz, sem):
        return self.copy(self.slot(zz), (self.z + 1) * self.xs + self.x, self.zsend.at[sem])

    def down(self, zz, sem):
        return self.copy(self.slot(zz), (self.z - 1) * self.xs + self.x, self.zsend.at[sem])

    def across(self, zz):
        if self.xsend is None:
            return []
        return [
            self.copy(
                self.slot(zz),
                self.z * self.xs + (self.x + i) % self.xs,
                self.xsend.at[zz * (self.xs - 1) + i - 1],
            )
            for i in range(1, self.xs)
        ]

    def start(self):
        pl.when(self.z + 1 < self.zs)(lambda: self.up(self.z, self.z).start())
        pl.when(self.z > 0)(lambda: self.down(self.z, self.zs).start())
        for c in self.across(self.z):
            c.start()

    def wait_slot(self, slot):
        self.copy(slot, 0, self.zsend.at[0]).wait_recv()

    def relay(self, hop):
        below, above = self.z - hop, self.z + hop

        @pl.when(below >= 0)
        def _():
            self.wait_slot(self.slot(below))
            pl.when(self.z + 1 < self.zs)(lambda: self.up(below, below).start())
            for c in self.across(below):
                c.start()

        @pl.when(above < self.zs)
        def _():
            self.wait_slot(self.slot(above))
            pl.when(self.z > 0)(lambda: self.down(above, above).start())
            for c in self.across(above):
                c.start()

    def partners(self):
        for i in range(1, self.xs):
            @pl.loop(0, self.zs)
            def _(zz):
                slot = zz * self.xs + (self.x + i) % self.xs
                self.wait_slot(slot)

    def finish(self):
        @pl.loop(0, self.zs)
        def _(zz):
            for c in self.across(zz):
                c.wait_send()
            pl.when((zz <= self.z) & (self.z + 1 < self.zs))(
                lambda: self.up(zz, zz).wait_send()
            )
            pl.when((zz > self.z) & (self.z > 0))(lambda: self.down(zz, zz).wait_send())
        pl.when(self.z > 0)(lambda: self.down(self.z, self.zs).wait_send())


def kernel(
    n, leaves, xs,
    src, b_hbm, bl_hbm, br_hbm, ci_hbm, co_hbm, shot_ref, cell_ref,
    sol_ref, grad_ref,
    b_ref, bl_ref, br_ref, ci_ref, co_ref, bt, col, buf, rg, zpart, zbuf, lg, cg,
    fwd_low, back_low, onehot, sols, zacc, u_ref, t_ref, sums, gpart, gbuf, lbuf,
    in_sem, col_sem, rz, rr, x_send, o_send, f_send, a_recv, z_send, z_recv,
    l_send, l_recv, cz, cx, cr, g_send, g_recv, h_send, h_recv,
):
    leaf, node = lax.axis_index("leaf"), lax.axis_index("node")
    zs = n // xs
    z_at, x_at = node // xs, node % xs
    k, block = bl_ref.shape
    shots = src.shape[0]
    total = n * shots

    pairs = (
        (b_hbm, b_ref), (bl_hbm, bl_ref), (br_hbm, br_ref), (ci_hbm, ci_ref), (co_hbm, co_ref),
    )
    loads = [pltpu.make_async_copy(a, v, in_sem.at[i]) for i, (a, v) in enumerate(pairs)]
    for c in loads:
        c.start()

    barrier = pltpu.get_barrier_semaphore()

    @pl.loop(1, n)
    def _(i):
        pl.semaphore_signal(
            barrier, inc=1, device_id=(leaf, (node + i) % n), device_id_type=MESH
        )

    @pl.loop(1, leaves)
    def _(i):
        pl.semaphore_signal(
            barrier, inc=1, device_id=((leaf + i) % leaves, node), device_id_type=MESH
        )

    def columns(j):
        return pl.ds(pl.multiple_of(j * block, block), block)

    def column_copy(zz):
        return pltpu.make_async_copy(
            src.at[:, columns(zz * xs + x_at)], col.at[zz], col_sem.at[zz]
        )

    for zz in range(zs):
        column_copy(zz).start()

    def send(a, slot, sem, dst):
        return pltpu.make_async_remote_copy(
            src_ref=a, dst_ref=buf.at[slot], send_sem=sem, recv_sem=a_recv.at[slot],
            device_id=(leaf, dst), device_id_type=MESH,
        )

    def arrived(slot):
        send(buf.at[slot], slot, f_send.at[0], node).wait_recv()

    def passing(x, zz):
        return jnp.where(zz == z_at, z_at * xs + x, n + x * zs + zz)

    def over_x(i, d):
        x, zz = (x_at + i) % xs, (z_at + d) % zs
        return send(
            src.at[:, columns(zz * xs + x)], passing(x_at, zz),
            x_send.at[(i - 1) * zs + d], z_at * xs + x,
        )

    def own_over_z(d):
        dst = ((z_at + d) % zs) * xs + x_at
        return send(col.at[(z_at + d) % zs], node, o_send.at[d], dst)

    def onward(i, d):
        x, zz = (x_at + i) % xs, (z_at + d) % zs
        slot = passing(x, zz)
        return send(buf.at[slot], z_at * xs + x, f_send.at[(i - 1) * zs + d], zz * xs + x_at)

    pl.semaphore_wait(barrier, n - 1 + leaves - 1)

    for i in range(1, xs):
        @pl.loop(1, zs + 1)
        def _(d):
            over_x(i, d % zs).start()

    for zz in range(zs):
        column_copy(zz).wait()
    if zs > 1:
        own_over_z(1).start()

    for c in loads:
        c.wait()
    b = b_ref[...]
    u = dot(ci_ref[...], b)
    u_ref[...] = u
    stacked = jnp.concatenate([co_ref[...], br_ref[...], half(u)], axis=0)
    t = dot_rows(stacked, b)
    t_ref[...] = t[:k]
    v = jnp.concatenate([bl_ref[...], half(t)], axis=0)
    rg[z_at, : 4 * k] = v
    rg[z_at, 4 * k :, : 4 * k] = half(dot_rows(ci_ref[...], v))
    rg[z_at, 4 * k :, 4 * k : 8 * k] = half(
        dot_rows(br_ref[...], jnp.concatenate([bl_ref[...], stacked], axis=0))
    )
    parts = rz.shape[0]
    basis = [Tree(rg, p, parts, rz, None, rr, leaf, node, zs, xs) for p in range(parts)]
    for part in basis:
        part.start()

    rows_at = min(256, total)
    steps = total // rows_at

    def one_hot(first, last):
        @pl.loop(first, last)
        def _(r):
            at = pl.multiple_of(r * rows_at, rows_at)
            row = lax.broadcasted_iota(jnp.int32, (rows_at, total), 0) + at
            onehot[pl.ds(at, rows_at), :] = half(jnp.where(row == shot_ref[...], 1.0, 0.0))

    one_hot(0, steps // 2)
    bt[...] = b.T

    for hop in range(1, zs):
        for part in basis:
            part.relay(hop)
        if hop + 1 < zs:
            own_over_z(hop + 1).start()

    early, late = 1 + (zs - 1) // 3, 1 + 2 * (zs - 1) // 3
    for i in range(1, xs):
        @pl.loop(1, zs)
        def _(d):
            arrived(passing((x_at + i) % xs, (z_at + d) % zs))
            pl.when(d < early)(lambda: onward(i, d).start())
        arrived(passing((x_at + i) % xs, z_at))

    s_part = rg[0, 4 * k :, :].astype(jnp.float32)
    for j in range(1, zs):
        s_part = s_part + rg[j, 4 * k :, :].astype(jnp.float32)

    def partial_copy(i, frm, rows, sem):
        return pltpu.make_async_remote_copy(
            src_ref=zpart.at[i - 1, rows], dst_ref=zbuf.at[frm, rows],
            send_sem=z_send.at[sem, i], recv_sem=z_recv.at[sem, frm],
            device_id=(leaf, z_at * xs + (x_at + i) % xs), device_id_type=MESH,
        )

    grams, projections = pl.ds(shots, 2 * k), pl.ds(0, shots)
    for i in range(1, xs):
        zpart[i - 1, shots : shots + k] = half(s_part[:, : 4 * k])
        zpart[i - 1, shots + k :] = half(s_part[:, 4 * k : 8 * k])
        partial_copy(i, x_at, grams, 0).start()
    for i in range(1, xs):
        x = (x_at + i) % xs
        acc = jnp.zeros((shots, 4 * k), jnp.float32)
        for zz in range(zs):
            acc = acc + dot_rows(buf[passing(x, zz)], rg[zz, : 4 * k])
        zpart[i - 1, :shots] = half(acc)
        partial_copy(i, x_at, projections, 1).start()

    z = jnp.zeros((shots, 4 * k), jnp.float32)
    for zz in range(zs):
        z = z + dot_rows(col[zz], rg[zz, : 4 * k])
    zacc[...] = z
    left, right = s_part[:, : 4 * k], s_part[:, 4 * k : 8 * k]
    for i in range(1, xs):
        x = (x_at + i) % xs
        partial_copy(i, x, grams, 0).wait_recv()
        left = left + zbuf[x, shots : shots + k].astype(jnp.float32)
        right = right + zbuf[x, shots + k :].astype(jnp.float32)
    s3t = half(left[:, :k])
    ss = half(right)
    f = left + dot(s3t, ss)
    fb = f[:, 2 * k : 3 * k]
    lift_map = f[:, 3 * k :] + dot_rows(half(fb), s3t)
    lg[leaf, shots:] = half(-jnp.concatenate([f[:, k : 2 * k], lift_map], axis=1))

    z = zacc[...]
    for i in range(1, xs):
        x = (x_at + i) % xs
        partial_copy(i, x, projections, 1).wait_recv()
        z = z + zbuf[x, :shots].astype(jnp.float32)
    proj = half(z[:, :k])
    zf = z + dot(proj, ss)
    carry, z2, z3 = zf[:, k : 2 * k], zf[:, 2 * k : 3 * k], zf[:, 3 * k :]
    lift = z3 + dot_rows(half(z2), s3t)
    lg[leaf, :shots] = half(jnp.concatenate([carry, lift], axis=1))

    def leaf_copy(i, frm):
        return pltpu.make_async_remote_copy(
            src_ref=lg.at[leaf], dst_ref=lg.at[frm], send_sem=l_send.at[i],
            recv_sem=l_recv.at[frm], device_id=((leaf + i) % leaves, node),
            device_id_type=MESH,
        )

    for i in range(1, leaves):
        leaf_copy(i, leaf).start()
    for i in range(1, xs):
        @pl.loop(early, late)
        def _(d):
            onward(i, d).start()

    fc = half(u_ref[...] + dot(s3t, br_ref[...]))
    s1 = half(right[:, k : 2 * k])
    bc = half(
        t_ref[...]
        + lax.dot_general(s1, bl_ref[...], (((0,), (0,)), ((), ())), preferred_element_type=jnp.float32)
    )
    fwd_low[...] = jnp.concatenate([br_ref[...], fc], axis=0)
    back_low[...] = jnp.concatenate([bl_ref[...], bc], axis=0)

    one_hot(steps // 2, steps)

    for i in range(1, leaves):
        leaf_copy(i, (leaf + i) % leaves).wait_recv()

    incoming = jnp.zeros((shots, k), jnp.float32)
    own_in = jnp.zeros((shots, k), jnp.float32)
    lifts = []
    for g in range(leaves):
        own_in = jnp.where(leaf == g, incoming, own_in)
        both = lg[g, :shots].astype(jnp.float32)
        if g > 0:
            both = both + dot(half(incoming), lg[g, shots:])
        incoming = both[:, :k]
        lifts.append(both[:, k:])
    returning = jnp.zeros((shots, k), jnp.float32)
    own_ret = jnp.zeros((shots, k), jnp.float32)
    for g in range(leaves - 1, -1, -1):
        own_ret = jnp.where(leaf == g, returning, own_ret)
        if g < leaves - 1:
            returning = lifts[g] + dot_rows(half(returning), lg[g, shots:, :k])
        else:
            returning = lifts[g]
    proj_fwd = z2 - dot(half(own_in), half(fb))
    cg[node] = half(
        jnp.concatenate([z[:, :k], -own_in, proj_fwd, -own_ret], axis=1)
    )

    coefs = [Tree(cg, p, parts, cz, cx, cr, leaf, node, zs, xs) for p in range(parts)]
    for part in coefs:
        part.start()
    for hop in range(1, zs):
        for part in coefs:
            part.relay(hop)
        if hop == max(zs - 2, 1):
            for i in range(1, xs):
                @pl.loop(late, zs)
                def _(d):
                    onward(i, d).start()
    for part in coefs:
        part.partners()

    sums[...] = jnp.zeros_like(sums)

    def shot_block(j, rhs):
        low = cg[j]
        fwd = half(dot(rhs, b_ref[...]) + dot(low[:, : 2 * k], fwd_low[...]))
        sol = half(dot(fwd, bt[...]) + dot(low[:, 2 * k :], back_low[...]))
        sols[pl.ds(pl.multiple_of(j * shots, shots), shots), :] = sol
        sums[...] += jnp.sum(
            sol.astype(jnp.float32) * fwd.astype(jnp.float32), axis=0, keepdims=True
        )

    shot_block(node, col[z_at])
    for i in range(1, xs):
        j = z_at * xs + (x_at + i) % xs
        shot_block(j, buf[j])
    for i in range(xs):
        @pl.loop(1, zs)
        def _(d):
            j = ((z_at + zs - d) % zs) * xs + (x_at + i) % xs
            arrived(j)
            shot_block(j, buf[j])

    corr = sums[...] / jnp.sqrt(jnp.float32(total))

    cell = cell_ref[...]
    slab = gpart.shape[1]
    high = lax.broadcasted_iota(jnp.int32, (n * slab, block), 0) == cell // LANES
    low_hit = lax.broadcasted_iota(jnp.int32, (LANES, block), 0) == cell % LANES
    placed = lax.dot_general(
        jnp.where(high, corr, 0.0),
        jnp.where(low_hit, 1.0, 0.0),
        (((1,), (1,)), ((), ())),
        preferred_element_type=jnp.float32,
        precision=lax.Precision.HIGHEST,
    )
    gpart[...] = placed.reshape(gpart.shape)

    def slab_copy(j, frm):
        return pltpu.make_async_remote_copy(
            src_ref=gpart.at[j], dst_ref=gbuf.at[frm], send_sem=g_send.at[j],
            recv_sem=g_recv.at[frm], device_id=(leaf, j), device_id_type=MESH,
        )

    @pl.loop(1, n)
    def _(i):
        slab_copy((node + i) % n, node).start()

    def permute(first, last):
        @pl.loop(first, last)
        def _(r):
            rows = pl.ds(pl.multiple_of(r * rows_at, rows_at), rows_at)
            sol_ref[rows, :] = half(dot(onehot[rows, :], sols[...]))

    permute(0, steps // 2)

    own = gpart[node]

    def add_slab(i, acc):
        j = (node + n - i) % n
        slab_copy(j, j).wait_recv()
        return acc + gbuf[j]

    own = lax.fori_loop(1, n, add_slab, own)
    lbuf[leaf] = own

    def grad_copy(i, frm):
        return pltpu.make_async_remote_copy(
            src_ref=lbuf.at[leaf], dst_ref=lbuf.at[frm], send_sem=h_send.at[i],
            recv_sem=h_recv.at[frm], device_id=((leaf + i) % leaves, node),
            device_id_type=MESH,
        )

    for i in range(1, leaves):
        grad_copy(i, leaf).start()
    permute(steps // 2, steps)
    for i in range(1, leaves):
        grad_copy(i, (leaf + leaves - i) % leaves).wait_recv()
    acc = lbuf[0]
    for g in range(1, leaves):
        acc = acc + lbuf[g]
    grad_ref[...] = acc


    for part in basis + coefs:
        part.finish()
    for i in range(1, leaves):
        leaf_copy(i, leaf).wait_send()
        grad_copy(i, leaf).wait_send()
    for i in range(1, xs):
        partial_copy(i, x_at, grams, 0).wait_send()
        partial_copy(i, x_at, projections, 1).wait_send()

        @pl.loop(0, zs)
        def _(d):
            over_x(i, d).wait_send()
            pl.when(d > 0)(lambda: onward(i, d).wait_send())

    @pl.loop(1, zs)
    def _(d):
        own_over_z(d).wait_send()

    @pl.loop(1, n)
    def _(i):
        slab_copy((node + i) % n, node).wait_send()


def per_device(n, leaves, sources, block_inverse, basis_left, basis_right, couple_in, couple_out, column_of_shot, cell_map):
    xs = max(d for d in range(1, n + 1) if n % d == 0 and (2 * d * d <= n or d == 1))
    zs = n // xs
    k, block = basis_left.shape
    shots = sources.shape[0]
    total = n * shots
    slab = CELL_DEV // LANES
    bf16, f32 = jnp.bfloat16, jnp.float32
    dma = pltpu.SemaphoreType.DMA
    anywhere = pl.BlockSpec(memory_space=pl.ANY)
    vmem = pl.BlockSpec(memory_space=pltpu.VMEM)
    vectors = max(zs * (xs - 1), 1)
    parts = 4 if shots % 64 == 0 else 1
    small = pltpu.VMEM((k, block), bf16)
    solution_out, grad = pl.pallas_call(
        functools.partial(kernel, n, leaves, xs),
        out_shape=(
            jax.ShapeDtypeStruct((total, block), bf16),
            jax.ShapeDtypeStruct((slab, LANES), f32),
        ),
        in_specs=[anywhere] * 6 + [vmem] * 2,
        out_specs=(vmem, vmem),
        scratch_shapes=[
            pltpu.VMEM((block, block), bf16), small, small, small, small,
            pltpu.VMEM((block, block), bf16),
            pltpu.VMEM((zs, shots, block), bf16),
            pltpu.VMEM((2 * n, shots, block), bf16),
            pltpu.VMEM((zs, 5 * k, block), bf16),
            pltpu.VMEM((max(xs - 1, 1), shots + 2 * k, 4 * k), bf16),
            pltpu.VMEM((xs, shots + 2 * k, 4 * k), bf16),
            pltpu.VMEM((leaves, shots + k, 2 * k), bf16),
            pltpu.VMEM((n, shots, 4 * k), bf16),
            pltpu.VMEM((2 * k, block), bf16),
            pltpu.VMEM((2 * k, block), bf16),
            pltpu.VMEM((total, total), bf16),
            pltpu.VMEM((total, block), bf16),
            pltpu.VMEM((shots, 4 * k), f32),
            pltpu.VMEM((k, block), f32),
            pltpu.VMEM((k, block), f32),
            pltpu.VMEM((1, block), f32),
            pltpu.VMEM((n, slab, LANES), f32),
            pltpu.VMEM((n, slab, LANES), f32),
            pltpu.VMEM((leaves, slab, LANES), f32),
            dma((5,)), dma((zs,)),
            dma((parts, zs + 1)), dma((parts, zs)),
            dma((vectors,)), dma((zs,)), dma((vectors,)), dma((2 * n,)),
            dma((2, xs)), dma((2, xs)),
            dma((leaves,)), dma((leaves,)),
            dma((parts, zs + 1)), dma((parts, vectors)), dma((parts, n)),
            dma((n,)), dma((n,)),
            dma((leaves,)), dma((leaves,)),
        ],
        compiler_params=pltpu.CompilerParams(
            collective_id=0, has_side_effects=True, vmem_limit_bytes=56 * 1024 * 1024
        ),
    )(
        sources, block_inverse, basis_left, basis_right, couple_in, couple_out,
        column_of_shot.reshape(1, -1), cell_map.reshape(1, -1),
    )
    return solution_out, grad.reshape(-1)


def solution(mesh):
    both = P(None, ("leaf", "node"))
    return jax.shard_map(
        functools.partial(per_device, mesh.shape["node"], mesh.shape["leaf"]),
        mesh=mesh,
        in_specs=(P("node", "leaf"), both, both, both, both, both, P(), P(("leaf", "node"))),
        out_specs=(both, P("node")),
        check_vma=False,
    )
```

```python
import functools

import jax
import jax.numpy as jnp
from jax import lax
from jax.experimental import pallas as pl
from jax.experimental.pallas import tpu as pltpu
from jax.sharding import PartitionSpec as P

CELL_DEV = 2048
LANES = 128
MESH = pl.DeviceIdType.MESH


def dot_rows(a, b):
    return lax.dot_general(a, b, (((1,), (1,)), ((), ())), preferred_element_type=jnp.float32)


def dot(a, b):
    return jnp.dot(a, b, preferred_element_type=jnp.float32)


def half(x):
    return x.astype(jnp.bfloat16)


class Tree:
    def __init__(self, buf, part, parts, zsend, xsend, recv, leaf, node, zs, xs):
        step = buf.shape[1] // parts
        self.rows = pl.ds(part * step, step)
        zsend, recv = zsend.at[part], recv.at[part]
        xsend = None if xsend is None else xsend.at[part]
        self.buf, self.zsend, self.xsend, self.recv = buf, zsend, xsend, recv
        self.leaf, self.zs, self.xs = leaf, zs, xs
        self.z, self.x = node // xs, node % xs

    def copy(self, slot, dst, sem):
        return pltpu.make_async_remote_copy(
            src_ref=self.buf.at[slot, self.rows],
            dst_ref=self.buf.at[slot, self.rows],
            send_sem=sem,
            recv_sem=self.recv.at[slot],
            device_id=(self.leaf, dst),
            device_id_type=MESH,
        )

    def slot(self, zz):
        return zz if self.xsend is None else zz * self.xs + self.x

    def up(self, zz, sem):
        return self.copy(self.slot(zz), (self.z + 1) * self.xs + self.x, self.zsend.at[sem])

    def down(self, zz, sem):
        return self.copy(self.slot(zz), (self.z - 1) * self.xs + self.x, self.zsend.at[sem])

    def across(self, zz):
        if self.xsend is None:
            return []
        return [
            self.copy(
                self.slot(zz),
                self.z * self.xs + (self.x + i) % self.xs,
                self.xsend.at[zz * (self.xs - 1) + i - 1],
            )
            for i in range(1, self.xs)
        ]

    def start(self):
        pl.when(self.z + 1 < self.zs)(lambda: self.up(self.z, self.z).start())
        pl.when(self.z > 0)(lambda: self.down(self.z, self.zs).start())
        for c in self.across(self.z):
            c.start()

    def wait_slot(self, slot):
        self.copy(slot, 0, self.zsend.at[0]).wait_recv()

    def relay(self, hop):
        below, above = self.z - hop, self.z + hop

        @pl.when(below >= 0)
        def _():
            self.wait_slot(self.slot(below))
            pl.when(self.z + 1 < self.zs)(lambda: self.up(below, below).start())
            for c in self.across(below):
                c.start()

        @pl.when(above < self.zs)
        def _():
            self.wait_slot(self.slot(above))
            pl.when(self.z > 0)(lambda: self.down(above, above).start())
            for c in self.across(above):
                c.start()

    def partners(self):
        for i in range(1, self.xs):
            @pl.loop(0, self.zs)
            def _(zz):
                slot = zz * self.xs + (self.x + i) % self.xs
                self.wait_slot(slot)

    def finish(self):
        @pl.loop(0, self.zs)
        def _(zz):
            for c in self.across(zz):
                c.wait_send()
            pl.when((zz <= self.z) & (self.z + 1 < self.zs))(
                lambda: self.up(zz, zz).wait_send()
            )
            pl.when((zz > self.z) & (self.z > 0))(lambda: self.down(zz, zz).wait_send())
        pl.when(self.z > 0)(lambda: self.down(self.z, self.zs).wait_send())


def kernel(
    n, leaves, xs,
    src, b_hbm, bl_hbm, br_hbm, ci_hbm, co_hbm, shot_ref, cell_ref,
    sol_ref, grad_ref,
    b_ref, bl_ref, br_ref, ci_ref, co_ref, bt, col, buf, rg, zpart, zbuf, lg, early_c, late_c,
    fwd_low, back_low, onehot, sols, zacc, u_ref, t_ref, sums, gpart, gbuf, lbuf,
    in_sem, col_sem, rz, rr, x_send, o_send, f_send, a_recv, z_send, z_recv,
    l_send, l_recv, cz, cx, cr, dz, dx, dr, g_send, g_recv, h_send, h_recv,
):
    leaf, node = lax.axis_index("leaf"), lax.axis_index("node")
    zs = n // xs
    z_at, x_at = node // xs, node % xs
    k, block = bl_ref.shape
    shots = src.shape[0]
    total = n * shots

    pairs = (
        (b_hbm, b_ref), (bl_hbm, bl_ref), (br_hbm, br_ref), (ci_hbm, ci_ref), (co_hbm, co_ref),
    )
    loads = [pltpu.make_async_copy(a, v, in_sem.at[i]) for i, (a, v) in enumerate(pairs)]
    for c in loads:
        c.start()

    barrier = pltpu.get_barrier_semaphore()

    @pl.loop(1, n)
    def _(i):
        pl.semaphore_signal(
            barrier, inc=1, device_id=(leaf, (node + i) % n), device_id_type=MESH
        )

    @pl.loop(1, leaves)
    def _(i):
        pl.semaphore_signal(
            barrier, inc=1, device_id=((leaf + i) % leaves, node), device_id_type=MESH
        )

    def columns(j):
        return pl.ds(pl.multiple_of(j * block, block), block)

    def column_copy(zz):
        return pltpu.make_async_copy(
            src.at[:, columns(zz * xs + x_at)], col.at[zz], col_sem.at[zz]
        )

    for zz in range(zs):
        column_copy(zz).start()

    def send(a, slot, sem, dst):
        return pltpu.make_async_remote_copy(
            src_ref=a, dst_ref=buf.at[slot], send_sem=sem, recv_sem=a_recv.at[slot],
            device_id=(leaf, dst), device_id_type=MESH,
        )

    def arrived(slot):
        send(buf.at[slot], slot, f_send.at[0], node).wait_recv()

    def passing(x, zz):
        return jnp.where(zz == z_at, z_at * xs + x, n + x * zs + zz)

    def over_x(i, d):
        x, zz = (x_at + i) % xs, (z_at + d) % zs
        return send(
            src.at[:, columns(zz * xs + x)], passing(x_at, zz),
            x_send.at[(i - 1) * zs + d], z_at * xs + x,
        )

    def own_over_z(d):
        dst = ((z_at + d) % zs) * xs + x_at
        return send(col.at[(z_at + d) % zs], node, o_send.at[d], dst)

    def onward(i, d):
        x, zz = (x_at + i) % xs, (z_at + d) % zs
        slot = passing(x, zz)
        return send(buf.at[slot], z_at * xs + x, f_send.at[(i - 1) * zs + d], zz * xs + x_at)

    pl.semaphore_wait(barrier, n - 1 + leaves - 1)

    for i in range(1, xs):
        @pl.loop(1, zs + 1)
        def _(d):
            over_x(i, d % zs).start()

    for zz in range(zs):
        column_copy(zz).wait()
    if zs > 1:
        own_over_z(1).start()

    for c in loads:
        c.wait()
    b = b_ref[...]
    u = dot(ci_ref[...], b)
    u_ref[...] = u
    stacked = jnp.concatenate([co_ref[...], br_ref[...], half(u)], axis=0)
    t = dot_rows(stacked, b)
    t_ref[...] = t[:k]
    v = jnp.concatenate([bl_ref[...], half(t)], axis=0)
    rg[z_at, : 4 * k] = v
    rg[z_at, 4 * k :, : 4 * k] = half(dot_rows(ci_ref[...], v))
    rg[z_at, 4 * k :, 4 * k : 8 * k] = half(
        dot_rows(br_ref[...], jnp.concatenate([bl_ref[...], stacked], axis=0))
    )
    parts = rz.shape[0]
    basis = [Tree(rg, p, parts, rz, None, rr, leaf, node, zs, xs) for p in range(parts)]
    for part in basis:
        part.start()

    rows_at = min(256, total)
    steps = total // rows_at

    def one_hot(first, last):
        @pl.loop(first, last)
        def _(r):
            at = pl.multiple_of(r * rows_at, rows_at)
            row = lax.broadcasted_iota(jnp.int32, (rows_at, total), 0) + at
            onehot[pl.ds(at, rows_at), :] = half(jnp.where(row == shot_ref[...], 1.0, 0.0))

    one_hot(0, steps // 2)
    bt[...] = b.T

    for hop in range(1, zs):
        for part in basis:
            part.relay(hop)
        if hop == max(zs - 2, 1):
            @pl.loop(2, zs)
            def _(d):
                own_over_z(d).start()

    early, late = 1 + (zs - 1) // 3, 1 + 2 * (zs - 1) // 3
    for i in range(1, xs):
        @pl.loop(1, zs)
        def _(d):
            arrived(passing((x_at + i) % xs, (z_at + d) % zs))
            pl.when(d < early)(lambda: onward(i, d).start())
        arrived(passing((x_at + i) % xs, z_at))

    s_part = rg[0, 4 * k :, :].astype(jnp.float32)
    for j in range(1, zs):
        s_part = s_part + rg[j, 4 * k :, :].astype(jnp.float32)

    def partial_copy(i, frm, rows, sem):
        return pltpu.make_async_remote_copy(
            src_ref=zpart.at[i - 1, rows], dst_ref=zbuf.at[frm, rows],
            send_sem=z_send.at[sem, i], recv_sem=z_recv.at[sem, frm],
            device_id=(leaf, z_at * xs + (x_at + i) % xs), device_id_type=MESH,
        )

    grams, projections = pl.ds(shots, 2 * k), pl.ds(0, shots)
    for i in range(1, xs):
        zpart[i - 1, shots : shots + k] = half(s_part[:, : 4 * k])
        zpart[i - 1, shots + k :] = half(s_part[:, 4 * k : 8 * k])
        partial_copy(i, x_at, grams, 0).start()
    for i in range(1, xs):
        x = (x_at + i) % xs
        acc = jnp.zeros((shots, 4 * k), jnp.float32)
        for zz in range(zs):
            acc = acc + dot_rows(buf[passing(x, zz)], rg[zz, : 4 * k])
        zpart[i - 1, :shots] = half(acc)
        partial_copy(i, x_at, projections, 1).start()

    z = jnp.zeros((shots, 4 * k), jnp.float32)
    for zz in range(zs):
        z = z + dot_rows(col[zz], rg[zz, : 4 * k])
    zacc[...] = z
    left, right = s_part[:, : 4 * k], s_part[:, 4 * k : 8 * k]
    for i in range(1, xs):
        x = (x_at + i) % xs
        partial_copy(i, x, grams, 0).wait_recv()
        left = left + zbuf[x, shots : shots + k].astype(jnp.float32)
        right = right + zbuf[x, shots + k :].astype(jnp.float32)
    s3t = half(left[:, :k])
    ss = half(right)
    f = left + dot(s3t, ss)
    fb = f[:, 2 * k : 3 * k]
    lift_map = f[:, 3 * k :] + dot_rows(half(fb), s3t)
    lg[leaf, shots:] = half(-jnp.concatenate([f[:, k : 2 * k], lift_map], axis=1))

    z = zacc[...]
    for i in range(1, xs):
        x = (x_at + i) % xs
        partial_copy(i, x, projections, 1).wait_recv()
        z = z + zbuf[x, :shots].astype(jnp.float32)
    proj = half(z[:, :k])
    zf = z + dot(proj, ss)
    carry, z2, z3 = zf[:, k : 2 * k], zf[:, 2 * k : 3 * k], zf[:, 3 * k :]
    early_c[node] = half(jnp.concatenate([z[:, :k], z2], axis=1))
    lift = z3 + dot_rows(half(z2), s3t)
    lg[leaf, :shots] = half(jnp.concatenate([carry, lift], axis=1))

    def leaf_copy(i, frm):
        return pltpu.make_async_remote_copy(
            src_ref=lg.at[leaf], dst_ref=lg.at[frm], send_sem=l_send.at[i],
            recv_sem=l_recv.at[frm], device_id=((leaf + i) % leaves, node),
            device_id_type=MESH,
        )

    for i in range(1, leaves):
        leaf_copy(i, leaf).start()
    halves = cz.shape[0]
    first = [Tree(early_c, p, halves, cz, cx, cr, leaf, node, zs, xs) for p in range(halves)]
    for part in first:
        part.start()
    for i in range(1, xs):
        @pl.loop(early, late)
        def _(d):
            onward(i, d).start()

    fc = half(u_ref[...] + dot(s3t, br_ref[...]))
    s1 = half(right[:, k : 2 * k])
    bc = half(
        t_ref[...]
        + lax.dot_general(s1, bl_ref[...], (((0,), (0,)), ((), ())), preferred_element_type=jnp.float32)
    )
    none = jnp.zeros_like(fc)
    fb_low = half(dot(half(fb), bl_ref[...]))
    fwd_low[...] = jnp.concatenate([br_ref[...], none, fc, none], axis=0)
    back_low[...] = jnp.concatenate([none, bl_ref[...], fb_low, bc], axis=0)

    one_hot(steps // 2, steps)

    for hop in range(1, min(zs, 2)):
        for part in first:
            part.relay(hop)

    for i in range(1, leaves):
        leaf_copy(i, (leaf + i) % leaves).wait_recv()

    incoming = jnp.zeros((shots, k), jnp.float32)
    own_in = jnp.zeros((shots, k), jnp.float32)
    lifts = []
    for g in range(leaves):
        own_in = jnp.where(leaf == g, incoming, own_in)
        both = lg[g, :shots].astype(jnp.float32)
        if g > 0:
            both = both + dot(half(incoming), lg[g, shots:])
        incoming = both[:, :k]
        lifts.append(both[:, k:])
    returning = jnp.zeros((shots, k), jnp.float32)
    own_ret = jnp.zeros((shots, k), jnp.float32)
    for g in range(leaves - 1, -1, -1):
        own_ret = jnp.where(leaf == g, returning, own_ret)
        if g < leaves - 1:
            returning = lifts[g] + dot_rows(half(returning), lg[g, shots:, :k])
        else:
            returning = lifts[g]
    late_c[node] = half(jnp.concatenate([-own_in, -own_ret], axis=1))

    coefs = [Tree(late_c, p, halves, dz, dx, dr, leaf, node, zs, xs) for p in range(halves)]
    for part in coefs:
        part.start()
    for hop in range(2, zs):
        for part in first:
            part.relay(hop)
    for hop in range(1, zs):
        for part in coefs:
            part.relay(hop)
        if hop == max(zs - 2, 1):
            for i in range(1, xs):
                @pl.loop(late, zs)
                def _(d):
                    onward(i, d).start()
    for part in first + coefs:
        part.partners()

    sums[...] = jnp.zeros_like(sums)

    def shot_block(j, rhs):
        low = jnp.concatenate([early_c[j], late_c[j]], axis=1)
        fwd = half(dot(rhs, b_ref[...]) + dot(low, fwd_low[...]))
        sol = half(dot(fwd, bt[...]) + dot(low, back_low[...]))
        sols[pl.ds(pl.multiple_of(j * shots, shots), shots), :] = sol
        sums[...] += jnp.sum(
            sol.astype(jnp.float32) * fwd.astype(jnp.float32), axis=0, keepdims=True
        )

    shot_block(node, col[z_at])
    for i in range(1, xs):
        j = z_at * xs + (x_at + i) % xs
        shot_block(j, buf[j])
    for i in range(xs):
        @pl.loop(1, zs)
        def _(d):
            j = ((z_at + zs - d) % zs) * xs + (x_at + i) % xs
            arrived(j)
            shot_block(j, buf[j])

    corr = sums[...] / jnp.sqrt(jnp.float32(total))

    cell = cell_ref[...]
    slab = gpart.shape[1]
    high = lax.broadcasted_iota(jnp.int32, (n * slab, block), 0) == cell // LANES
    low_hit = lax.broadcasted_iota(jnp.int32, (LANES, block), 0) == cell % LANES
    placed = lax.dot_general(
        jnp.where(high, corr, 0.0),
        jnp.where(low_hit, 1.0, 0.0),
        (((1,), (1,)), ((), ())),
        preferred_element_type=jnp.float32,
        precision=lax.Precision.HIGHEST,
    )
    gpart[...] = placed.reshape(gpart.shape)

    def slab_copy(j, frm):
        return pltpu.make_async_remote_copy(
            src_ref=gpart.at[j], dst_ref=gbuf.at[frm], send_sem=g_send.at[j],
            recv_sem=g_recv.at[frm], device_id=(leaf, j), device_id_type=MESH,
        )

    @pl.loop(1, n)
    def _(i):
        slab_copy((node + i) % n, node).start()

    def permute(first, last):
        @pl.loop(first, last)
        def _(r):
            rows = pl.ds(pl.multiple_of(r * rows_at, rows_at), rows_at)
            sol_ref[rows, :] = half(dot(onehot[rows, :], sols[...]))

    permute(0, steps // 2)

    own = gpart[node]

    def add_slab(i, acc):
        j = (node + n - i) % n
        slab_copy(j, j).wait_recv()
        return acc + gbuf[j]

    own = lax.fori_loop(1, n, add_slab, own)
    lbuf[leaf] = own

    def grad_copy(i, frm):
        return pltpu.make_async_remote_copy(
            src_ref=lbuf.at[leaf], dst_ref=lbuf.at[frm], send_sem=h_send.at[i],
            recv_sem=h_recv.at[frm], device_id=((leaf + i) % leaves, node),
            device_id_type=MESH,
        )

    for i in range(1, leaves):
        grad_copy(i, leaf).start()
    permute(steps // 2, steps)
    for i in range(1, leaves):
        grad_copy(i, (leaf + leaves - i) % leaves).wait_recv()
    acc = lbuf[0]
    for g in range(1, leaves):
        acc = acc + lbuf[g]
    grad_ref[...] = acc


    for part in basis + first + coefs:
        part.finish()
    for i in range(1, leaves):
        leaf_copy(i, leaf).wait_send()
        grad_copy(i, leaf).wait_send()
    for i in range(1, xs):
        partial_copy(i, x_at, grams, 0).wait_send()
        partial_copy(i, x_at, projections, 1).wait_send()

        @pl.loop(0, zs)
        def _(d):
            over_x(i, d).wait_send()
            pl.when(d > 0)(lambda: onward(i, d).wait_send())

    @pl.loop(1, zs)
    def _(d):
        own_over_z(d).wait_send()

    @pl.loop(1, n)
    def _(i):
        slab_copy((node + i) % n, node).wait_send()


def per_device(n, leaves, sources, block_inverse, basis_left, basis_right, couple_in, couple_out, column_of_shot, cell_map):
    xs = max(d for d in range(1, n + 1) if n % d == 0 and (2 * d * d <= n or d == 1))
    zs = n // xs
    k, block = basis_left.shape
    shots = sources.shape[0]
    total = n * shots
    slab = CELL_DEV // LANES
    bf16, f32 = jnp.bfloat16, jnp.float32
    dma = pltpu.SemaphoreType.DMA
    anywhere = pl.BlockSpec(memory_space=pl.ANY)
    vmem = pl.BlockSpec(memory_space=pltpu.VMEM)
    vectors = max(zs * (xs - 1), 1)
    halves = 2 if shots % 32 == 0 else 1
    parts = 4 if shots % 64 == 0 else 1
    small = pltpu.VMEM((k, block), bf16)
    solution_out, grad = pl.pallas_call(
        functools.partial(kernel, n, leaves, xs),
        out_shape=(
            jax.ShapeDtypeStruct((total, block), bf16),
            jax.ShapeDtypeStruct((slab, LANES), f32),
        ),
        in_specs=[anywhere] * 6 + [vmem] * 2,
        out_specs=(vmem, vmem),
        scratch_shapes=[
            pltpu.VMEM((block, block), bf16), small, small, small, small,
            pltpu.VMEM((block, block), bf16),
            pltpu.VMEM((zs, shots, block), bf16),
            pltpu.VMEM((2 * n, shots, block), bf16),
            pltpu.VMEM((zs, 5 * k, block), bf16),
            pltpu.VMEM((max(xs - 1, 1), shots + 2 * k, 4 * k), bf16),
            pltpu.VMEM((xs, shots + 2 * k, 4 * k), bf16),
            pltpu.VMEM((leaves, shots + k, 2 * k), bf16),
            pltpu.VMEM((n, shots, 2 * k), bf16),
            pltpu.VMEM((n, shots, 2 * k), bf16),
            pltpu.VMEM((4 * k, block), bf16),
            pltpu.VMEM((4 * k, block), bf16),
            pltpu.VMEM((total, total), bf16),
            pltpu.VMEM((total, block), bf16),
            pltpu.VMEM((shots, 4 * k), f32),
            pltpu.VMEM((k, block), f32),
            pltpu.VMEM((k, block), f32),
            pltpu.VMEM((1, block), f32),
            pltpu.VMEM((n, slab, LANES), f32),
            pltpu.VMEM((n, slab, LANES), f32),
            pltpu.VMEM((leaves, slab, LANES), f32),
            dma((5,)), dma((zs,)),
            dma((parts, zs + 1)), dma((parts, zs)),
            dma((vectors,)), dma((zs,)), dma((vectors,)), dma((2 * n,)),
            dma((2, xs)), dma((2, xs)),
            dma((leaves,)), dma((leaves,)),
            dma((halves, zs + 1)), dma((halves, vectors)), dma((halves, n)),
            dma((halves, zs + 1)), dma((halves, vectors)), dma((halves, n)),
            dma((n,)), dma((n,)),
            dma((leaves,)), dma((leaves,)),
        ],
        compiler_params=pltpu.CompilerParams(
            collective_id=0, has_side_effects=True, vmem_limit_bytes=56 * 1024 * 1024
        ),
    )(
        sources, block_inverse, basis_left, basis_right, couple_in, couple_out,
        column_of_shot.reshape(1, -1), cell_map.reshape(1, -1),
    )
    return solution_out, grad.reshape(-1)


def solution(mesh):
    both = P(None, ("leaf", "node"))
    return jax.shard_map(
        functools.partial(per_device, mesh.shape["node"], mesh.shape["leaf"]),
        mesh=mesh,
        in_specs=(P("node", "leaf"), both, both, both, both, both, P(), P(("leaf", "node"))),
        out_specs=(both, P("node")),
        check_vma=False,
    )
```

```python
import functools

import jax
import jax.numpy as jnp
from jax import lax
from jax.experimental import pallas as pl
from jax.experimental.pallas import tpu as pltpu
from jax.sharding import PartitionSpec as P

CELL_DEV = 2048
LANES = 128
MESH = pl.DeviceIdType.MESH


def dot_rows(a, b):
    return lax.dot_general(a, b, (((1,), (1,)), ((), ())), preferred_element_type=jnp.float32)


def dot(a, b):
    return jnp.dot(a, b, preferred_element_type=jnp.float32)


def half(x):
    return x.astype(jnp.bfloat16)


class Tree:
    def __init__(self, buf, part, parts, zsend, xsend, recv, leaf, node, zs, xs):
        step = buf.shape[1] // parts
        self.rows = pl.ds(part * step, step)
        zsend, recv = zsend.at[part], recv.at[part]
        xsend = None if xsend is None else xsend.at[part]
        self.buf, self.zsend, self.xsend, self.recv = buf, zsend, xsend, recv
        self.leaf, self.zs, self.xs = leaf, zs, xs
        self.z, self.x = node // xs, node % xs

    def copy(self, slot, dst, sem):
        return pltpu.make_async_remote_copy(
            src_ref=self.buf.at[slot, self.rows],
            dst_ref=self.buf.at[slot, self.rows],
            send_sem=sem,
            recv_sem=self.recv.at[slot],
            device_id=(self.leaf, dst),
            device_id_type=MESH,
        )

    def slot(self, zz):
        return zz if self.xsend is None else zz * self.xs + self.x

    def up(self, zz, sem):
        return self.copy(self.slot(zz), (self.z + 1) * self.xs + self.x, self.zsend.at[sem])

    def down(self, zz, sem):
        return self.copy(self.slot(zz), (self.z - 1) * self.xs + self.x, self.zsend.at[sem])

    def across(self, zz):
        if self.xsend is None:
            return []
        return [
            self.copy(
                self.slot(zz),
                self.z * self.xs + (self.x + i) % self.xs,
                self.xsend.at[zz * (self.xs - 1) + i - 1],
            )
            for i in range(1, self.xs)
        ]

    def start(self):
        pl.when(self.z + 1 < self.zs)(lambda: self.up(self.z, self.z).start())
        pl.when(self.z > 0)(lambda: self.down(self.z, self.zs).start())
        for c in self.across(self.z):
            c.start()

    def wait_slot(self, slot):
        self.copy(slot, 0, self.zsend.at[0]).wait_recv()

    def relay(self, hop):
        below, above = self.z - hop, self.z + hop

        @pl.when(below >= 0)
        def _():
            self.wait_slot(self.slot(below))
            pl.when(self.z + 1 < self.zs)(lambda: self.up(below, below).start())
            for c in self.across(below):
                c.start()

        @pl.when(above < self.zs)
        def _():
            self.wait_slot(self.slot(above))
            pl.when(self.z > 0)(lambda: self.down(above, above).start())
            for c in self.across(above):
                c.start()

    def partners(self):
        for i in range(1, self.xs):
            @pl.loop(0, self.zs)
            def _(zz):
                slot = zz * self.xs + (self.x + i) % self.xs
                self.wait_slot(slot)

    def finish(self):
        @pl.loop(0, self.zs)
        def _(zz):
            for c in self.across(zz):
                c.wait_send()
            pl.when((zz <= self.z) & (self.z + 1 < self.zs))(
                lambda: self.up(zz, zz).wait_send()
            )
            pl.when((zz > self.z) & (self.z > 0))(lambda: self.down(zz, zz).wait_send())
        pl.when(self.z > 0)(lambda: self.down(self.z, self.zs).wait_send())


def kernel(
    n, leaves, xs,
    src, b_hbm, bl_hbm, br_hbm, ci_hbm, co_hbm, shot_ref, cell_ref,
    sol_ref, grad_ref,
    b_ref, bl_ref, br_ref, ci_ref, co_ref, bt, col, buf, rg, zpart, zbuf, lg, early_c, late_c,
    fwd_low, back_low, onehot, sols, zacc, u_ref, t_ref, sums, gpart, gbuf, lbuf,
    in_sem, col_sem, rz, rr, x_send, o_send, f_send, a_recv, z_send, z_recv,
    l_send, l_recv, cz, cx, cr, dz, dx, dr, g_send, g_recv, h_send, h_recv,
):
    leaf, node = lax.axis_index("leaf"), lax.axis_index("node")
    zs = n // xs
    z_at, x_at = node // xs, node % xs
    k, block = bl_ref.shape
    shots = src.shape[0]
    total = n * shots

    pairs = (
        (b_hbm, b_ref), (bl_hbm, bl_ref), (br_hbm, br_ref), (ci_hbm, ci_ref), (co_hbm, co_ref),
    )
    loads = [pltpu.make_async_copy(a, v, in_sem.at[i]) for i, (a, v) in enumerate(pairs)]
    for c in loads:
        c.start()

    barrier = pltpu.get_barrier_semaphore()

    @pl.loop(1, n)
    def _(i):
        pl.semaphore_signal(
            barrier, inc=1, device_id=(leaf, (node + i) % n), device_id_type=MESH
        )

    @pl.loop(1, leaves)
    def _(i):
        pl.semaphore_signal(
            barrier, inc=1, device_id=((leaf + i) % leaves, node), device_id_type=MESH
        )

    def columns(j):
        return pl.ds(pl.multiple_of(j * block, block), block)

    def column_copy(zz):
        return pltpu.make_async_copy(
            src.at[:, columns(zz * xs + x_at)], col.at[zz], col_sem.at[zz]
        )

    for zz in range(zs):
        column_copy(zz).start()

    def send(a, slot, sem, dst):
        return pltpu.make_async_remote_copy(
            src_ref=a, dst_ref=buf.at[slot], send_sem=sem, recv_sem=a_recv.at[slot],
            device_id=(leaf, dst), device_id_type=MESH,
        )

    def arrived(slot):
        send(buf.at[slot], slot, f_send.at[0], node).wait_recv()

    def passing(x, zz):
        return jnp.where(zz == z_at, z_at * xs + x, n + x * zs + zz)

    def over_x(i, d):
        x, zz = (x_at + i) % xs, (z_at + d) % zs
        return send(
            src.at[:, columns(zz * xs + x)], passing(x_at, zz),
            x_send.at[(i - 1) * zs + d], z_at * xs + x,
        )

    def own_over_z(d):
        dst = ((z_at + d) % zs) * xs + x_at
        return send(col.at[(z_at + d) % zs], node, o_send.at[d], dst)

    def onward(i, d):
        x, zz = (x_at + i) % xs, (z_at + d) % zs
        slot = passing(x, zz)
        return send(buf.at[slot], z_at * xs + x, f_send.at[(i - 1) * zs + d], zz * xs + x_at)

    for c in loads:
        c.wait()
    b = b_ref[...]
    u = dot(ci_ref[...], b)
    u_ref[...] = u
    stacked = jnp.concatenate([co_ref[...], br_ref[...], half(u)], axis=0)
    t = dot_rows(stacked, b)
    t_ref[...] = t[:k]
    v = jnp.concatenate([bl_ref[...], half(t)], axis=0)
    rg[z_at, : 4 * k] = v
    rg[z_at, 4 * k :, : 4 * k] = half(dot_rows(ci_ref[...], v))
    rg[z_at, 4 * k :, 4 * k : 8 * k] = half(
        dot_rows(br_ref[...], jnp.concatenate([bl_ref[...], stacked], axis=0))
    )
    pl.semaphore_wait(barrier, n - 1 + leaves - 1)

    parts = rz.shape[0]
    basis = [Tree(rg, p, parts, rz, None, rr, leaf, node, zs, xs) for p in range(parts)]
    for part in basis:
        part.start()

    for i in range(1, xs):
        @pl.loop(1, zs + 1)
        def _(d):
            over_x(i, d % zs).start()

    for zz in range(zs):
        column_copy(zz).wait()
    if zs > 1:
        own_over_z(1).start()

    rows_at = min(256, total)
    steps = total // rows_at

    def one_hot(first, last):
        @pl.loop(first, last)
        def _(r):
            at = pl.multiple_of(r * rows_at, rows_at)
            row = lax.broadcasted_iota(jnp.int32, (rows_at, total), 0) + at
            onehot[pl.ds(at, rows_at), :] = half(jnp.where(row == shot_ref[...], 1.0, 0.0))

    one_hot(0, steps // 2)
    bt[...] = b.T

    for hop in range(1, zs):
        for part in basis:
            part.relay(hop)
        if hop == max(zs - 2, 1):
            @pl.loop(2, zs)
            def _(d):
                own_over_z(d).start()

    early, late = 1 + (zs - 1) // 3, 1 + 2 * (zs - 1) // 3
    for i in range(1, xs):
        @pl.loop(1, zs)
        def _(d):
            arrived(passing((x_at + i) % xs, (z_at + d) % zs))
            pl.when(d < early)(lambda: onward(i, d).start())
        arrived(passing((x_at + i) % xs, z_at))

    s_part = rg[0, 4 * k :, :].astype(jnp.float32)
    for j in range(1, zs):
        s_part = s_part + rg[j, 4 * k :, :].astype(jnp.float32)

    def partial_copy(i, frm, rows, sem):
        return pltpu.make_async_remote_copy(
            src_ref=zpart.at[i - 1, rows], dst_ref=zbuf.at[frm, rows],
            send_sem=z_send.at[sem, i], recv_sem=z_recv.at[sem, frm],
            device_id=(leaf, z_at * xs + (x_at + i) % xs), device_id_type=MESH,
        )

    grams, projections = pl.ds(shots, 2 * k), pl.ds(0, shots)
    for i in range(1, xs):
        zpart[i - 1, shots : shots + k] = half(s_part[:, : 4 * k])
        zpart[i - 1, shots + k :] = half(s_part[:, 4 * k : 8 * k])
        partial_copy(i, x_at, grams, 0).start()
    for i in range(1, xs):
        x = (x_at + i) % xs
        acc = jnp.zeros((shots, 4 * k), jnp.float32)
        for zz in range(zs):
            acc = acc + dot_rows(buf[passing(x, zz)], rg[zz, : 4 * k])
        zpart[i - 1, :shots] = half(acc)
        partial_copy(i, x_at, projections, 1).start()

    z = jnp.zeros((shots, 4 * k), jnp.float32)
    for zz in range(zs):
        z = z + dot_rows(col[zz], rg[zz, : 4 * k])
    zacc[...] = z
    left, right = s_part[:, : 4 * k], s_part[:, 4 * k : 8 * k]
    for i in range(1, xs):
        x = (x_at + i) % xs
        partial_copy(i, x, grams, 0).wait_recv()
        left = left + zbuf[x, shots : shots + k].astype(jnp.float32)
        right = right + zbuf[x, shots + k :].astype(jnp.float32)
    s3t = half(left[:, :k])
    ss = half(right)
    f = left + dot(s3t, ss)
    fb = f[:, 2 * k : 3 * k]
    lift_map = f[:, 3 * k :] + dot_rows(half(fb), s3t)
    lg[leaf, shots:] = half(-jnp.concatenate([f[:, k : 2 * k], lift_map], axis=1))

    z = zacc[...]
    for i in range(1, xs):
        x = (x_at + i) % xs
        partial_copy(i, x, projections, 1).wait_recv()
        z = z + zbuf[x, :shots].astype(jnp.float32)
    proj = half(z[:, :k])
    zf = z + dot(proj, ss)
    carry, z2, z3 = zf[:, k : 2 * k], zf[:, 2 * k : 3 * k], zf[:, 3 * k :]
    early_c[node] = half(jnp.concatenate([z[:, :k], z2], axis=1))
    lift = z3 + dot_rows(half(z2), s3t)
    lg[leaf, :shots] = half(jnp.concatenate([carry, lift], axis=1))

    def leaf_copy(i, frm):
        return pltpu.make_async_remote_copy(
            src_ref=lg.at[leaf], dst_ref=lg.at[frm], send_sem=l_send.at[i],
            recv_sem=l_recv.at[frm], device_id=((leaf + i) % leaves, node),
            device_id_type=MESH,
        )

    for i in range(1, leaves):
        leaf_copy(i, leaf).start()
    halves = cz.shape[0]
    first = [Tree(early_c, p, halves, cz, cx, cr, leaf, node, zs, xs) for p in range(halves)]
    for part in first:
        part.start()
    for i in range(1, xs):
        @pl.loop(early, late)
        def _(d):
            onward(i, d).start()

    fc = half(u_ref[...] + dot(s3t, br_ref[...]))
    s1 = half(right[:, k : 2 * k])
    bc = half(
        t_ref[...]
        + lax.dot_general(s1, bl_ref[...], (((0,), (0,)), ((), ())), preferred_element_type=jnp.float32)
    )
    none = jnp.zeros_like(fc)
    fb_low = half(dot(half(fb), bl_ref[...]))
    fwd_low[...] = jnp.concatenate([br_ref[...], none, fc, none], axis=0)
    back_low[...] = jnp.concatenate([none, bl_ref[...], fb_low, bc], axis=0)

    one_hot(steps // 2, steps)

    for hop in range(1, min(zs, 2)):
        for part in first:
            part.relay(hop)

    for i in range(1, leaves):
        leaf_copy(i, (leaf + i) % leaves).wait_recv()

    incoming = jnp.zeros((shots, k), jnp.float32)
    own_in = jnp.zeros((shots, k), jnp.float32)
    lifts = []
    for g in range(leaves):
        own_in = jnp.where(leaf == g, incoming, own_in)
        both = lg[g, :shots].astype(jnp.float32)
        if g > 0:
            both = both + dot(half(incoming), lg[g, shots:])
        incoming = both[:, :k]
        lifts.append(both[:, k:])
    returning = jnp.zeros((shots, k), jnp.float32)
    own_ret = jnp.zeros((shots, k), jnp.float32)
    for g in range(leaves - 1, -1, -1):
        own_ret = jnp.where(leaf == g, returning, own_ret)
        if g < leaves - 1:
            returning = lifts[g] + dot_rows(half(returning), lg[g, shots:, :k])
        else:
            returning = lifts[g]
    late_c[node] = half(jnp.concatenate([-own_in, -own_ret], axis=1))

    coefs = [Tree(late_c, p, halves, dz, dx, dr, leaf, node, zs, xs) for p in range(halves)]
    for part in coefs:
        part.start()
    for hop in range(2, zs):
        for part in first:
            part.relay(hop)
    for hop in range(1, zs):
        for part in coefs:
            part.relay(hop)
        if hop == 1:
            for i in range(1, xs):
                @pl.loop(late, zs)
                def _(d):
                    onward(i, d).start()
    for part in first + coefs:
        part.partners()

    sums[...] = jnp.zeros_like(sums)

    def shot_block(j, rhs):
        low = jnp.concatenate([early_c[j], late_c[j]], axis=1)
        fwd = half(dot(rhs, b_ref[...]) + dot(low, fwd_low[...]))
        sol = half(dot(fwd, bt[...]) + dot(low, back_low[...]))
        sols[pl.ds(pl.multiple_of(j * shots, shots), shots), :] = sol
        sums[...] += jnp.sum(
            sol.astype(jnp.float32) * fwd.astype(jnp.float32), axis=0, keepdims=True
        )

    shot_block(node, col[z_at])
    for i in range(1, xs):
        j = z_at * xs + (x_at + i) % xs
        shot_block(j, buf[j])
    for i in range(xs):
        @pl.loop(1, zs)
        def _(d):
            j = ((z_at + zs - d) % zs) * xs + (x_at + i) % xs
            arrived(j)
            shot_block(j, buf[j])

    corr = sums[...] / jnp.sqrt(jnp.float32(total))

    cell = cell_ref[...]
    slab = gpart.shape[1]
    high = lax.broadcasted_iota(jnp.int32, (n * slab, block), 0) == cell // LANES
    low_hit = lax.broadcasted_iota(jnp.int32, (LANES, block), 0) == cell % LANES
    placed = lax.dot_general(
        jnp.where(high, corr, 0.0),
        jnp.where(low_hit, 1.0, 0.0),
        (((1,), (1,)), ((), ())),
        preferred_element_type=jnp.float32,
        precision=lax.Precision.HIGHEST,
    )
    gpart[...] = placed.reshape(gpart.shape)

    def slab_copy(j, frm):
        return pltpu.make_async_remote_copy(
            src_ref=gpart.at[j], dst_ref=gbuf.at[frm], send_sem=g_send.at[j],
            recv_sem=g_recv.at[frm], device_id=(leaf, j), device_id_type=MESH,
        )

    @pl.loop(1, n)
    def _(i):
        slab_copy((node + i) % n, node).start()

    def permute(first, last):
        @pl.loop(first, last)
        def _(r):
            rows = pl.ds(pl.multiple_of(r * rows_at, rows_at), rows_at)
            sol_ref[rows, :] = half(dot(onehot[rows, :], sols[...]))

    permute(0, steps // 2)

    own = gpart[node]

    def add_slab(i, acc):
        j = (node + n - i) % n
        slab_copy(j, j).wait_recv()
        return acc + gbuf[j]

    own = lax.fori_loop(1, n, add_slab, own)
    lbuf[leaf] = own

    def grad_copy(i, frm):
        return pltpu.make_async_remote_copy(
            src_ref=lbuf.at[leaf], dst_ref=lbuf.at[frm], send_sem=h_send.at[i],
            recv_sem=h_recv.at[frm], device_id=((leaf + i) % leaves, node),
            device_id_type=MESH,
        )

    for i in range(1, leaves):
        grad_copy(i, leaf).start()
    permute(steps // 2, steps)
    for i in range(1, leaves):
        grad_copy(i, (leaf + leaves - i) % leaves).wait_recv()
    acc = lbuf[0]
    for g in range(1, leaves):
        acc = acc + lbuf[g]
    grad_ref[...] = acc


    for part in basis + first + coefs:
        part.finish()
    for i in range(1, leaves):
        leaf_copy(i, leaf).wait_send()
        grad_copy(i, leaf).wait_send()
    for i in range(1, xs):
        partial_copy(i, x_at, grams, 0).wait_send()
        partial_copy(i, x_at, projections, 1).wait_send()

        @pl.loop(0, zs)
        def _(d):
            over_x(i, d).wait_send()
            pl.when(d > 0)(lambda: onward(i, d).wait_send())

    @pl.loop(1, zs)
    def _(d):
        own_over_z(d).wait_send()

    @pl.loop(1, n)
    def _(i):
        slab_copy((node + i) % n, node).wait_send()


def per_device(n, leaves, sources, block_inverse, basis_left, basis_right, couple_in, couple_out, column_of_shot, cell_map):
    xs = max(d for d in range(1, n + 1) if n % d == 0 and (2 * d * d <= n or d == 1))
    zs = n // xs
    k, block = basis_left.shape
    shots = sources.shape[0]
    total = n * shots
    slab = CELL_DEV // LANES
    bf16, f32 = jnp.bfloat16, jnp.float32
    dma = pltpu.SemaphoreType.DMA
    anywhere = pl.BlockSpec(memory_space=pl.ANY)
    vmem = pl.BlockSpec(memory_space=pltpu.VMEM)
    vectors = max(zs * (xs - 1), 1)
    halves = 2 if shots % 32 == 0 else 1
    parts = 4 if shots % 64 == 0 else 1
    small = pltpu.VMEM((k, block), bf16)
    solution_out, grad = pl.pallas_call(
        functools.partial(kernel, n, leaves, xs),
        out_shape=(
            jax.ShapeDtypeStruct((total, block), bf16),
            jax.ShapeDtypeStruct((slab, LANES), f32),
        ),
        in_specs=[anywhere] * 6 + [vmem] * 2,
        out_specs=(vmem, vmem),
        scratch_shapes=[
            pltpu.VMEM((block, block), bf16), small, small, small, small,
            pltpu.VMEM((block, block), bf16),
            pltpu.VMEM((zs, shots, block), bf16),
            pltpu.VMEM((2 * n, shots, block), bf16),
            pltpu.VMEM((zs, 5 * k, block), bf16),
            pltpu.VMEM((max(xs - 1, 1), shots + 2 * k, 4 * k), bf16),
            pltpu.VMEM((xs, shots + 2 * k, 4 * k), bf16),
            pltpu.VMEM((leaves, shots + k, 2 * k), bf16),
            pltpu.VMEM((n, shots, 2 * k), bf16),
            pltpu.VMEM((n, shots, 2 * k), bf16),
            pltpu.VMEM((4 * k, block), bf16),
            pltpu.VMEM((4 * k, block), bf16),
            pltpu.VMEM((total, total), bf16),
            pltpu.VMEM((total, block), bf16),
            pltpu.VMEM((shots, 4 * k), f32),
            pltpu.VMEM((k, block), f32),
            pltpu.VMEM((k, block), f32),
            pltpu.VMEM((1, block), f32),
            pltpu.VMEM((n, slab, LANES), f32),
            pltpu.VMEM((n, slab, LANES), f32),
            pltpu.VMEM((leaves, slab, LANES), f32),
            dma((5,)), dma((zs,)),
            dma((parts, zs + 1)), dma((parts, zs)),
            dma((vectors,)), dma((zs,)), dma((vectors,)), dma((2 * n,)),
            dma((2, xs)), dma((2, xs)),
            dma((leaves,)), dma((leaves,)),
            dma((halves, zs + 1)), dma((halves, vectors)), dma((halves, n)),
            dma((halves, zs + 1)), dma((halves, vectors)), dma((halves, n)),
            dma((n,)), dma((n,)),
            dma((leaves,)), dma((leaves,)),
        ],
        compiler_params=pltpu.CompilerParams(
            collective_id=0, has_side_effects=True, vmem_limit_bytes=56 * 1024 * 1024
        ),
    )(
        sources, block_inverse, basis_left, basis_right, couple_in, couple_out,
        column_of_shot.reshape(1, -1), cell_map.reshape(1, -1),
    )
    return solution_out, grad.reshape(-1)


def solution(mesh):
    both = P(None, ("leaf", "node"))
    return jax.shard_map(
        functools.partial(per_device, mesh.shape["node"], mesh.shape["leaf"]),
        mesh=mesh,
        in_specs=(P("node", "leaf"), both, both, both, both, both, P(), P(("leaf", "node"))),
        out_specs=(both, P("node")),
        check_vma=False,
    )
```
